32 devices in a mesh: grp: 4 (over y, x), blk: 8 (over z, core).
Axes of the slice: x: 2, y: 2, z: 4, core: 2. Of those that a mesh axis runs over, the one named last changes fastest.
Arguments:
- adjoint_init: float32 [5, 128, 8192], P(None, 'grp', 'blk'), may hold values from -6 to 6
- adjoint_rhs: float32 [5, 128, 8192], P(None, 'grp', 'blk'), may hold values from -24 to 24
- flow_state: float32 [5, 128, 8192], P(None, 'grp', 'blk'), may hold values from -2 to 8, as said below
- face_weights: bfloat16 [6, 128, 8192], P(None, 'grp', 'blk'), may hold values from 0.29882812 to 1.1953125
- pseudo_time: float32 [128, 8192], P('grp', 'blk'), may hold values from 1 to 4
- tet_coords: float32 [4, 3, 65536], P(None, None, ('grp', 'blk')), may hold values from -6 to 6
- tet_weights: float32 [4, 65536], P(None, ('grp', 'blk')), may hold values from 0.25 to 1
- tet_cell: int32 [65536], P(('grp', 'blk')), may hold values from 0 to 32767
- tet_vertex: int32 [4, 65536], P(None, ('grp', 'blk')), may hold values from 0 to 1535
- tet_count: int32 [32, 8], P(('grp', 'blk')), may hold values from 1 to 256, as said below
Outputs:
- adjoint_field: float32 [5, 128, 8192], P(None, 'grp', 'blk')
- sensitivity: float32 [3, 49152], P(None, ('grp', 'blk'))
The draws below stay inside these ranges and needn't reach their ends.
Inputs may be any that keep to these rules, and one draw needn't show every extreme that they name: `flow_state`: the density is 0.5 to 2, pressure 0.4 (energy - momentum squared / (2 density)) is about 0.5 to 2, each velocity component is below 1 in magnitude. A block's slots are grouped by owner: slots o * 256 to (o + 1) * 256 - 1 of a block are for owner o of its group, and the first tet_count[block, o] of them are live. In every group one owner, drawn from the seed, gets exactly 256 live tetrahedra from every block of the group. `tet_vertex`: A corner's vertex belongs to the owner of its slot's range. `tet_cell`: cell index x 32 * 32 + y * 32 + z within the block.
All inputs are finite; a program needn't handle non-finite values.
Results may differ from the reference program's by a relative error of at most 0.0003.
Values sent between devices are 32-bit elements; how exact they have to be, the bound alone decides.
No kernel may reach another device: no remote copies, remote signals or barrier semaphores. Data moves between devices by JAX's collectives and lax.ppermute only.
A program may use at most 128 MiB of HBM per device.

```python
import math
import jax
import jax.numpy as jnp
from jax import lax

EDGE = 32
SWEEPS = 2
TET_DEV = 2048
VERT_DEV = 1536
OWNERS = 8
SOURCES = 32
CAP = 256
CELLS = 32768
NX = 128
NYZ = 8192
TETS = 65536
NVERT = 49152


GAMMA = 1.4


def draw_flow_state(key, part):
    keys = jax.random.split(key, 3)
    shape = (NX, NYZ)
    density = jnp.exp(jax.random.uniform(keys[0], shape, jnp.float32, math.log(0.5), math.log(2.0)))
    velocity = jnp.clip(0.3 * jax.random.normal(keys[1], (3,) + shape, jnp.float32), -0.9, 0.9)
    pressure = jnp.exp(jax.random.uniform(keys[2], shape, jnp.float32, math.log(0.5), math.log(2.0)))
    energy = pressure / (GAMMA - 1.0) + 0.5 * density * jnp.sum(velocity * velocity, axis=0)
    return jnp.concatenate([density[None], density[None] * velocity, energy[None]], 0).astype(jnp.float32)


def draw_tet_count(key, part):
    keys = jax.random.split(key, 3)
    ceiling = jax.random.randint(keys[0], (SOURCES, 1), max(CAP // 4, 1), CAP + 1)
    drawn_counts = jax.random.randint(keys[1], (SOURCES, OWNERS), jnp.maximum(ceiling // 2, 1), ceiling + 1)
    full_owner = jax.random.randint(keys[2], (SOURCES // OWNERS, 1), 0, OWNERS)
    group_of = jnp.arange(SOURCES) // OWNERS
    is_full = full_owner[group_of] == jnp.arange(OWNERS)[None, :]
    return jnp.where(is_full, CAP, drawn_counts).astype(jnp.int32)


def with_ends(entries, rng, low, top_value):
    place = [jax.random.randint(jax.random.fold_in(rng, axis), (), 0, length) for axis, length in enumerate(entries.shape)]
    longest = entries.shape.index(max(entries.shape))
    next_to = place[:longest] + [(place[longest] + 1) % entries.shape[longest]] + place[longest + 1:]
    return entries.at[tuple(place)].set(low).at[tuple(next_to)].set(top_value)


def level_of(key, dims, shards, smallest, top_value):
    loudness = 1.0
    for position, shards_of in shards:
        draws = jax.random.uniform(jax.random.fold_in(jax.random.fold_in(key, 6), position), (shards_of,), jnp.float32, smallest / len(shards), top_value / len(shards))
        loudness = loudness * jnp.repeat(jnp.exp(draws), dims[position] // shards_of).reshape((-1,) + (1,) * (len(dims) - 1 - position))
    return loudness


def gaussian(rng, dims, deviation, bound, cuts=(), held_as=jnp.bfloat16):
    values = deviation * jax.random.normal(rng, dims, jnp.float32)
    if cuts:
        values = values * level_of(rng, dims, cuts, -0.22, 0.18)
    return jnp.clip(values, -bound, bound).astype(held_as)


def setup_inputs(seed: int = 0) -> dict:
    key_of = jax.random.split(jax.random.key(seed), 11)
    return {
        "adjoint_init": gaussian(key_of[0], (5, NX, NYZ), 1.0, 6.0, ((1, 4), (2, 8)), jnp.float32),
        "adjoint_rhs": gaussian(key_of[1], (5, NX, NYZ), 4.0, 24.0, ((1, 4), (2, 8)), jnp.float32),
        "flow_state": draw_flow_state(jax.random.fold_in(key_of[10], 71), 0),
        "face_weights": jnp.clip(0.29882812 + 0.8964844 * jax.random.uniform(key_of[3], (6, NX, NYZ), jnp.float32) ** level_of(key_of[3], (6, NX, NYZ), ((1, 4), (2, 8)), -0.2, 0.2), 0.29882812, 1.1953125).astype(jnp.bfloat16),
        "pseudo_time": jnp.clip(jnp.exp(math.log(4.0) - 1.3862944 * jax.random.uniform(key_of[4], (NX, NYZ), jnp.float32) ** level_of(key_of[4], (NX, NYZ), ((0, 4), (1, 8)), -0.2, 0.2)), 1.0, 4.0),
        "tet_coords": gaussian(key_of[5], (4, 3, TETS), 1.0, 6.0, ((2, 32),), jnp.float32),
        "tet_weights": jnp.clip(0.25 + 0.75 * jax.random.uniform(key_of[6], (4, TETS), jnp.float32) ** level_of(key_of[6], (4, TETS), ((1, 32),), -0.2, 0.2), 0.25, 1.0),
        "tet_cell": with_ends(jax.random.randint(key_of[7], (TETS,), 0, CELLS), jax.random.fold_in(key_of[7], 1), 0, CELLS - 1).astype(jnp.int32),
        "tet_vertex": with_ends(jax.random.randint(key_of[8], (4, TETS), 0, VERT_DEV), jax.random.fold_in(key_of[8], 1), 0, VERT_DEV - 1).astype(jnp.int32),
        "tet_count": draw_tet_count(jax.random.fold_in(key_of[10], 71), 0),
    }


GAMMA = 1.4

def flow_split(state):
    density = state[0]
    velocity = state[1:4] / density
    speed_sq = lax.optimization_barrier(jnp.sum(velocity * velocity, axis=0))
    pressure = (GAMMA - 1.0) * (state[4] - 0.5 * density * speed_sq)
    return (velocity, speed_sq, pressure)

def jacobians(state):
    density = state[0]
    velocity, speed_sq, pressure = flow_split(state)
    enthalpy = (state[4] + pressure) / density
    reach = jnp.sqrt(speed_sq) + jnp.sqrt(GAMMA * pressure / density)
    half_sq = 0.5 * (GAMMA - 1.0) * speed_sq
    tables = []
    for axis_id in range(3):
        normal_vel = velocity[axis_id]
        matrix = [[1.0 if column == axis_id + 1 else 0.0 for column in range(5)]]
        for first in range(3):
            n_first = 1.0 if first == axis_id else 0.0
            line = [half_sq * n_first - velocity[first] * normal_vel]
            for second in range(3):
                n_second = 1.0 if second == axis_id else 0.0
                entry = velocity[first] * n_second - (GAMMA - 1.0) * n_first * velocity[second]
                if first == second:
                    entry = entry + normal_vel
                line.append(entry)
            line.append((GAMMA - 1.0) * n_first)
            matrix.append(line)
        energy_line = [normal_vel * (half_sq - enthalpy)]
        for second in range(3):
            n_second = 1.0 if second == axis_id else 0.0
            energy_line.append(enthalpy * n_second - (GAMMA - 1.0) * normal_vel * velocity[second])
        energy_line.append(GAMMA * normal_vel)
        matrix.append(energy_line)
        tables.append(matrix)
    return (reach, tables)

def apply_transpose(matrix, adjoint):
    result = []
    for column in range(5):
        total = matrix[0][column] * adjoint[0]
        for line in range(1, 5):
            total = total + matrix[line][column] * adjoint[line]
        result.append(total)
    return jnp.stack(result)

def relax_cells(reach, tables, faces, pseudo, rhs, neighbours):
    total = rhs
    weight = pseudo
    for direction in range(6):
        axis_id = direction // 2
        sign_value = 1.0 if direction % 2 == 0 else -1.0
        nearby = neighbours[direction]
        face = faces[direction].astype(jnp.float32)
        total = total + 0.5 * face * (sign_value * apply_transpose(tables[axis_id], nearby) + reach * nearby)
        weight = weight + 0.5 * reach * face
    return total / weight

def cross_product(left, right):
    return jnp.stack([left[1] * right[2] - left[2] * right[1], left[2] * right[0] - left[0] * right[2], left[0] * right[1] - left[1] * right[0]])

def tet_terms(adj_tet, state_tet, coords, weights, live):
    velocity, speed_sq, pressure = flow_split(state_tet)
    volume_weight = pressure * adj_tet[4]
    face_weight = pressure * adj_tet[1:4]
    corner = [coords[k] for k in range(4)]
    edge_one = corner[1] - corner[0]
    edge_two = corner[2] - corner[0]
    edge_three = corner[3] - corner[0]
    grad_one = cross_product(edge_two, edge_three) / 6.0
    grad_two = cross_product(edge_three, edge_one) / 6.0
    grad_three = cross_product(edge_one, edge_two) / 6.0
    grad_zero = -(grad_one + grad_two + grad_three)
    side_one = corner[2] - corner[1]
    side_two = corner[3] - corner[1]
    face_two = 0.5 * cross_product(side_two, face_weight)
    face_three = 0.5 * cross_product(face_weight, side_one)
    face_one = -(face_two + face_three)
    terms = jnp.stack([volume_weight * grad_zero, volume_weight * grad_one + face_one, volume_weight * grad_two + face_two, volume_weight * grad_three + face_three])
    return terms * (weights * live)[:, None, :]

def reference(adjoint_init, adjoint_rhs, flow_state, face_weights, pseudo_time, tet_coords, tet_weights, tet_cell, tet_vertex, tet_count):
    column_pos = jnp.arange(NYZ, dtype=jnp.int32) % EDGE
    keep_upper = (column_pos != EDGE - 1).astype(jnp.float32)
    keep_lower = (column_pos != 0).astype(jnp.float32)
    zero_span = jnp.zeros((5, EDGE), jnp.float32)
    zero_single = jnp.zeros((5, 1), jnp.float32)

    def sweep_once(adjoint):
        padded = jnp.pad(adjoint, ((0, 0), (1, 1), (0, 0)))

        def plane(row):
            here = lax.dynamic_index_in_dim(padded, row + 1, 1, keepdims=False)
            above = lax.dynamic_index_in_dim(padded, row + 2, 1, keepdims=False)
            below = lax.dynamic_index_in_dim(padded, row, 1, keepdims=False)
            state = lax.dynamic_index_in_dim(flow_state, row, 1, keepdims=False)
            faces = lax.dynamic_index_in_dim(face_weights, row, 1, keepdims=False)
            pseudo = lax.dynamic_index_in_dim(pseudo_time, row, 0, keepdims=False)
            rhs = lax.dynamic_index_in_dim(adjoint_rhs, row, 1, keepdims=False)
            neighbours = [above, below, jnp.concatenate([here[:, EDGE:], zero_span], 1), jnp.concatenate([zero_span, here[:, :-EDGE]], 1), jnp.concatenate([here[:, 1:], zero_single], 1) * keep_upper, jnp.concatenate([zero_single, here[:, :-1]], 1) * keep_lower]
            reach, tables = jacobians(state)
            return relax_cells(reach, tables, faces, pseudo, rhs, neighbours)
        planes = lax.map(plane, jnp.arange(NX, dtype=jnp.int32))
        return jnp.transpose(planes, (1, 0, 2))
    adjoint = adjoint_init
    for sweep_index in range(SWEEPS):
        adjoint = sweep_once(adjoint)
    index = jnp.arange(TETS, dtype=jnp.int32)
    source = index // TET_DEV
    slot = index % TET_DEV
    owner_slot = slot // CAP
    live = (slot % CAP < tet_count[source, owner_slot]).astype(jnp.float32)
    group = source // OWNERS
    column = source % OWNERS
    grid_x = group * EDGE + tet_cell // (EDGE * EDGE)
    grid_col = column * (EDGE * EDGE) + tet_cell % (EDGE * EDGE)
    adj_tet = adjoint[:, grid_x, grid_col]
    state_tet = flow_state[:, grid_x, grid_col]
    terms = tet_terms(adj_tet, state_tet, tet_coords, tet_weights, live)
    target = (((group * OWNERS + owner_slot) * VERT_DEV)[None, :] + tet_vertex).reshape(-1)
    data = jnp.transpose(terms, (1, 0, 2)).reshape(3, -1)
    sums = jnp.stack([jax.ops.segment_sum(data[k], target, num_segments=NVERT) for k in range(3)])
    return (adjoint, sums)
```

```python
import functools
import jax
import jax.numpy as jnp
from jax import lax
from jax.experimental import pallas as pl
from jax.experimental.pallas import tpu as pltpu
from jax.sharding import PartitionSpec as P

VERT_DEV = 1536
GAMMA = 1.4
LANES = 128
ROWS = 8
PARTS = VERT_DEV // LANES
F32 = jnp.float32
BF16 = jnp.bfloat16
VMEM = pl.BlockSpec(memory_space=pltpu.VMEM)
SMEM = pl.BlockSpec(memory_space=pltpu.SMEM)
HBM = pl.BlockSpec(memory_space=pl.ANY)
LIMIT = 40 * 1024 * 1024


def call(kernel, outs, in_specs, out_specs, scratch, name, cost=None):
    return pl.pallas_call(
        kernel,
        out_shape=outs,
        in_specs=in_specs,
        out_specs=out_specs,
        scratch_shapes=scratch,
        compiler_params=pltpu.CompilerParams(vmem_limit_bytes=LIMIT),
        cost_estimate=cost,
        name=name,
    )


def is_even(axis):
    return lax.rem(lax.axis_index(axis), 2) == 0


def reach_of(speed_sq, enthalpy):
    sound_sq = (GAMMA - 1.0) * (enthalpy - 0.5 * speed_sq)
    return jnp.sqrt(speed_sq) + jnp.sqrt(sound_sq)


def transposed(vel, enthalpy, half_sq, axis_id, field):
    normal = vel[axis_id]
    energy = normal * field[4]
    common = vel[0] * field[1] + vel[1] * field[2] + vel[2] * field[3] + enthalpy * field[4]
    along = field[1 + axis_id] + energy
    scaled = (GAMMA - 1.0) * along
    out = [half_sq * along - normal * common]
    for j in range(3):
        entry = normal * field[1 + j] - vel[j] * scaled
        if j == axis_id:
            entry = entry + (field[0] + common)
        out.append(entry)
    out.append(scaled + energy)
    return out


def one_sided(vel, enthalpy, axis_id, sign, field):
    speed_sq = vel[0] * vel[0] + vel[1] * vel[1] + vel[2] * vel[2]
    reach = reach_of(speed_sq, enthalpy)
    turned = transposed(vel, enthalpy, 0.5 * (GAMMA - 1.0) * speed_sq, axis_id, field)
    return [sign * turned[k] + reach * field[k] for k in range(5)]


def cell_state(state):
    density, m1, m2, m3, energy = state
    inverse = 1.0 / density
    vel = [m1 * inverse, m2 * inverse, m3 * inverse]
    speed_sq = vel[0] * vel[0] + vel[1] * vel[1] + vel[2] * vel[2]
    pressure = (GAMMA - 1.0) * (energy - 0.5 * density * speed_sq)
    enthalpy = (energy + pressure) * inverse
    reach = jnp.sqrt(speed_sq) + jnp.sqrt(GAMMA * pressure * inverse)
    return vel, speed_sq, pressure, enthalpy, reach


def sweep_tile(grid, row, lane, edge, vel, speed_sq, enthalpy, reach, faces, rhs):
    def at(k, drow, dlane):
        return grid[k, pl.ds(row + drow, ROWS), pl.ds(lane + dlane, LANES)]

    place = lax.broadcasted_iota(jnp.int32, (ROWS, LANES), 1)
    depth = lax.rem(place, edge)
    first = place < edge
    last = place >= LANES - edge
    zero = jnp.zeros((ROWS, LANES), F32)
    faces = list(faces)
    faces[4] = jnp.where(depth == edge - 1, zero, faces[4])
    faces[5] = jnp.where(depth == 0, zero, faces[5])
    here = [at(k, 0, 0) for k in range(5)]
    spread = None
    total = None
    for axis_id in range(3):
        if axis_id == 0:
            upper = [at(k, 1, 0) for k in range(5)]
            lower = [at(k, -1, 0) for k in range(5)]
        elif axis_id == 1:
            upper = [
                pltpu.roll(jnp.where(first, at(k, 0, LANES), here[k]), LANES - edge, 1) for k in range(5)
            ]
            lower = [pltpu.roll(jnp.where(last, at(k, 0, -LANES), here[k]), edge, 1) for k in range(5)]
        else:
            upper = [pltpu.roll(here[k], LANES - 1, 1) for k in range(5)]
            lower = [pltpu.roll(here[k], 1, 1) for k in range(5)]
        upper = [faces[2 * axis_id] * v for v in upper]
        lower = [faces[2 * axis_id + 1] * v for v in lower]
        both = [u + v for u, v in zip(upper, lower)]
        difference = [u - v for u, v in zip(upper, lower)]
        spread = both if spread is None else [u + v for u, v in zip(spread, both)]
        turned = transposed(vel, enthalpy, 0.5 * (GAMMA - 1.0) * speed_sq, axis_id, difference)
        total = turned if total is None else [u + v for u, v in zip(total, turned)]
    return [rhs[k] + total[k] + reach * spread[k] for k in range(5)]


def tile_coefficients(i_half, rows, lanes, state_ref, face_tiles, pseudo_ref, rhs_ref):
    state = [state_ref[k, rows, lanes] for k in range(5)]
    vel, speed_sq, pressure, enthalpy, reach = cell_state(state)
    faces = [f[i_half * ROWS : (i_half + 1) * ROWS] for f in face_tiles]
    area = faces[0]
    for f in faces[1:]:
        area = area + f
    inverse = 1.0 / (pseudo_ref[rows, lanes] + 0.5 * reach * area)
    half = 0.5 * inverse
    faces = [half * f for f in faces]
    rhs = [rhs_ref[k, rows, lanes] * inverse for k in range(5)]
    return vel, speed_sq, pressure, enthalpy, reach, faces, rhs


def clear_pads(grid, edge, span):
    high = grid.shape[1]
    wide = grid.shape[2]
    for k in range(5):
        grid[k, 0:ROWS, :] = jnp.zeros((ROWS, wide), F32)
        grid[k, ROWS + edge : high, :] = jnp.zeros((high - ROWS - edge, wide), F32)
        grid[k, ROWS : ROWS + edge, 0:LANES] = jnp.zeros((edge, LANES), F32)
        grid[k, ROWS : ROWS + edge, LANES + span : wide] = jnp.zeros((edge, LANES), F32)


def for_each_tile(edge, span, body):
    for top in range(0, edge, 2 * ROWS):

        def step(j, carry, top=top):
            body(top, pl.multiple_of(j * LANES, LANES))
            return carry

        lax.fori_loop(0, span // LANES, step, 0)


def first_kernel(
    adjoint_ref, rhs_ref, state_ref, face_ref, pseudo_ref,
    part_ref, xa_ref, xb_ref, ylo_ref, yhi_ref,
    grid, coef, xsides, sem,
):
    edge, span = pseudo_ref.shape
    copy = pltpu.make_async_copy(
        adjoint_ref, grid.at[:, pl.ds(ROWS, edge), pl.ds(LANES, span)], sem
    )
    copy.start()
    clear_pads(grid, edge, span)
    copy.wait()

    def body(top, offset):
        lanes = pl.ds(offset, LANES)
        face_tiles = [face_ref[d, pl.ds(top, 2 * ROWS), lanes].astype(F32) for d in range(6)]
        for i_half in range(2):
            rows = pl.ds(top + i_half * ROWS, ROWS)
            vel, speed_sq, pressure, enthalpy, reach, faces, rhs = tile_coefficients(
                i_half, rows, lanes, state_ref, face_tiles, pseudo_ref, rhs_ref
            )
            out = sweep_tile(
                grid, ROWS + top + i_half * ROWS, pl.multiple_of(LANES + offset, LANES), edge,
                vel, speed_sq, enthalpy, reach, faces, rhs,
            )
            for k in range(5):
                part_ref[k, rows, lanes] = out[k]
            for k, value in enumerate(vel + [enthalpy] + faces[:4]):
                coef[k, rows, lanes] = value

    for_each_tile(edge, span, body)

    even = is_even("grp")
    place = lax.broadcasted_iota(jnp.int32, (1, span), 1)
    for side, row in ((0, 0), (1, edge - 1)):
        slot = jnp.where(even, 1 - side, side)
        at = slice(row, row + 1)
        message = [part_ref[k, at, :] for k in range(5)]
        message += [grid[k, ROWS + row : ROWS + row + 1, LANES : LANES + span] for k in range(5)]
        message += [coef[4 + 1 - side, at, :]]
        message += [coef[k, at, :] for k in range(4)]
        message += [jnp.where(place < edge, coef[7, at, :], coef[6, at, :])]
        for k, value in enumerate(message):
            xsides[slot, k : k + 1, :] = value
    xa_ref[...] = xsides[0]
    xb_ref[...] = xsides[1]

    lane = lax.broadcasted_iota(jnp.int32, (edge, LANES), 1)
    quarter = lane // edge
    for side, base, ref in ((0, 0, ylo_ref), (1, span - LANES, yhi_ref)):
        lanes = slice(base, base + LANES)
        fields = [part_ref[k, :, lanes] for k in range(5)]
        fields += [grid[k, ROWS : ROWS + edge, LANES + base : LANES + base + LANES] for k in range(5)]
        fields += [coef[6 + 1 - side, :, lanes]]
        fields += [coef[k, :, lanes] for k in range(4)]
        start = 0 if side == 0 else LANES - edge
        per = LANES // edge
        for g in range(4):
            packed = None
            for q in range(per):
                k = g * per + q
                if k >= len(fields):
                    value = jnp.zeros((edge, LANES), F32)
                else:
                    shift = (q * edge - start) % LANES
                    value = pltpu.roll(fields[k], shift, 1) if shift else fields[k]
                packed = value if packed is None else jnp.where(quarter == q, value, packed)
            ref[g] = packed


def meet(axis_id, side, own, other):
    sign = 1.0 if side == 1 else -1.0
    mine = one_sided(own[11:14], own[14], axis_id, sign, other[5:10])
    theirs = one_sided(other[11:14], other[14], axis_id, -sign, own[5:10])
    added = [own[10] * v for v in mine]
    finished = [other[k] + other[10] * theirs[k] for k in range(5)]
    return added, finished


def second_kernel(xa_ref, xb_ref, ra_ref, rb_ref, ylo_ref, yhi_ref, res_ref, ya_ref, yb_ref, ysides):
    span = xa_ref.shape[1]
    edge = ylo_ref.shape[1]
    per = LANES // edge
    even = is_even("grp")
    even_y = is_even("blk")
    ysides[0] = ylo_ref[...]
    ysides[1] = yhi_ref[...]
    lane = lax.broadcasted_iota(jnp.int32, (1, LANES), 1)
    quarter = lane // edge

    def pick(a_ref, b_ref, flag):
        return [jnp.where(flag, a_ref[k : k + 1, :], b_ref[k : k + 1, :]) for k in range(15)]

    for side in (0, 1):
        flag = even if side == 1 else jnp.logical_not(even)
        own = pick(xa_ref, xb_ref, flag)
        other = pick(ra_ref, rb_ref, flag)
        added, finished = meet(0, side, own, other)
        row = 0 if side == 0 else edge - 1
        for k in range(5):
            res_ref[side, k : k + 1, :] = added[k]
            res_ref[side, 5 + k : 6 + k, :] = finished[k]
        for ys, base, start in ((0, 0, 0), (1, span - LANES, LANES - edge)):
            for k in range(5):
                g, q = divmod(k, per)
                shift = (q * edge - start) % LANES
                piece = added[k][:, base : base + LANES]
                piece = pltpu.roll(piece, shift, 1) if shift else piece
                old = ysides[ys, g, row : row + 1, :]
                ysides[ys, g, row : row + 1, :] = old + jnp.where(quarter == q, piece, 0.0)
                g, q = divmod(15, per)
                shift = (q * edge - start) % LANES
                piece = other[5 + k][:, base : base + LANES]
                piece = pltpu.roll(piece, shift, 1) if shift else piece
                at = 2 * k + side
                old = ysides[ys, g, at : at + 1, :]
                ysides[ys, g, at : at + 1, :] = jnp.where(quarter == q, piece, old)
    ya_ref[...] = ysides[jnp.where(even_y, 1, 0)]
    yb_ref[...] = ysides[jnp.where(even_y, 0, 1)]


def cross(left, right):
    return [
        left[1] * right[2] - left[2] * right[1],
        left[2] * right[0] - left[0] * right[2],
        left[0] * right[1] - left[1] * right[0],
    ]


def minus(left, right):
    return [u - v for u, v in zip(left, right)]


def tet_terms(volume, face, corner, weights):
    edge_one = minus(corner[1], corner[0])
    edge_two = minus(corner[2], corner[0])
    edge_three = minus(corner[3], corner[0])
    sixth = volume * (1.0 / 6.0)
    g1 = [sixth * v for v in cross(edge_two, edge_three)]
    g2 = [sixth * v for v in cross(edge_three, edge_one)]
    g3 = [sixth * v for v in cross(edge_one, edge_two)]
    side_one = minus(corner[2], corner[1])
    side_two = minus(corner[3], corner[1])
    half = [0.5 * v for v in face]
    h2 = cross(side_two, half)
    h3 = cross(half, side_one)
    terms = [[], [], [], []]
    for k in range(3):
        terms[0].append(-weights[0] * (g1[k] + g2[k] + g3[k]))
        terms[1].append(weights[1] * (g1[k] - (h2[k] + h3[k])))
        terms[2].append(weights[2] * (g2[k] + h2[k]))
        terms[3].append(weights[3] * (g3[k] + h3[k]))
    return terms


def split(value):
    high = value.astype(BF16)
    return high, (value - high.astype(F32)).astype(BF16)


def hot(shape, index):
    rows = lax.broadcasted_iota(jnp.int32, shape, 0)
    return jnp.where(rows == index, 1.0, 0.0).astype(BF16)


def third_kernel(
    part_ref, rhs_ref, state_ref, face_ref, pseudo_ref, res_ref, ra_ref, rb_ref, ya_ref, yb_ref, sa_ref, sb_ref,
    coord_ref, weight_ref, cell_ref, vertex_ref, count_ref,
    out_ref, keep_ref, send_ref,
    grid, field, high, low, sums, sem,
):
    edge, span = pseudo_ref.shape
    per = LANES // edge
    owners = count_ref.shape[1]
    slots = weight_ref.shape[1]
    capacity = slots // owners
    copy = pltpu.make_async_copy(
        part_ref, grid.at[:, pl.ds(ROWS, edge), pl.ds(LANES, span)], sem.at[0]
    )
    copy.start()
    even = is_even("grp")
    even_y = is_even("blk")
    for k in range(5):
        for side, row in ((0, ROWS - 1), (1, ROWS + edge)):
            grid[k, row : row + 1, LANES : LANES + span] = res_ref[side, 5 + k : 6 + k, :]
    copy.wait()
    for k in range(5):
        for side, row in ((0, ROWS), (1, ROWS + edge - 1)):
            at = (k, slice(row, row + 1), slice(LANES, LANES + span))
            grid[at] = grid[at] + res_ref[side, k : k + 1, :]

    lane = lax.broadcasted_iota(jnp.int32, (edge, LANES), 1)
    lane_row = lax.broadcasted_iota(jnp.int32, (1, LANES), 1)

    def pick(a_ref, b_ref, flag, k):
        g, q = divmod(k, per)
        value = jnp.where(flag, a_ref[g], b_ref[g])
        return pltpu.roll(value, LANES - q * edge, 1) if q else value

    for side in (0, 1):
        flag = even_y if side == 1 else jnp.logical_not(even_y)
        own = [pick(ya_ref, yb_ref, flag, k) for k in range(15)]
        other = [pick(sa_ref, sb_ref, flag, k) for k in range(16)]
        added, finished = meet(1, side, own, other[:15])
        base = LANES if side == 0 else span
        beyond = 0 if side == 0 else LANES + span
        rows = slice(ROWS, ROWS + edge)
        for k in range(5):
            if side == 0:
                extra = jnp.where(lane < edge, added[k], 0.0)
                halo = pltpu.roll(finished[k], LANES - edge, 1)
            else:
                extra = jnp.where(lane >= LANES - edge, pltpu.roll(added[k], LANES - edge, 1), 0.0)
                halo = finished[k]
            at = (k, rows, slice(base, base + LANES))
            grid[at] = grid[at] + extra
            grid[k, rows, beyond : beyond + LANES] = halo
        start = 0 if side == 0 else span - LANES
        for xs, row in ((0, ROWS - 1), (1, ROWS + edge)):
            flag_x = even if xs == 1 else jnp.logical_not(even)
            lanes = slice(start, start + LANES)
            state = [jnp.where(flag_x, ra_ref[k : k + 1, lanes], rb_ref[k : k + 1, lanes]) for k in range(11, 16)]
            corner = [other[15][2 * k + xs : 2 * k + xs + 1, :] for k in range(5)]
            if side == 1:
                corner = [pltpu.roll(v, LANES - edge, 1) for v in corner]
            extra = one_sided(state[:3], state[3], 1, 1.0 if side == 1 else -1.0, corner)
            inside = lane_row < edge if side == 0 else lane_row >= LANES - edge
            for k in range(5):
                at = (k, slice(row, row + 1), slice(base, base + LANES))
                grid[at] = grid[at] + jnp.where(inside, state[4] * extra[k], 0.0)

    def body(top, offset):
        lanes = pl.ds(offset, LANES)
        face_tiles = [face_ref[d, pl.ds(top, 2 * ROWS), lanes].astype(F32) for d in range(6)]
        tables = [[], [], [], []]
        for i_half in range(2):
            rows = pl.ds(top + i_half * ROWS, ROWS)
            vel, speed_sq, pressure, enthalpy, reach, faces, rhs = tile_coefficients(
                i_half, rows, lanes, state_ref, face_tiles, pseudo_ref, rhs_ref
            )
            out = sweep_tile(
                grid, ROWS + top + i_half * ROWS, pl.multiple_of(LANES + offset, LANES), edge,
                vel, speed_sq, enthalpy, reach, faces, rhs,
            )
            for k in range(5):
                field[k, rows, lanes] = out[k]
            for k in range(4):
                tables[k].append(pressure * out[1 + k])
        column = offset // (2 * LANES)
        wide = pl.ds(pl.multiple_of(lax.rem(offset, 2 * LANES), LANES), LANES)
        for k in range(4):
            big, small = split(jnp.concatenate(tables[k], axis=0))
            at = pl.ds(pl.multiple_of(k * (high.shape[0] // 4) + column * edge + top, 2 * ROWS), 2 * ROWS)
            high[at, wide] = big
            low[at, wide] = small

    for_each_tile(edge, span, body)
    store = pltpu.make_async_copy(field, out_ref, sem.at[1])
    store.start()

    table_rows = high.shape[0] // 4
    width = 2 * LANES
    step = min(slots, 512)
    gathered = [[], [], [], []]
    for s in range(0, slots, step):
        cell = cell_ref[:, s : s + step]
        x = cell // span
        yz = lax.rem(cell, span)
        row = (yz // width) * edge + x
        column = hot((width, step), lax.rem(yz, width))
        product = jnp.dot(high[...], column, preferred_element_type=F32)
        product = product + jnp.dot(low[...], column, preferred_element_type=F32)
        here = lax.broadcasted_iota(jnp.int32, (table_rows, step), 0) == row
        for k in range(4):
            piece = product[k * table_rows : (k + 1) * table_rows]
            gathered[k].append(jnp.sum(jnp.where(here, piece, 0.0), axis=0, keepdims=True))
    gathered = [jnp.concatenate(v, axis=1) for v in gathered]

    group = max(capacity, LANES)
    together = group // capacity
    vertex_rows = -(-together * PARTS // 16) * 16
    lane_group = lax.broadcasted_iota(jnp.int32, (1, group), 1)
    chunk = lane_group // capacity
    within = lax.rem(lane_group, capacity)
    for s in range(0, slots // group):
        lanes = slice(s * group, (s + 1) * group)
        count = count_ref[0, s * together]
        for q in range(1, together):
            count = jnp.where(chunk == q, count_ref[0, s * together + q], count)
        live = jnp.where(within < count, 1.0, 0.0)
        corner = [[coord_ref[c, k : k + 1, lanes] for k in range(3)] for c in range(4)]
        weights = [weight_ref[c : c + 1, lanes] * live for c in range(4)]
        terms = tet_terms(gathered[3][:, lanes], [gathered[k][:, lanes] for k in range(3)], corner, weights)
        left, right = [], []
        for c in range(4):
            vertex = vertex_ref[c : c + 1, lanes]
            row = vertex // LANES + chunk * PARTS
            match = lax.broadcasted_iota(jnp.int32, (vertex_rows, group), 0) == row
            blocks = []
            for k in range(3):
                blocks += split(jnp.where(match, terms[c][k], 0.0))
            left.append(jnp.concatenate(blocks, axis=0))
            right.append(hot((LANES, group), lax.rem(vertex, LANES)))
        product = lax.dot_general(
            jnp.concatenate(left, axis=1), jnp.concatenate(right, axis=1),
            (((1,), (1,)), ((), ())), preferred_element_type=F32,
        )
        for k in range(3):
            big = product[2 * k * vertex_rows : (2 * k + 1) * vertex_rows]
            small = product[(2 * k + 1) * vertex_rows : (2 * k + 2) * vertex_rows]
            total = big + small
            for q in range(together):
                owner = s * together + q
                sums[owner % 2, owner // 2, k * PARTS : (k + 1) * PARTS, :] = total[q * PARTS : (q + 1) * PARTS]
    core = lax.rem(lax.axis_index("blk"), 2)
    keep_ref[...] = sums[core]
    send_ref[...] = sums[1 - core]
    store.wait()


def fourth_kernel(keep_ref, got_ref, mine_ref, *refs):
    count = keep_ref.shape[0]
    me = lax.rem(lax.axis_index("blk") // 2, count)
    mine_ref[...] = keep_ref[me] + got_ref[me]
    for k, ref in enumerate(refs):
        partner = lax.bitwise_xor(me, k + 1)
        ref[...] = keep_ref[partner] + got_ref[partner]


def last_kernel(*refs):
    total = refs[0][...]
    for ref in refs[1:-1]:
        total = total + ref[...]
    for k in range(3):
        for part in range(PARTS):
            at = k * PARTS + part
            refs[-1][k : k + 1, part * LANES : (part + 1) * LANES] = total[at : at + 1, :]


def swap(value, axis, pairs):
    return lax.ppermute(value, axis, pairs + [(b, a) for a, b in pairs])


def neighbours(value_a, value_b, axis):
    count = lax.axis_size(axis)
    first = [(i, i + 1) for i in range(0, count - 1, 2)]
    second = [(i, i + 1) for i in range(1, count - 1, 2)]
    return swap(value_a, axis, first), swap(value_b, axis, second)


def local(
    adjoint_init, adjoint_rhs, flow_state, face_weights, pseudo_time,
    tet_coords, tet_weights, tet_cell, tet_vertex, tet_count,
):
    edge, span = pseudo_time.shape
    owners = tet_count.shape[1]
    blocks = lax.axis_size("blk")
    padded = (5, edge + 2 * ROWS, span + 2 * LANES)
    struct = jax.ShapeDtypeStruct
    packed = (16 * edge // LANES, edge, LANES)
    part, xa, xb, ylo, yhi = call(
        first_kernel,
        [struct((5, edge, span), F32), struct((16, span), F32), struct((16, span), F32),
         struct(packed, F32), struct(packed, F32)],
        [HBM, VMEM, VMEM, VMEM, VMEM],
        [VMEM] * 5,
        [pltpu.VMEM(padded, F32), pltpu.VMEM((8, edge, span), F32), pltpu.VMEM((2, 16, span), F32),
         pltpu.SemaphoreType.DMA],
        "partial_sweep",
    )(adjoint_init, adjoint_rhs, flow_state, face_weights, pseudo_time)
    ra, rb = neighbours(xa, xb, "grp")
    res, ya, yb = call(
        second_kernel,
        [struct((2, 16, span), F32), struct(packed, F32), struct(packed, F32)],
        [VMEM] * 6,
        [VMEM] * 3,
        [pltpu.VMEM((2,) + packed, F32)],
        "streamwise_halo",
    )(xa, xb, ra, rb, ylo, yhi)
    sa, sb = neighbours(ya, yb, "blk")
    half = owners // 2
    sums_shape = (half, 3 * PARTS, LANES)
    table = (4 * edge * span // (2 * LANES), 2 * LANES)
    adjoint, keep, send = call(
        third_kernel,
        [struct((5, edge, span), F32), struct(sums_shape, F32), struct(sums_shape, F32)],
        [HBM] + [VMEM] * 15 + [SMEM],
        [HBM, VMEM, VMEM],
        [pltpu.VMEM(padded, F32), pltpu.VMEM((5, edge, span), F32), pltpu.VMEM(table, BF16),
         pltpu.VMEM(table, BF16), pltpu.VMEM((2,) + sums_shape, F32), pltpu.SemaphoreType.DMA((2,))],
        "last_sweep_and_tets",
    )(
        part, adjoint_rhs, flow_state, face_weights, pseudo_time, res, ra, rb, ya, yb, sa, sb,
        tet_coords, tet_weights, tet_cell.reshape(1, -1), tet_vertex, tet_count,
    )
    got = swap(send, "blk", [(i, i + 1) for i in range(0, blocks, 2)])
    place = lax.axis_index("blk") // 2
    while half > 4:
        half //= 2
        both = (keep + got).reshape(2, half, 3 * PARTS, LANES)
        bit = lax.rem(place // half, 2)
        keep = lax.dynamic_index_in_dim(both, bit, 0, keepdims=False)
        send = lax.dynamic_index_in_dim(both, 1 - bit, 0, keepdims=False)
        got = lax.ppermute(send, "blk", [(i, i ^ (2 * half)) for i in range(blocks)])
    one = struct((3 * PARTS, LANES), F32)
    mine, *others = call(
        fourth_kernel, [one] * half, [VMEM] * 2, [VMEM] * half, [], "core_pair_sums"
    )(keep, got)
    others = [
        lax.ppermute(v, "blk", [(i, i ^ (2 * (k + 1))) for i in range(blocks)]) for k, v in enumerate(others)
    ]
    sensitivity = call(
        last_kernel, struct((3, VERT_DEV), F32), [VMEM] * half, VMEM, [], "own_sums"
    )(mine, *others)
    return adjoint, sensitivity


def solution(mesh):
    return jax.shard_map(
        local,
        mesh=mesh,
        in_specs=(
            P(None, "grp", "blk"),
            P(None, "grp", "blk"),
            P(None, "grp", "blk"),
            P(None, "grp", "blk"),
            P("grp", "blk"),
            P(None, None, ("grp", "blk")),
            P(None, ("grp", "blk")),
            P(("grp", "blk")),
            P(None, ("grp", "blk")),
            P(("grp", "blk"), None),
        ),
        out_specs=(P(None, "grp", "blk"), P(None, ("grp", "blk"))),
        check_vma=False,
    )
```

```python
import functools
import jax
import jax.numpy as jnp
from jax import lax
from jax.experimental import pallas as pl
from jax.experimental.pallas import tpu as pltpu
from jax.sharding import PartitionSpec as P

VERT_DEV = 1536
GAMMA = 1.4
LANES = 128
ROWS = 8
PARTS = VERT_DEV // LANES
F32 = jnp.float32
BF16 = jnp.bfloat16
VMEM = pl.BlockSpec(memory_space=pltpu.VMEM)
SMEM = pl.BlockSpec(memory_space=pltpu.SMEM)
HBM = pl.BlockSpec(memory_space=pltpu.HBM)
LIMIT = 40 * 1024 * 1024


def call(kernel, outs, in_specs, out_specs, scratch, name, flops=1000, aliases={}):
    return pl.pallas_call(
        kernel,
        out_shape=outs,
        in_specs=in_specs,
        out_specs=out_specs,
        scratch_shapes=scratch,
        compiler_params=pltpu.CompilerParams(vmem_limit_bytes=LIMIT),
        cost_estimate=pl.CostEstimate(flops=flops, bytes_accessed=flops // 4, transcendentals=0),
        input_output_aliases=aliases,
        name=name,
    )


def is_even(axis):
    return lax.rem(lax.axis_index(axis), 2) == 0


def reach_of(speed_sq, enthalpy):
    sound_sq = (GAMMA - 1.0) * (enthalpy - 0.5 * speed_sq)
    return jnp.sqrt(speed_sq) + jnp.sqrt(sound_sq)


def transposed(vel, enthalpy, half_sq, axis_id, field):
    normal = vel[axis_id]
    energy = normal * field[4]
    common = vel[0] * field[1] + vel[1] * field[2] + vel[2] * field[3] + enthalpy * field[4]
    along = field[1 + axis_id] + energy
    scaled = (GAMMA - 1.0) * along
    out = [half_sq * along - normal * common]
    for j in range(3):
        entry = normal * field[1 + j] - vel[j] * scaled
        if j == axis_id:
            entry = entry + (field[0] + common)
        out.append(entry)
    out.append(scaled + energy)
    return out


def one_sided(vel, enthalpy, axis_id, sign, field):
    speed_sq = vel[0] * vel[0] + vel[1] * vel[1] + vel[2] * vel[2]
    reach = reach_of(speed_sq, enthalpy)
    turned = transposed(vel, enthalpy, 0.5 * (GAMMA - 1.0) * speed_sq, axis_id, field)
    return [sign * turned[k] + reach * field[k] for k in range(5)]


def cell_state(state):
    density, m1, m2, m3, energy = state
    inverse = 1.0 / density
    vel = [m1 * inverse, m2 * inverse, m3 * inverse]
    speed_sq = vel[0] * vel[0] + vel[1] * vel[1] + vel[2] * vel[2]
    pressure = (GAMMA - 1.0) * (energy - 0.5 * density * speed_sq)
    enthalpy = (energy + pressure) * inverse
    reach = jnp.sqrt(speed_sq) + jnp.sqrt(GAMMA * pressure * inverse)
    return vel, speed_sq, pressure, enthalpy, reach


def combine(rhs, reach, vel, speed_sq, enthalpy, faces, pairs):
    spread = None
    total = None
    for axis_id, (upper, lower) in enumerate(pairs):
        upper = [faces[2 * axis_id] * v for v in upper]
        lower = [faces[2 * axis_id + 1] * v for v in lower]
        both = [u + v for u, v in zip(upper, lower)]
        difference = [u - v for u, v in zip(upper, lower)]
        spread = both if spread is None else [u + v for u, v in zip(spread, both)]
        turned = transposed(vel, enthalpy, 0.5 * (GAMMA - 1.0) * speed_sq, axis_id, difference)
        total = turned if total is None else [u + v for u, v in zip(total, turned)]
    return [rhs[k] + total[k] + reach * spread[k] for k in range(5)]


def inside_faces(faces, edge, shape):
    depth = lax.rem(lax.broadcasted_iota(jnp.int32, shape, 1), edge)
    faces = list(faces)
    faces[4] = jnp.where(depth == edge - 1, 0.0, faces[4])
    faces[5] = jnp.where(depth == 0, 0.0, faces[5])
    return faces


def lane_pairs(here, after, before, edge, shape):
    place = lax.broadcasted_iota(jnp.int32, shape, 1)
    first = place < edge
    last = place >= LANES - edge
    along_y = (
        [pltpu.roll(jnp.where(first, a, h), LANES - edge, 1) for h, a in zip(here, after)],
        [pltpu.roll(jnp.where(last, b, h), edge, 1) for h, b in zip(here, before)],
    )
    along_z = ([pltpu.roll(h, LANES - 1, 1) for h in here], [pltpu.roll(h, 1, 1) for h in here])
    return along_y, along_z


def sweep_tile(grid, row, lane, edge, vel, speed_sq, enthalpy, reach, faces, rhs):
    def at(drow, dlane):
        return [grid[k, pl.ds(row + drow, ROWS), pl.ds(lane + dlane, LANES)] for k in range(5)]

    shape = (ROWS, LANES)
    pairs = lane_pairs(at(0, 0), at(0, LANES), at(0, -LANES), edge, shape)
    return combine(
        rhs, reach, vel, speed_sq, enthalpy, inside_faces(faces, edge, shape), ((at(1, 0), at(-1, 0)),) + pairs
    )


def coefficients(state, faces, pseudo, rhs):
    vel, speed_sq, pressure, enthalpy, reach = cell_state(state)
    area = faces[0]
    for f in faces[1:]:
        area = area + f
    inverse = 1.0 / (pseudo + 0.5 * reach * area)
    half = 0.5 * inverse
    return vel, speed_sq, pressure, enthalpy, reach, [half * f for f in faces], [inverse * v for v in rhs]


def tile_coefficients(i_half, rows, lanes, state_ref, face_tiles, pseudo_ref, rhs_ref):
    return coefficients(
        [state_ref[k, rows, lanes] for k in range(5)],
        [f[i_half * ROWS : (i_half + 1) * ROWS] for f in face_tiles],
        pseudo_ref[rows, lanes],
        [rhs_ref[k, rows, lanes] for k in range(5)],
    )


def clear_pads(grid, edge, span):
    high = grid.shape[1]
    wide = grid.shape[2]
    for k in range(5):
        grid[k, 0:ROWS, :] = jnp.zeros((ROWS, wide), F32)
        grid[k, ROWS + edge : high, :] = jnp.zeros((high - ROWS - edge, wide), F32)
        grid[k, ROWS : ROWS + edge, 0:LANES] = jnp.zeros((edge, LANES), F32)
        grid[k, ROWS : ROWS + edge, LANES + span : wide] = jnp.zeros((edge, LANES), F32)


def for_each_tile(edge, first, last, body):
    for top in range(0, edge, 2 * ROWS):

        def step(j, carry, top=top):
            body(top, pl.multiple_of(j * LANES, LANES))
            return carry

        lax.fori_loop(first, last, step, 0)


def plane_kernel(
    adjoint_hbm, rhs_hbm, state_hbm, face_hbm, pseudo_hbm,
    xa_ref, xb_ref,
    adjoint_ref, rhs_ref, state_ref, face_ref, pseudo_ref, xsides, sem,
):
    edge, span = pseudo_hbm.shape
    copies = [pltpu.make_async_copy(face_hbm, face_ref, sem.at[0])]
    for source, target in (
        (state_hbm, state_ref), (adjoint_hbm, adjoint_ref), (rhs_hbm, rhs_ref), (pseudo_hbm, pseudo_ref)
    ):
        for side in (0, 1):
            there = pl.ds(side * (edge - ROWS), ROWS)
            here = pl.ds(side * ROWS, ROWS)
            whole = (slice(None),) * (len(source.shape) - 2)
            copies.append(
                pltpu.make_async_copy(
                    source.at[whole + (there,)], target.at[whole + (here,)], sem.at[len(copies)]
                )
            )
    for copy in copies:
        copy.start()
    for copy in copies:
        copy.wait()
    even = is_even("grp")
    shape = (2, LANES)
    upper_row = lax.broadcasted_iota(jnp.int32, shape, 0) == 1
    sub = lax.broadcasted_iota(jnp.int32, (ROWS, LANES), 0)
    place = lax.broadcasted_iota(jnp.int32, shape, 1)
    tiles = span // LANES
    zero = jnp.zeros(shape, F32)

    def planes(ref, k, j, inner=0):
        at = (k,) if k is not None else ()
        lanes = slice(j * LANES, (j + 1) * LANES)
        last = 2 * ROWS - 2 - inner
        return jnp.where(upper_row, ref[at + (slice(last, last + 2), lanes)], ref[at + (slice(inner, inner + 2), lanes)])

    for j in range(tiles):
        lanes = pl.ds(j * LANES, LANES)
        faces = []
        for d in range(6):
            low = face_ref[d, pl.ds(0, 2 * ROWS), lanes].astype(F32)[:ROWS]
            high = face_ref[d, pl.ds(edge - 2 * ROWS, 2 * ROWS), lanes].astype(F32)[ROWS:]
            faces.append(jnp.where(sub == 0, low, pltpu.roll(high, 2, 0))[:2])
        vel, speed_sq, pressure, enthalpy, reach, faces, rhs = coefficients(
            [planes(state_ref, k, j) for k in range(5)],
            faces,
            planes(pseudo_ref, None, j),
            [planes(rhs_ref, k, j) for k in range(5)],
        )
        here = [planes(adjoint_ref, k, j) for k in range(5)]
        after = [planes(adjoint_ref, k, j + 1) if j + 1 < tiles else zero for k in range(5)]
        before = [planes(adjoint_ref, k, j - 1) if j > 0 else zero for k in range(5)]
        inner = [planes(adjoint_ref, k, j, 1) for k in range(5)]
        along_x = ([jnp.where(upper_row, 0.0, v) for v in inner], [jnp.where(upper_row, v, 0.0) for v in inner])
        pairs = lane_pairs(here, after, before, edge, shape)
        out = combine(
            rhs, reach, vel, speed_sq, enthalpy, inside_faces(faces, edge, shape), (along_x,) + pairs
        )
        message = out + here + [jnp.where(upper_row, faces[0], faces[1])] + vel + [enthalpy]
        message.append(jnp.where(place < edge, faces[3], faces[2]) if j == 0 else faces[2])
        for side in (0, 1):
            slot = jnp.where(even, 1 - side, side)
            for k, value in enumerate(message):
                xsides[slot, k : k + 1, lanes] = value[side : side + 1]
    xa_ref[...] = xsides[0]
    xb_ref[...] = xsides[1]


def first_kernel(
    adjoint_ref, rhs_ref, state_ref, face_ref, pseudo_ref, coord_ref, weight_ref, cell_ref, vertex_ref, count_ref,
    part_ref, ylo_ref, yhi_ref, column_ref, vertex_hot_ref, shape_ref,
    grid, coef,
):
    edge, span = pseudo_ref.shape
    clear_pads(grid, edge, span)
    for k in range(5):
        grid[k, ROWS : ROWS + edge, LANES : LANES + span] = adjoint_ref[k]

    def body(top, offset):
        lanes = pl.ds(offset, LANES)
        face_tiles = [face_ref[d, pl.ds(top, 2 * ROWS), lanes].astype(F32) for d in range(6)]
        for i_half in range(2):
            rows = pl.ds(top + i_half * ROWS, ROWS)
            vel, speed_sq, pressure, enthalpy, reach, faces, rhs = tile_coefficients(
                i_half, rows, lanes, state_ref, face_tiles, pseudo_ref, rhs_ref
            )
            out = sweep_tile(
                grid, ROWS + top + i_half * ROWS, pl.multiple_of(LANES + offset, LANES), edge,
                vel, speed_sq, enthalpy, reach, faces, rhs,
            )
            for k in range(5):
                part_ref[k, rows, lanes] = out[k]
            for k, value in enumerate(vel + [enthalpy] + faces[2:4]):
                coef[k, rows, lanes] = value

    for_each_tile(edge, 0, span // LANES, body)

    lane = lax.broadcasted_iota(jnp.int32, (edge, LANES), 1)
    quarter = lane // edge
    for side, base, ref in ((0, 0, ylo_ref), (1, span - LANES, yhi_ref)):
        lanes = slice(base, base + LANES)
        fields = [part_ref[k, :, lanes] for k in range(5)]
        fields += [grid[k, ROWS : ROWS + edge, LANES + base : LANES + base + LANES] for k in range(5)]
        fields += [coef[4 + 1 - side, :, lanes]]
        fields += [coef[k, :, lanes] for k in range(4)]
        start = 0 if side == 0 else LANES - edge
        per = LANES // edge
        for g in range(4):
            packed = None
            for q in range(per):
                k = g * per + q
                if k >= len(fields):
                    value = jnp.zeros((edge, LANES), F32)
                else:
                    shift = (q * edge - start) % LANES
                    value = pltpu.roll(fields[k], shift, 1) if shift else fields[k]
                packed = value if packed is None else jnp.where(quarter == q, value, packed)
            ref[g] = packed

    owners = count_ref.shape[1]
    slots = weight_ref.shape[1]
    capacity = slots // owners
    width = 2 * LANES
    step = min(slots, 512)
    for s in range(0, slots, step):
        part = slice(s, s + step)
        column = lax.rem(cell_ref[:, part] + LANES, width)
        column_ref[:, part] = hot((width, step), column)
        for c in range(4):
            vertex_hot_ref[c, :, part] = hot((LANES, step), lax.rem(vertex_ref[c : c + 1, part], LANES))

    group = max(capacity, LANES)
    together = group // capacity
    lane_group = lax.broadcasted_iota(jnp.int32, (1, group), 1)
    chunk = lane_group // capacity
    within = lax.rem(lane_group, capacity)
    for s in range(0, slots // group):
        lanes = slice(s * group, (s + 1) * group)
        count = count_ref[0, s * together]
        for q in range(1, together):
            count = jnp.where(chunk == q, count_ref[0, s * together + q], count)
        live = jnp.where(within < count, 1.0, 0.0)
        weights = [weight_ref[c : c + 1, lanes] * live for c in range(4)]
        corner = [[coord_ref[k, c : c + 1, lanes] for k in range(3)] for c in range(4)]
        for k, value in enumerate(tet_shapes(corner, weights)):
            shape_ref[k : k + 1, lanes] = value


def meet(axis_id, side, own, other):
    sign = 1.0 if side == 1 else -1.0
    mine = one_sided(own[11:14], own[14], axis_id, sign, other[5:10])
    theirs = one_sided(other[11:14], other[14], axis_id, -sign, own[5:10])
    added = [own[10] * v for v in mine]
    finished = [other[k] + other[10] * theirs[k] for k in range(5)]
    return added, finished


def second_kernel(xa_ref, xb_ref, ra_ref, rb_ref, ylo_ref, yhi_ref, res_ref, ya_ref, yb_ref, ysides):
    span = xa_ref.shape[1]
    edge = ylo_ref.shape[1]
    per = LANES // edge
    even = is_even("grp")
    even_y = is_even("blk")
    ysides[0] = ylo_ref[...]
    ysides[1] = yhi_ref[...]
    lane = lax.broadcasted_iota(jnp.int32, (1, LANES), 1)
    quarter = lane // edge

    def pick(a_ref, b_ref, flag):
        return [jnp.where(flag, a_ref[k : k + 1, :], b_ref[k : k + 1, :]) for k in range(15)]

    for side in (0, 1):
        flag = even if side == 1 else jnp.logical_not(even)
        own = pick(xa_ref, xb_ref, flag)
        other = pick(ra_ref, rb_ref, flag)
        added, finished = meet(0, side, own, other)
        row = 0 if side == 0 else edge - 1
        for k in range(5):
            res_ref[side, k : k + 1, :] = added[k]
            res_ref[side, 5 + k : 6 + k, :] = finished[k]
        for ys, base, start in ((0, 0, 0), (1, span - LANES, LANES - edge)):
            for k in range(5):
                g, q = divmod(k, per)
                shift = (q * edge - start) % LANES
                piece = added[k][:, base : base + LANES]
                piece = pltpu.roll(piece, shift, 1) if shift else piece
                old = ysides[ys, g, row : row + 1, :]
                ysides[ys, g, row : row + 1, :] = old + jnp.where(quarter == q, piece, 0.0)
                g, q = divmod(15, per)
                shift = (q * edge - start) % LANES
                piece = other[5 + k][:, base : base + LANES]
                piece = pltpu.roll(piece, shift, 1) if shift else piece
                at = 2 * k + side
                old = ysides[ys, g, at : at + 1, :]
                ysides[ys, g, at : at + 1, :] = jnp.where(quarter == q, piece, old)
    ya_ref[...] = ysides[jnp.where(even_y, 1, 0)]
    yb_ref[...] = ysides[jnp.where(even_y, 0, 1)]


def cross(left, right):
    return [
        left[1] * right[2] - left[2] * right[1],
        left[2] * right[0] - left[0] * right[2],
        left[0] * right[1] - left[1] * right[0],
    ]


def minus(left, right):
    return [u - v for u, v in zip(left, right)]


def tet_shapes(corner, weights):
    edge_one = minus(corner[1], corner[0])
    edge_two = minus(corner[2], corner[0])
    edge_three = minus(corner[3], corner[0])
    g1 = cross(edge_two, edge_three)
    g2 = cross(edge_three, edge_one)
    g3 = cross(edge_one, edge_two)
    g0 = [-(u + v + w) for u, v, w in zip(g1, g2, g3)]
    sixth = [w * (1.0 / 6.0) for w in weights]
    half = [w * 0.5 for w in weights]
    out = []
    for c, g in enumerate((g0, g1, g2, g3)):
        out += [sixth[c] * v for v in g]
    out += [half[1] * v for v in minus(corner[2], corner[3])]
    out += [half[2] * v for v in minus(corner[3], corner[1])]
    out += [half[3] * v for v in minus(corner[1], corner[2])]
    return out


def tet_terms(volume, face, shape):
    terms = []
    for c in range(4):
        term = [volume * shape[3 * c + k] for k in range(3)]
        if c:
            turned = cross(shape[9 + 3 * c : 12 + 3 * c], face)
            term = [u + v for u, v in zip(term, turned)]
        terms.append(term)
    return terms


def split(value):
    high = value.astype(BF16)
    return high, (value - high.astype(F32)).astype(BF16)


def hot(shape, index):
    rows = lax.broadcasted_iota(jnp.int32, shape, 0)
    return jnp.where(rows == index, 1.0, 0.0).astype(BF16)


def gather(high, low, column_ref, row):
    table_rows = high.shape[0] // 4
    slots = column_ref.shape[1]
    step = min(slots, 512)
    gathered = [[], [], [], []]
    for s in range(0, slots, step):
        column = column_ref[:, s : s + step]
        product = jnp.dot(high[...], column, preferred_element_type=F32)
        product = product + jnp.dot(low[...], column, preferred_element_type=F32)
        here = lax.broadcasted_iota(jnp.int32, (table_rows, step), 0) == row[:, s : s + step]
        for k in range(4):
            piece = product[k * table_rows : (k + 1) * table_rows]
            gathered[k].append(jnp.sum(jnp.where(here, piece, 0.0), axis=0, keepdims=True))
    return [jnp.concatenate(v, axis=1) for v in gathered]


def chunk_of(cell, span):
    yz = lax.rem(cell, span) + LANES
    return cell // span, lax.rem(yz // (2 * LANES), span // (2 * LANES))


def middle_kernel(
    part_ref, rhs_ref, state_ref, face_ref, pseudo_ref, res_ref, column_ref, cell_ref,
    out_ref, gathered_ref,
    grid, field, high, low, sem,
):
    edge, span = pseudo_ref.shape
    tiles = span // LANES
    for k in range(5):
        grid[k, ROWS : ROWS + edge, LANES : LANES + span] = part_ref[k]
    for k in range(5):
        for side, row, beyond in ((0, ROWS, ROWS - 1), (1, ROWS + edge - 1, ROWS + edge)):
            at = (k, slice(row, row + 1), slice(LANES, LANES + span))
            grid[at] = grid[at] + res_ref[side, k : k + 1, :]
            grid[k, beyond : beyond + 1, LANES : LANES + span] = res_ref[side, 5 + k : 6 + k, :]

    def body(top, offset):
        lanes = pl.ds(offset, LANES)
        face_tiles = [face_ref[d, pl.ds(top, 2 * ROWS), lanes].astype(F32) for d in range(6)]
        tables = [[], [], [], []]
        for i_half in range(2):
            rows = pl.ds(top + i_half * ROWS, ROWS)
            vel, speed_sq, pressure, enthalpy, reach, faces, rhs = tile_coefficients(
                i_half, rows, lanes, state_ref, face_tiles, pseudo_ref, rhs_ref
            )
            out = sweep_tile(
                grid, ROWS + top + i_half * ROWS, pl.multiple_of(LANES + offset, LANES), edge,
                vel, speed_sq, enthalpy, reach, faces, rhs,
            )
            for k in range(5):
                field[k, rows, pl.ds(pl.multiple_of(offset - LANES, LANES), LANES)] = out[k]
            for k in range(4):
                tables[k].append(pressure * out[1 + k])
        chunk = (offset - LANES) // (2 * LANES)
        wide = pl.ds(pl.multiple_of(lax.rem(offset - LANES, 2 * LANES), LANES), LANES)
        for k in range(4):
            big, small = split(jnp.concatenate(tables[k], axis=0))
            at = pl.ds(pl.multiple_of(k * (high.shape[0] // 4) + chunk * edge + top, 2 * ROWS), 2 * ROWS)
            high[at, wide] = big
            low[at, wide] = small

    for_each_tile(edge, 1, tiles - 1, body)
    store = pltpu.make_async_copy(field, out_ref.at[:, :, pl.ds(LANES, span - 2 * LANES)], sem)
    store.start()
    x, chunk = chunk_of(cell_ref[...], span)
    row = jnp.where(chunk > 0, (chunk - 1) * edge + x, -1)
    for k, value in enumerate(gather(high, low, column_ref, row)):
        gathered_ref[k : k + 1, :] = value
    store.wait()


def third_kernel(
    adjoint_ref, part_ref, rhs_ref, state_ref, face_ref, pseudo_ref, res_ref, ra_ref, rb_ref,
    ya_ref, yb_ref, sa_ref, sb_ref, gathered_ref, column_ref, cell_ref, vertex_ref, vertex_hot_ref, shape_ref,
    out_ref, keep_ref, send_ref,
    grids, field, high, low, sums, sem,
):
    edge, span = pseudo_ref.shape
    per = LANES // edge
    owners = 2 * keep_ref.shape[0]
    slots = cell_ref.shape[1]
    capacity = slots // owners
    even = is_even("grp")
    even_y = is_even("blk")
    lane = lax.broadcasted_iota(jnp.int32, (edge, LANES), 1)
    lane_row = lax.broadcasted_iota(jnp.int32, (1, LANES), 1)
    rows = slice(ROWS, ROWS + edge)
    stores = []

    def pick(a_ref, b_ref, flag, k):
        g, q = divmod(k, per)
        value = jnp.where(flag, a_ref[g], b_ref[g])
        return pltpu.roll(value, LANES - q * edge, 1) if q else value

    for side in (0, 1):
        grid = grids.at[side]
        start = 0 if side == 0 else span - 2 * LANES
        lanes = slice(start, start + 2 * LANES)
        base = LANES if side == 0 else 0
        into = slice(base, base + 2 * LANES)
        for k in range(5):
            grid[k, rows, into] = part_ref[k, :, lanes]
            for xs, row, beyond in ((0, ROWS, ROWS - 1), (1, ROWS + edge - 1, ROWS + edge)):
                at = (k, slice(row, row + 1), into)
                grid[at] = grid[at] + res_ref[xs, k : k + 1, lanes]
                grid[k, beyond : beyond + 1, into] = res_ref[xs, 5 + k : 6 + k, lanes]
        flag = even_y if side == 1 else jnp.logical_not(even_y)
        own = [pick(ya_ref, yb_ref, flag, k) for k in range(15)]
        other = [pick(sa_ref, sb_ref, flag, k) for k in range(16)]
        added, finished = meet(1, side, own, other[:15])
        beyond = 0 if side == 0 else 2 * LANES
        for k in range(5):
            if side == 0:
                extra = jnp.where(lane < edge, added[k], 0.0)
                halo = pltpu.roll(finished[k], LANES - edge, 1)
            else:
                extra = jnp.where(lane >= LANES - edge, pltpu.roll(added[k], LANES - edge, 1), 0.0)
                halo = finished[k]
            at = (k, rows, slice(LANES, 2 * LANES))
            grid[at] = grid[at] + extra
            grid[k, rows, beyond : beyond + LANES] = halo
        start = 0 if side == 0 else span - LANES
        for xs, row in ((0, ROWS - 1), (1, ROWS + edge)):
            flag_x = even if xs == 1 else jnp.logical_not(even)
            lanes = slice(start, start + LANES)
            state = [jnp.where(flag_x, ra_ref[k : k + 1, lanes], rb_ref[k : k + 1, lanes]) for k in range(11, 16)]
            corner = [other[15][2 * k + xs : 2 * k + xs + 1, :] for k in range(5)]
            if side == 1:
                corner = [pltpu.roll(v, LANES - edge, 1) for v in corner]
            extra = one_sided(state[:3], state[3], 1, 1.0 if side == 1 else -1.0, corner)
            inside = lane_row < edge if side == 0 else lane_row >= LANES - edge
            for k in range(5):
                at = (k, slice(row, row + 1), slice(LANES, 2 * LANES))
                grid[at] = grid[at] + jnp.where(inside, state[4] * extra[k], 0.0)

        lanes = pl.ds(start, LANES)
        wide = slice(LANES, 2 * LANES) if side == 0 else slice(0, LANES)
        for top in range(0, edge, 2 * ROWS):
            face_tiles = [face_ref[d, pl.ds(top, 2 * ROWS), lanes].astype(F32) for d in range(6)]
            tables = [[], [], [], []]
            for i_half in range(2):
                here = pl.ds(top + i_half * ROWS, ROWS)
                vel, speed_sq, pressure, enthalpy, reach, faces, rhs = tile_coefficients(
                    i_half, here, lanes, state_ref, face_tiles, pseudo_ref, rhs_ref
                )
                out = sweep_tile(
                    grid, ROWS + top + i_half * ROWS, LANES, edge, vel, speed_sq, enthalpy, reach, faces, rhs
                )
                for k in range(5):
                    field[side, k, here, :] = out[k]
                for k in range(4):
                    tables[k].append(pressure * out[1 + k])
            for k in range(4):
                big, small = split(jnp.concatenate(tables[k], axis=0))
                at = slice(k * edge + top, k * edge + top + 2 * ROWS)
                high[at, wide] = big
                low[at, wide] = small
        store = pltpu.make_async_copy(field.at[side], out_ref.at[:, :, lanes], sem.at[side])
        store.start()
        stores.append(store)

    x, number = chunk_of(cell_ref[...], span)
    gathered = gather(high, low, column_ref, jnp.where(number == 0, x, -1))
    gathered = [gathered_ref[k : k + 1, :] + v for k, v in enumerate(gathered)]

    group = max(capacity, LANES)
    together = group // capacity
    vertex_rows = -(-together * PARTS // 16) * 16
    chunk = lax.broadcasted_iota(jnp.int32, (1, group), 1) // capacity
    for s in range(0, slots // group):
        lanes = slice(s * group, (s + 1) * group)
        shape = [shape_ref[k : k + 1, lanes] for k in range(21)]
        terms = tet_terms(gathered[3][:, lanes], [gathered[k][:, lanes] for k in range(3)], shape)
        left, right = [], []
        for c in range(4):
            row = vertex_ref[c : c + 1, lanes] // LANES + chunk * PARTS
            match = lax.broadcasted_iota(jnp.int32, (vertex_rows, group), 0) == row
            blocks = []
            for k in range(3):
                blocks += split(jnp.where(match, terms[c][k], 0.0))
            left.append(jnp.concatenate(blocks, axis=0))
            right.append(vertex_hot_ref[c, :, lanes])
        product = lax.dot_general(
            jnp.concatenate(left, axis=1), jnp.concatenate(right, axis=1),
            (((1,), (1,)), ((), ())), preferred_element_type=F32,
        )
        for k in range(3):
            big = product[2 * k * vertex_rows : (2 * k + 1) * vertex_rows]
            small = product[(2 * k + 1) * vertex_rows : (2 * k + 2) * vertex_rows]
            total = big + small
            for q in range(together):
                owner = s * together + q
                sums[owner % 2, owner // 2, k * PARTS : (k + 1) * PARTS, :] = total[q * PARTS : (q + 1) * PARTS]
    core = lax.rem(lax.axis_index("blk"), 2)
    keep_ref[...] = sums[core]
    send_ref[...] = sums[1 - core]
    for store in stores:
        store.wait()


def fourth_kernel(keep_ref, got_ref, mine_ref, *refs):
    count = keep_ref.shape[0]
    me = lax.rem(lax.axis_index("blk") // 2, count)
    mine_ref[...] = keep_ref[me] + got_ref[me]
    for k, ref in enumerate(refs):
        partner = lax.bitwise_xor(me, k + 1)
        ref[...] = keep_ref[partner] + got_ref[partner]


def last_kernel(*refs):
    total = refs[0][...]
    for ref in refs[1:-1]:
        total = total + ref[...]
    for k in range(3):
        for part in range(PARTS):
            at = k * PARTS + part
            refs[-1][k : k + 1, part * LANES : (part + 1) * LANES] = total[at : at + 1, :]


def swap(value, axis, pairs):
    return lax.ppermute(value, axis, pairs + [(b, a) for a, b in pairs])


def neighbours(value_a, value_b, axis):
    count = lax.axis_size(axis)
    first = [(i, i + 1) for i in range(0, count - 1, 2)]
    second = [(i, i + 1) for i in range(1, count - 1, 2)]
    return swap(value_a, axis, first), swap(value_b, axis, second)


def local(
    adjoint_init, adjoint_rhs, flow_state, face_weights, pseudo_time,
    tet_coords, tet_weights, tet_cell, tet_vertex, tet_count,
):
    edge, span = pseudo_time.shape
    owners = tet_count.shape[1]
    blocks = lax.axis_size("blk")
    padded = (5, edge + 2 * ROWS, span + 2 * LANES)
    struct = jax.ShapeDtypeStruct
    packed = (16 * edge // LANES, edge, LANES)
    slots = tet_cell.shape[0]
    cell = tet_cell.reshape(1, slots)
    message = struct((16, span), F32)
    fields = (adjoint_init, adjoint_rhs, flow_state, face_weights, pseudo_time)
    xa, xb = call(
        plane_kernel,
        [message] * 2,
        [HBM] * 5,
        [VMEM] * 2,
        [pltpu.VMEM((5, 2 * ROWS, span), F32)] * 3
        + [pltpu.VMEM((6, edge, span), BF16), pltpu.VMEM((2 * ROWS, span), F32), pltpu.VMEM((2, 16, span), F32),
           pltpu.SemaphoreType.DMA((9,))],
        "plane_messages",
    )(*fields)
    ra, rb = neighbours(xa, xb, "grp")
    part, ylo, yhi, column, vertex_hot, shapes = call(
        first_kernel,
        [struct((5, edge, span), F32), struct(packed, F32), struct(packed, F32), struct((2 * LANES, slots), BF16),
         struct((4, LANES, slots), BF16), struct((24, slots), F32)],
        [VMEM] * 9 + [SMEM],
        [VMEM] * 6,
        [pltpu.VMEM(padded, F32), pltpu.VMEM((6, edge, span), F32)],
        "partial_sweep",
        flops=12_000_000,
    )(*fields, jnp.transpose(tet_coords, (1, 0, 2)), tet_weights, cell, tet_vertex, tet_count)
    res, ya, yb = call(
        second_kernel,
        [struct((2, 16, span), F32), struct(packed, F32), struct(packed, F32)],
        [VMEM] * 6,
        [VMEM] * 3,
        [pltpu.VMEM((2,) + packed, F32)],
        "streamwise_halo",
    )(xa, xb, ra, rb, ylo, yhi)
    sa, sb = neighbours(ya, yb, "blk")
    table = (4 * edge * (span // (2 * LANES) - 1), 2 * LANES)
    adjoint, gathered = call(
        middle_kernel,
        [struct((5, edge, span), F32), struct((4, slots), F32)],
        [VMEM] * 8,
        [HBM, VMEM],
        [pltpu.VMEM(padded, F32), pltpu.VMEM((5, edge, span - 2 * LANES), F32), pltpu.VMEM(table, BF16),
         pltpu.VMEM(table, BF16), pltpu.SemaphoreType.DMA],
        "middle_sweep",
        flops=12_000_000,
    )(part, *fields[1:], res, column, cell)
    half = owners // 2
    sums_shape = (half, 3 * PARTS, LANES)
    table = (4 * edge, 2 * LANES)
    adjoint, keep, send = call(
        third_kernel,
        [struct((5, edge, span), F32), struct(sums_shape, F32), struct(sums_shape, F32)],
        [HBM] + [VMEM] * 18,
        [HBM, VMEM, VMEM],
        [pltpu.VMEM((2, 5, edge + 2 * ROWS, 3 * LANES), F32), pltpu.VMEM((2, 5, edge, LANES), F32),
         pltpu.VMEM(table, BF16), pltpu.VMEM(table, BF16), pltpu.VMEM((2,) + sums_shape, F32),
         pltpu.SemaphoreType.DMA((2,))],
        "edge_sweep_and_sums",
        flops=12_000_000,
        aliases={0: 0},
    )(
        adjoint, part, *fields[1:], res, ra, rb, ya, yb, sa, sb,
        gathered, column, cell, tet_vertex, vertex_hot, shapes,
    )
    got = swap(send, "blk", [(i, i + 1) for i in range(0, blocks, 2)])
    place = lax.axis_index("blk") // 2
    while half > 4:
        half //= 2
        both = (keep + got).reshape(2, half, 3 * PARTS, LANES)
        bit = lax.rem(place // half, 2)
        keep = lax.dynamic_index_in_dim(both, bit, 0, keepdims=False)
        send = lax.dynamic_index_in_dim(both, 1 - bit, 0, keepdims=False)
        got = lax.ppermute(send, "blk", [(i, i ^ (2 * half)) for i in range(blocks)])
    one = struct((3 * PARTS, LANES), F32)
    mine, *others = call(
        fourth_kernel, [one] * half, [VMEM] * 2, [VMEM] * half, [], "core_pair_sums"
    )(keep, got)
    others = [
        lax.ppermute(v, "blk", [(i, i ^ (2 * (k + 1))) for i in range(blocks)]) for k, v in enumerate(others)
    ]
    sensitivity = call(
        last_kernel, struct((3, VERT_DEV), F32), [VMEM] * half, VMEM, [], "own_sums"
    )(mine, *others)
    return adjoint, sensitivity


def solution(mesh):
    return jax.shard_map(
        local,
        mesh=mesh,
        in_specs=(
            P(None, "grp", "blk"),
            P(None, "grp", "blk"),
            P(None, "grp", "blk"),
            P(None, "grp", "blk"),
            P("grp", "blk"),
            P(None, None, ("grp", "blk")),
            P(None, ("grp", "blk")),
            P(("grp", "blk")),
            P(None, ("grp", "blk")),
            P(("grp", "blk"), None),
        ),
        out_specs=(P(None, "grp", "blk"), P(None, ("grp", "blk"))),
        check_vma=False,
    )
```

```python
import functools
import jax
import jax.numpy as jnp
from jax import lax
from jax.experimental import pallas as pl
from jax.experimental.pallas import tpu as pltpu
from jax.sharding import PartitionSpec as P

VERT_DEV = 1536
GAMMA = 1.4
LANES = 128
ROWS = 8
PARTS = VERT_DEV // LANES
F32 = jnp.float32
BF16 = jnp.bfloat16
VMEM = pl.BlockSpec(memory_space=pltpu.VMEM)
SMEM = pl.BlockSpec(memory_space=pltpu.SMEM)
HBM = pl.BlockSpec(memory_space=pltpu.HBM)
LIMIT = 40 * 1024 * 1024


def call(kernel, outs, in_specs, out_specs, scratch, name, flops=1000, aliases={}):
    return pl.pallas_call(
        kernel,
        out_shape=outs,
        in_specs=in_specs,
        out_specs=out_specs,
        scratch_shapes=scratch,
        compiler_params=pltpu.CompilerParams(vmem_limit_bytes=LIMIT),
        cost_estimate=pl.CostEstimate(flops=flops, bytes_accessed=flops // 4, transcendentals=0),
        input_output_aliases=aliases,
        name=name,
    )


def is_even(axis):
    return lax.rem(lax.axis_index(axis), 2) == 0


def reach_of(speed_sq, enthalpy):
    sound_sq = (GAMMA - 1.0) * (enthalpy - 0.5 * speed_sq)
    return jnp.sqrt(speed_sq) + jnp.sqrt(sound_sq)


def transposed(vel, enthalpy, half_sq, axis_id, field):
    normal = vel[axis_id]
    energy = normal * field[4]
    common = vel[0] * field[1] + vel[1] * field[2] + vel[2] * field[3] + enthalpy * field[4]
    along = field[1 + axis_id] + energy
    scaled = (GAMMA - 1.0) * along
    out = [half_sq * along - normal * common]
    for j in range(3):
        entry = normal * field[1 + j] - vel[j] * scaled
        if j == axis_id:
            entry = entry + (field[0] + common)
        out.append(entry)
    out.append(scaled + energy)
    return out


def one_sided(vel, enthalpy, axis_id, sign, field):
    speed_sq = vel[0] * vel[0] + vel[1] * vel[1] + vel[2] * vel[2]
    reach = reach_of(speed_sq, enthalpy)
    turned = transposed(vel, enthalpy, 0.5 * (GAMMA - 1.0) * speed_sq, axis_id, field)
    return [sign * turned[k] + reach * field[k] for k in range(5)]


def cell_state(state):
    density, m1, m2, m3, energy = state
    inverse = 1.0 / density
    vel = [m1 * inverse, m2 * inverse, m3 * inverse]
    speed_sq = vel[0] * vel[0] + vel[1] * vel[1] + vel[2] * vel[2]
    pressure = (GAMMA - 1.0) * (energy - 0.5 * density * speed_sq)
    enthalpy = (energy + pressure) * inverse
    reach = jnp.sqrt(speed_sq) + jnp.sqrt(GAMMA * pressure * inverse)
    return vel, speed_sq, pressure, enthalpy, reach


def combine(rhs, reach, vel, speed_sq, enthalpy, faces, pairs):
    spread = None
    scaled = None
    for axis_id, (upper, lower) in enumerate(pairs):
        upper = [faces[2 * axis_id] * v for v in upper]
        lower = [faces[2 * axis_id + 1] * v for v in lower]
        both = [u + v for u, v in zip(upper, lower)]
        field = [u - v for u, v in zip(upper, lower)]
        spread = both if spread is None else [u + v for u, v in zip(spread, both)]
        normal = vel[axis_id]
        energy = normal * field[4]
        common = vel[0] * field[1] + vel[1] * field[2] + vel[2] * field[3] + enthalpy * field[4]
        along = field[1 + axis_id] + energy
        parts = [normal * common] + [normal * field[1 + j] for j in range(3)] + [energy]
        parts[1 + axis_id] = parts[1 + axis_id] + (field[0] + common)
        if scaled is None:
            scaled, total = along, parts
        else:
            scaled = scaled + along
            total = [u + v for u, v in zip(total, parts)]
    scaled = (GAMMA - 1.0) * scaled
    turned = [0.5 * speed_sq * scaled - total[0]]
    turned += [total[1 + j] - vel[j] * scaled for j in range(3)]
    turned.append(scaled + total[4])
    return [rhs[k] + turned[k] + reach * spread[k] for k in range(5)]


def inside_faces(faces, edge, shape):
    depth = lax.rem(lax.broadcasted_iota(jnp.int32, shape, 1), edge)
    faces = list(faces)
    faces[4] = jnp.where(depth == edge - 1, 0.0, faces[4])
    faces[5] = jnp.where(depth == 0, 0.0, faces[5])
    return faces


def lane_pairs(here, after, before, edge, shape):
    place = lax.broadcasted_iota(jnp.int32, shape, 1)
    first = place < edge
    last = place >= LANES - edge
    along_y = (
        [pltpu.roll(jnp.where(first, a, h), LANES - edge, 1) for h, a in zip(here, after)],
        [pltpu.roll(jnp.where(last, b, h), edge, 1) for h, b in zip(here, before)],
    )
    along_z = ([pltpu.roll(h, LANES - 1, 1) for h in here], [pltpu.roll(h, 1, 1) for h in here])
    return along_y, along_z


def sweep_tile(grid, row, lane, edge, vel, speed_sq, enthalpy, reach, faces, rhs):
    def at(drow, dlane):
        return [grid[k, pl.ds(row + drow, ROWS), pl.ds(lane + dlane, LANES)] for k in range(5)]

    shape = (ROWS, LANES)
    pairs = lane_pairs(at(0, 0), at(0, LANES), at(0, -LANES), edge, shape)
    return combine(
        rhs, reach, vel, speed_sq, enthalpy, inside_faces(faces, edge, shape), ((at(1, 0), at(-1, 0)),) + pairs
    )


def coefficients(state, faces, pseudo, rhs):
    vel, speed_sq, pressure, enthalpy, reach = cell_state(state)
    area = faces[0]
    for f in faces[1:]:
        area = area + f
    inverse = 1.0 / (pseudo + 0.5 * reach * area)
    half = 0.5 * inverse
    return vel, speed_sq, pressure, enthalpy, reach, [half * f for f in faces], [inverse * v for v in rhs]


def tile_coefficients(i_half, rows, lanes, state_ref, face_tiles, pseudo_ref, rhs_ref):
    return coefficients(
        [state_ref[k, rows, lanes] for k in range(5)],
        [f[i_half * ROWS : (i_half + 1) * ROWS] for f in face_tiles],
        pseudo_ref[rows, lanes],
        [rhs_ref[k, rows, lanes] for k in range(5)],
    )


def clear_pads(grid, edge, span):
    high = grid.shape[1]
    wide = grid.shape[2]
    for k in range(5):
        grid[k, 0:ROWS, :] = jnp.zeros((ROWS, wide), F32)
        grid[k, ROWS + edge : high, :] = jnp.zeros((high - ROWS - edge, wide), F32)
        grid[k, ROWS : ROWS + edge, 0:LANES] = jnp.zeros((edge, LANES), F32)
        grid[k, ROWS : ROWS + edge, LANES + span : wide] = jnp.zeros((edge, LANES), F32)


def for_each_tile(edge, first, last, body):
    for top in range(0, edge, 2 * ROWS):

        def step(j, carry, top=top):
            body(top, pl.multiple_of(j * LANES, LANES))
            return carry

        lax.fori_loop(first, last, step, 0, unroll=True)


def plane_kernel(
    adjoint_hbm, rhs_hbm, state_hbm, face_hbm, pseudo_hbm, coord_hbm, weight_hbm, cell_hbm, vertex_hbm,
    xa_ref, xb_ref, adjoint_ref, rhs_ref, state_ref, face_ref, pseudo_ref, coord_ref, weight_ref, cell_ref,
    vertex_ref,
    xsides, sem,
):
    edge, span = pseudo_hbm.shape
    early, late = [], []

    def move(into, source, target):
        into.append(pltpu.make_async_copy(source, target, sem.at[len(early) + len(late)]))
        into[-1].start()

    fields = (
        (state_hbm, state_ref), (adjoint_hbm, adjoint_ref), (rhs_hbm, rhs_ref), (pseudo_hbm, pseudo_ref)
    )

    def rows_of(ref, first, count):
        return ref.at[(slice(None),) * (len(ref.shape) - 2) + (pl.ds(first, count),)]

    move(early, face_hbm, face_ref)
    for source, target in fields:
        for first in (0, edge - ROWS):
            move(early, rows_of(source, first, ROWS), rows_of(target, first, ROWS))
    for source, target in fields:
        move(late, rows_of(source, ROWS, edge - 2 * ROWS), rows_of(target, ROWS, edge - 2 * ROWS))
    for source, target in (
        (coord_hbm, coord_ref), (weight_hbm, weight_ref), (cell_hbm, cell_ref), (vertex_hbm, vertex_ref)
    ):
        move(late, source, target)
    for copy in early:
        copy.wait()
    even = is_even("grp")
    shape = (2, LANES)
    upper_row = lax.broadcasted_iota(jnp.int32, shape, 0) == 1
    sub = lax.broadcasted_iota(jnp.int32, (ROWS, LANES), 0)
    place = lax.broadcasted_iota(jnp.int32, shape, 1)
    tiles = span // LANES
    zero = jnp.zeros(shape, F32)

    def planes(ref, k, j, inner=0):
        at = (k,) if k is not None else ()
        lanes = slice(j * LANES, (j + 1) * LANES)
        last = edge - 2 - inner
        return jnp.where(upper_row, ref[at + (slice(last, last + 2), lanes)], ref[at + (slice(inner, inner + 2), lanes)])

    for j in range(tiles):
        lanes = pl.ds(j * LANES, LANES)
        faces = []
        for d in range(6):
            low = face_ref[d, pl.ds(0, 2 * ROWS), lanes].astype(F32)[:ROWS]
            high = face_ref[d, pl.ds(edge - 2 * ROWS, 2 * ROWS), lanes].astype(F32)[ROWS:]
            faces.append(jnp.where(sub == 0, low, pltpu.roll(high, 2, 0))[:2])
        vel, speed_sq, pressure, enthalpy, reach, faces, rhs = coefficients(
            [planes(state_ref, k, j) for k in range(5)],
            faces,
            planes(pseudo_ref, None, j),
            [planes(rhs_ref, k, j) for k in range(5)],
        )
        here = [planes(adjoint_ref, k, j) for k in range(5)]
        after = [planes(adjoint_ref, k, j + 1) if j + 1 < tiles else zero for k in range(5)]
        before = [planes(adjoint_ref, k, j - 1) if j > 0 else zero for k in range(5)]
        inner = [planes(adjoint_ref, k, j, 1) for k in range(5)]
        along_x = ([jnp.where(upper_row, 0.0, v) for v in inner], [jnp.where(upper_row, v, 0.0) for v in inner])
        pairs = lane_pairs(here, after, before, edge, shape)
        out = combine(
            rhs, reach, vel, speed_sq, enthalpy, inside_faces(faces, edge, shape), (along_x,) + pairs
        )
        message = out + here + [jnp.where(upper_row, faces[0], faces[1])] + vel + [enthalpy]
        message.append(jnp.where(place < edge, faces[3], faces[2]) if j == 0 else faces[2])
        for side in (0, 1):
            slot = jnp.where(even, 1 - side, side)
            for k, value in enumerate(message):
                xsides[slot, k : k + 1, lanes] = value[side : side + 1]
    xa_ref[...] = xsides[0]
    xb_ref[...] = xsides[1]
    for copy in late:
        copy.wait()


def first_kernel(
    adjoint_ref, rhs_ref, state_ref, face_ref, pseudo_ref, coord_ref, weight_ref, cell_ref, vertex_ref, count_ref,
    part_ref, ylo_ref, yhi_ref, column_ref, vertex_hot_ref, shape_ref,
    grid, coef,
):
    edge, span = pseudo_ref.shape
    clear_pads(grid, edge, span)
    for k in range(5):
        grid[k, ROWS : ROWS + edge, LANES : LANES + span] = adjoint_ref[k]

    def body(top, offset):
        lanes = pl.ds(offset, LANES)
        face_tiles = [face_ref[d, pl.ds(top, 2 * ROWS), lanes].astype(F32) for d in range(6)]
        for i_half in range(2):
            rows = pl.ds(top + i_half * ROWS, ROWS)
            vel, speed_sq, pressure, enthalpy, reach, faces, rhs = tile_coefficients(
                i_half, rows, lanes, state_ref, face_tiles, pseudo_ref, rhs_ref
            )
            out = sweep_tile(
                grid, ROWS + top + i_half * ROWS, pl.multiple_of(LANES + offset, LANES), edge,
                vel, speed_sq, enthalpy, reach, faces, rhs,
            )
            for k in range(5):
                part_ref[k, rows, lanes] = out[k]
            for k, value in enumerate(vel + [enthalpy] + faces[2:4]):
                coef[k, rows, lanes] = value

    for_each_tile(edge, 0, span // LANES, body)

    lane = lax.broadcasted_iota(jnp.int32, (edge, LANES), 1)
    quarter = lane // edge
    for side, base, ref in ((0, 0, ylo_ref), (1, span - LANES, yhi_ref)):
        lanes = slice(base, base + LANES)
        fields = [part_ref[k, :, lanes] for k in range(5)]
        fields += [grid[k, ROWS : ROWS + edge, LANES + base : LANES + base + LANES] for k in range(5)]
        fields += [coef[4 + 1 - side, :, lanes]]
        fields += [coef[k, :, lanes] for k in range(4)]
        start = 0 if side == 0 else LANES - edge
        per = LANES // edge
        for g in range(4):
            packed = None
            for q in range(per):
                k = g * per + q
                if k >= len(fields):
                    value = jnp.zeros((edge, LANES), F32)
                else:
                    shift = (q * edge - start) % LANES
                    value = pltpu.roll(fields[k], shift, 1) if shift else fields[k]
                packed = value if packed is None else jnp.where(quarter == q, value, packed)
            ref[g] = packed

    owners = count_ref.shape[1]
    slots = weight_ref.shape[1]
    capacity = slots // owners
    width = 2 * LANES
    step = min(slots, 512)
    for s in range(0, slots, step):
        part = slice(s, s + step)
        column = lax.rem(cell_ref[:, part] + LANES, width)
        column_ref[:, part] = hot((width, step), column)
        for c in range(4):
            vertex_hot_ref[c, :, part] = hot((LANES, step), lax.rem(vertex_ref[c : c + 1, part], LANES))

    group = max(capacity, LANES)
    together = group // capacity
    lane_group = lax.broadcasted_iota(jnp.int32, (1, group), 1)
    chunk = lane_group // capacity
    within = lax.rem(lane_group, capacity)
    for s in range(0, slots // group):
        lanes = slice(s * group, (s + 1) * group)
        count = count_ref[0, s * together]
        for q in range(1, together):
            count = jnp.where(chunk == q, count_ref[0, s * together + q], count)
        live = jnp.where(within < count, 1.0, 0.0)
        weights = [weight_ref[c : c + 1, lanes] * live for c in range(4)]
        corner = [[coord_ref[k, c : c + 1, lanes] for k in range(3)] for c in range(4)]
        for k, value in enumerate(tet_shapes(corner, weights)):
            shape_ref[k : k + 1, lanes] = value


def meet(axis_id, side, own, other):
    sign = 1.0 if side == 1 else -1.0
    mine = one_sided(own[11:14], own[14], axis_id, sign, other[5:10])
    theirs = one_sided(other[11:14], other[14], axis_id, -sign, own[5:10])
    added = [own[10] * v for v in mine]
    finished = [other[k] + other[10] * theirs[k] for k in range(5)]
    return added, finished


def second_kernel(xa_ref, xb_ref, ra_ref, rb_ref, ylo_ref, yhi_ref, res_ref, ya_ref, yb_ref, ysides):
    span = xa_ref.shape[1]
    edge = ylo_ref.shape[1]
    per = LANES // edge
    even = is_even("grp")
    even_y = is_even("blk")
    ysides[0] = ylo_ref[...]
    ysides[1] = yhi_ref[...]
    lane = lax.broadcasted_iota(jnp.int32, (1, LANES), 1)
    quarter = lane // edge

    def pick(a_ref, b_ref, flag):
        return [jnp.where(flag, a_ref[k : k + 1, :], b_ref[k : k + 1, :]) for k in range(15)]

    for side in (0, 1):
        flag = even if side == 1 else jnp.logical_not(even)
        own = pick(xa_ref, xb_ref, flag)
        other = pick(ra_ref, rb_ref, flag)
        added, finished = meet(0, side, own, other)
        row = 0 if side == 0 else edge - 1
        for k in range(5):
            res_ref[side, k : k + 1, :] = added[k]
            res_ref[side, 5 + k : 6 + k, :] = finished[k]
        for ys, base, start in ((0, 0, 0), (1, span - LANES, LANES - edge)):
            for k in range(5):
                g, q = divmod(k, per)
                shift = (q * edge - start) % LANES
                piece = added[k][:, base : base + LANES]
                piece = pltpu.roll(piece, shift, 1) if shift else piece
                old = ysides[ys, g, row : row + 1, :]
                ysides[ys, g, row : row + 1, :] = old + jnp.where(quarter == q, piece, 0.0)
                g, q = divmod(15, per)
                shift = (q * edge - start) % LANES
                piece = other[5 + k][:, base : base + LANES]
                piece = pltpu.roll(piece, shift, 1) if shift else piece
                at = 2 * k + side
                old = ysides[ys, g, at : at + 1, :]
                ysides[ys, g, at : at + 1, :] = jnp.where(quarter == q, piece, old)
    ya_ref[...] = ysides[jnp.where(even_y, 1, 0)]
    yb_ref[...] = ysides[jnp.where(even_y, 0, 1)]


def cross(left, right):
    return [
        left[1] * right[2] - left[2] * right[1],
        left[2] * right[0] - left[0] * right[2],
        left[0] * right[1] - left[1] * right[0],
    ]


def minus(left, right):
    return [u - v for u, v in zip(left, right)]


def tet_shapes(corner, weights):
    edge_one = minus(corner[1], corner[0])
    edge_two = minus(corner[2], corner[0])
    edge_three = minus(corner[3], corner[0])
    g1 = cross(edge_two, edge_three)
    g2 = cross(edge_three, edge_one)
    g3 = cross(edge_one, edge_two)
    g0 = [-(u + v + w) for u, v, w in zip(g1, g2, g3)]
    sixth = [w * (1.0 / 6.0) for w in weights]
    half = [w * 0.5 for w in weights]
    out = []
    for c, g in enumerate((g0, g1, g2, g3)):
        out += [sixth[c] * v for v in g]
    out += [half[1] * v for v in minus(corner[2], corner[3])]
    out += [half[2] * v for v in minus(corner[3], corner[1])]
    out += [half[3] * v for v in minus(corner[1], corner[2])]
    return out


def tet_terms(volume, face, shape):
    terms = []
    for c in range(4):
        term = [volume * shape[3 * c + k] for k in range(3)]
        if c:
            turned = cross(shape[9 + 3 * c : 12 + 3 * c], face)
            term = [u + v for u, v in zip(term, turned)]
        terms.append(term)
    return terms


def split(value):
    high = value.astype(BF16)
    return high, (value - high.astype(F32)).astype(BF16)


def hot(shape, index):
    rows = lax.broadcasted_iota(jnp.int16, shape, 0)
    return jnp.where(rows == index.astype(jnp.int16), jnp.ones((), BF16), jnp.zeros((), BF16))


def gather(high, low, column_ref, row):
    table_rows = high.shape[0] // 4
    slots = column_ref.shape[1]
    step = min(slots, 512)
    gathered = [[], [], [], []]
    for s in range(0, slots, step):
        column = column_ref[:, s : s + step]
        product = jnp.dot(high[...], column, preferred_element_type=F32)
        product = product + jnp.dot(low[...], column, preferred_element_type=F32)
        here = lax.broadcasted_iota(jnp.int32, (table_rows, step), 0) == row[:, s : s + step]
        for k in range(4):
            piece = product[k * table_rows : (k + 1) * table_rows]
            gathered[k].append(jnp.sum(jnp.where(here, piece, 0.0), axis=0, keepdims=True))
    return [jnp.concatenate(v, axis=1) for v in gathered]


def chunk_of(cell, span):
    yz = lax.rem(cell, span) + LANES
    return cell // span, lax.rem(yz // (2 * LANES), span // (2 * LANES))


def middle_kernel(
    part_ref, rhs_ref, state_ref, face_ref, pseudo_ref, res_ref, column_ref, cell_ref,
    out_ref, gathered_ref,
    grid, field, high, low, sem,
):
    edge, span = pseudo_ref.shape
    tiles = span // LANES
    for k in range(5):
        grid[k, ROWS : ROWS + edge, LANES : LANES + span] = part_ref[k]
    for k in range(5):
        for side, row, beyond in ((0, ROWS, ROWS - 1), (1, ROWS + edge - 1, ROWS + edge)):
            at = (k, slice(row, row + 1), slice(LANES, LANES + span))
            grid[at] = grid[at] + res_ref[side, k : k + 1, :]
            grid[k, beyond : beyond + 1, LANES : LANES + span] = res_ref[side, 5 + k : 6 + k, :]

    def body(top, offset):
        lanes = pl.ds(offset, LANES)
        face_tiles = [face_ref[d, pl.ds(top, 2 * ROWS), lanes].astype(F32) for d in range(6)]
        tables = [[], [], [], []]
        for i_half in range(2):
            rows = pl.ds(top + i_half * ROWS, ROWS)
            vel, speed_sq, pressure, enthalpy, reach, faces, rhs = tile_coefficients(
                i_half, rows, lanes, state_ref, face_tiles, pseudo_ref, rhs_ref
            )
            out = sweep_tile(
                grid, ROWS + top + i_half * ROWS, pl.multiple_of(LANES + offset, LANES), edge,
                vel, speed_sq, enthalpy, reach, faces, rhs,
            )
            for k in range(5):
                field[k, rows, pl.ds(pl.multiple_of(offset - LANES, LANES), LANES)] = out[k]
            for k in range(4):
                tables[k].append(pressure * out[1 + k])
        chunk = (offset - LANES) // (2 * LANES)
        wide = pl.ds(pl.multiple_of(lax.rem(offset - LANES, 2 * LANES), LANES), LANES)
        for k in range(4):
            big, small = split(jnp.concatenate(tables[k], axis=0))
            at = pl.ds(pl.multiple_of(k * (high.shape[0] // 4) + chunk * edge + top, 2 * ROWS), 2 * ROWS)
            high[at, wide] = big
            low[at, wide] = small

    for_each_tile(edge, 1, tiles - 1, body)
    store = pltpu.make_async_copy(field, out_ref.at[:, :, pl.ds(LANES, span - 2 * LANES)], sem)
    store.start()
    x, chunk = chunk_of(cell_ref[...], span)
    row = jnp.where(chunk > 0, (chunk - 1) * edge + x, -1)
    for k, value in enumerate(gather(high, low, column_ref, row)):
        gathered_ref[k : k + 1, :] = value
    store.wait()


def third_kernel(
    adjoint_ref, part_ref, rhs_ref, state_ref, face_ref, pseudo_ref, res_ref, ra_ref, rb_ref,
    ya_ref, yb_ref, sa_ref, sb_ref, gathered_ref, column_ref, cell_ref, vertex_ref, vertex_hot_ref, shape_ref,
    out_ref, keep_ref, send_ref,
    grids, field, high, low, sums, sem,
):
    edge, span = pseudo_ref.shape
    per = LANES // edge
    owners = 2 * keep_ref.shape[0]
    slots = cell_ref.shape[1]
    capacity = slots // owners
    even = is_even("grp")
    even_y = is_even("blk")
    lane = lax.broadcasted_iota(jnp.int32, (edge, LANES), 1)
    lane_row = lax.broadcasted_iota(jnp.int32, (1, LANES), 1)
    rows = slice(ROWS, ROWS + edge)
    stores = []

    def pick(a_ref, b_ref, flag, k):
        g, q = divmod(k, per)
        value = jnp.where(flag, a_ref[g], b_ref[g])
        return pltpu.roll(value, LANES - q * edge, 1) if q else value

    for side in (0, 1):
        grid = grids.at[side]
        start = 0 if side == 0 else span - 2 * LANES
        lanes = slice(start, start + 2 * LANES)
        base = LANES if side == 0 else 0
        into = slice(base, base + 2 * LANES)
        for k in range(5):
            grid[k, rows, into] = part_ref[k, :, lanes]
            for xs, row, beyond in ((0, ROWS, ROWS - 1), (1, ROWS + edge - 1, ROWS + edge)):
                at = (k, slice(row, row + 1), into)
                grid[at] = grid[at] + res_ref[xs, k : k + 1, lanes]
                grid[k, beyond : beyond + 1, into] = res_ref[xs, 5 + k : 6 + k, lanes]
        flag = even_y if side == 1 else jnp.logical_not(even_y)
        own = [pick(ya_ref, yb_ref, flag, k) for k in range(15)]
        other = [pick(sa_ref, sb_ref, flag, k) for k in range(16)]
        added, finished = meet(1, side, own, other[:15])
        beyond = 0 if side == 0 else 2 * LANES
        for k in range(5):
            if side == 0:
                extra = jnp.where(lane < edge, added[k], 0.0)
                halo = pltpu.roll(finished[k], LANES - edge, 1)
            else:
                extra = jnp.where(lane >= LANES - edge, pltpu.roll(added[k], LANES - edge, 1), 0.0)
                halo = finished[k]
            at = (k, rows, slice(LANES, 2 * LANES))
            grid[at] = grid[at] + extra
            grid[k, rows, beyond : beyond + LANES] = halo
        start = 0 if side == 0 else span - LANES
        for xs, row in ((0, ROWS - 1), (1, ROWS + edge)):
            flag_x = even if xs == 1 else jnp.logical_not(even)
            lanes = slice(start, start + LANES)
            state = [jnp.where(flag_x, ra_ref[k : k + 1, lanes], rb_ref[k : k + 1, lanes]) for k in range(11, 16)]
            corner = [other[15][2 * k + xs : 2 * k + xs + 1, :] for k in range(5)]
            if side == 1:
                corner = [pltpu.roll(v, LANES - edge, 1) for v in corner]
            extra = one_sided(state[:3], state[3], 1, 1.0 if side == 1 else -1.0, corner)
            inside = lane_row < edge if side == 0 else lane_row >= LANES - edge
            for k in range(5):
                at = (k, slice(row, row + 1), slice(LANES, 2 * LANES))
                grid[at] = grid[at] + jnp.where(inside, state[4] * extra[k], 0.0)

        lanes = pl.ds(start, LANES)
        wide = slice(LANES, 2 * LANES) if side == 0 else slice(0, LANES)
        for top in range(0, edge, 2 * ROWS):
            face_tiles = [face_ref[d, pl.ds(top, 2 * ROWS), lanes].astype(F32) for d in range(6)]
            tables = [[], [], [], []]
            for i_half in range(2):
                here = pl.ds(top + i_half * ROWS, ROWS)
                vel, speed_sq, pressure, enthalpy, reach, faces, rhs = tile_coefficients(
                    i_half, here, lanes, state_ref, face_tiles, pseudo_ref, rhs_ref
                )
                out = sweep_tile(
                    grid, ROWS + top + i_half * ROWS, LANES, edge, vel, speed_sq, enthalpy, reach, faces, rhs
                )
                for k in range(5):
                    field[side, k, here, :] = out[k]
                for k in range(4):
                    tables[k].append(pressure * out[1 + k])
            for k in range(4):
                big, small = split(jnp.concatenate(tables[k], axis=0))
                at = slice(k * edge + top, k * edge + top + 2 * ROWS)
                high[at, wide] = big
                low[at, wide] = small
        store = pltpu.make_async_copy(field.at[side], out_ref.at[:, :, lanes], sem.at[side])
        store.start()
        stores.append(store)

    x, number = chunk_of(cell_ref[...], span)
    gathered = gather(high, low, column_ref, jnp.where(number == 0, x, -1))
    gathered = [gathered_ref[k : k + 1, :] + v for k, v in enumerate(gathered)]

    group = max(capacity, LANES)
    together = group // capacity
    vertex_rows = -(-together * PARTS // 16) * 16
    chunk = lax.broadcasted_iota(jnp.int32, (1, group), 1) // capacity
    for s in range(0, slots // group):
        lanes = slice(s * group, (s + 1) * group)
        shape = [shape_ref[k : k + 1, lanes] for k in range(21)]
        terms = tet_terms(gathered[3][:, lanes], [gathered[k][:, lanes] for k in range(3)], shape)
        left, right = [], []
        for c in range(4):
            row = vertex_ref[c : c + 1, lanes] // LANES + chunk * PARTS
            match = lax.broadcasted_iota(jnp.int16, (vertex_rows, group), 0) == row.astype(jnp.int16)
            blocks = []
            for k in range(3):
                blocks += [jnp.where(match, v, jnp.zeros((), BF16)) for v in split(terms[c][k])]
            left.append(jnp.concatenate(blocks, axis=0))
            right.append(vertex_hot_ref[c, :, lanes])
        product = lax.dot_general(
            jnp.concatenate(left, axis=1), jnp.concatenate(right, axis=1),
            (((1,), (1,)), ((), ())), preferred_element_type=F32,
        )
        for k in range(3):
            big = product[2 * k * vertex_rows : (2 * k + 1) * vertex_rows]
            small = product[(2 * k + 1) * vertex_rows : (2 * k + 2) * vertex_rows]
            total = big + small
            for q in range(together):
                owner = s * together + q
                sums[owner % 2, owner // 2, k * PARTS : (k + 1) * PARTS, :] = total[q * PARTS : (q + 1) * PARTS]
    core = lax.rem(lax.axis_index("blk"), 2)
    keep_ref[...] = sums[core]
    send_ref[...] = sums[1 - core]
    for store in stores:
        store.wait()


def fourth_kernel(keep_ref, got_ref, mine_ref, *refs):
    count = keep_ref.shape[0]
    me = lax.rem(lax.axis_index("blk") // 2, count)
    mine_ref[...] = keep_ref[me] + got_ref[me]
    for k, ref in enumerate(refs):
        partner = lax.bitwise_xor(me, k + 1)
        ref[...] = keep_ref[partner] + got_ref[partner]


def last_kernel(*refs):
    total = refs[0][...]
    for ref in refs[1:-1]:
        total = total + ref[...]
    for k in range(3):
        for part in range(PARTS):
            at = k * PARTS + part
            refs[-1][k : k + 1, part * LANES : (part + 1) * LANES] = total[at : at + 1, :]


def swap(value, axis, pairs):
    return lax.ppermute(value, axis, pairs + [(b, a) for a, b in pairs])


def neighbours(value_a, value_b, axis):
    count = lax.axis_size(axis)
    first = [(i, i + 1) for i in range(0, count - 1, 2)]
    second = [(i, i + 1) for i in range(1, count - 1, 2)]
    return swap(value_a, axis, first), swap(value_b, axis, second)


def local(
    adjoint_init, adjoint_rhs, flow_state, face_weights, pseudo_time,
    tet_coords, tet_weights, tet_cell, tet_vertex, tet_count,
):
    edge, span = pseudo_time.shape
    owners = tet_count.shape[1]
    blocks = lax.axis_size("blk")
    padded = (5, edge + 2 * ROWS, span + 2 * LANES)
    struct = jax.ShapeDtypeStruct
    packed = (16 * edge // LANES, edge, LANES)
    slots = tet_cell.shape[0]
    cell = tet_cell.reshape(1, slots)
    message = struct((16, span), F32)
    fields = (adjoint_init, adjoint_rhs, flow_state, face_weights, pseudo_time)
    arrays = (*fields, jnp.transpose(tet_coords, (1, 0, 2)), tet_weights, cell, tet_vertex)
    xa, xb, *arrays = call(
        plane_kernel,
        [message] * 2 + [struct(v.shape, v.dtype) for v in arrays],
        [HBM] * 9,
        [VMEM] * 11,
        [pltpu.VMEM((2, 16, span), F32), pltpu.SemaphoreType.DMA((17,))],
        "plane_messages",
    )(*(pltpu.with_memory_space_constraint(v, pltpu.HBM) for v in arrays))
    fields, (coords, weights, cell, vertex) = arrays[:5], arrays[5:]
    ra, rb = neighbours(xa, xb, "grp")
    part, ylo, yhi, column, vertex_hot, shapes = call(
        first_kernel,
        [struct((5, edge, span), F32), struct(packed, F32), struct(packed, F32), struct((2 * LANES, slots), BF16),
         struct((4, LANES, slots), BF16), struct((24, slots), F32)],
        [VMEM] * 9 + [SMEM],
        [VMEM] * 6,
        [pltpu.VMEM(padded, F32), pltpu.VMEM((6, edge, span), F32)],
        "partial_sweep",
        flops=12_000_000,
    )(*fields, coords, weights, cell, vertex, tet_count)
    res, ya, yb = call(
        second_kernel,
        [struct((2, 16, span), F32), struct(packed, F32), struct(packed, F32)],
        [VMEM] * 6,
        [VMEM] * 3,
        [pltpu.VMEM((2,) + packed, F32)],
        "streamwise_halo",
    )(xa, xb, ra, rb, ylo, yhi)
    sa, sb = neighbours(ya, yb, "blk")
    table = (4 * edge * (span // (2 * LANES) - 1), 2 * LANES)
    adjoint, gathered = call(
        middle_kernel,
        [struct((5, edge, span), F32), struct((4, slots), F32)],
        [VMEM] * 8,
        [HBM, VMEM],
        [pltpu.VMEM(padded, F32), pltpu.VMEM((5, edge, span - 2 * LANES), F32), pltpu.VMEM(table, BF16),
         pltpu.VMEM(table, BF16), pltpu.SemaphoreType.DMA],
        "middle_sweep",
        flops=12_000_000,
    )(part, *fields[1:], res, column, cell)
    half = owners // 2
    sums_shape = (half, 3 * PARTS, LANES)
    table = (4 * edge, 2 * LANES)
    adjoint, keep, send = call(
        third_kernel,
        [struct((5, edge, span), F32), struct(sums_shape, F32), struct(sums_shape, F32)],
        [HBM] + [VMEM] * 18,
        [HBM, VMEM, VMEM],
        [pltpu.VMEM((2, 5, edge + 2 * ROWS, 3 * LANES), F32), pltpu.VMEM((2, 5, edge, LANES), F32),
         pltpu.VMEM(table, BF16), pltpu.VMEM(table, BF16), pltpu.VMEM((2,) + sums_shape, F32),
         pltpu.SemaphoreType.DMA((2,))],
        "edge_sweep_and_sums",
        flops=12_000_000,
        aliases={0: 0},
    )(
        adjoint, part, *fields[1:], res, ra, rb, ya, yb, sa, sb,
        gathered, column, cell, vertex, vertex_hot, shapes,
    )
    got = swap(send, "blk", [(i, i + 1) for i in range(0, blocks, 2)])
    place = lax.axis_index("blk") // 2
    while half > 4:
        half //= 2
        both = (keep + got).reshape(2, half, 3 * PARTS, LANES)
        bit = lax.rem(place // half, 2)
        keep = lax.dynamic_index_in_dim(both, bit, 0, keepdims=False)
        send = lax.dynamic_index_in_dim(both, 1 - bit, 0, keepdims=False)
        got = lax.ppermute(send, "blk", [(i, i ^ (2 * half)) for i in range(blocks)])
    one = struct((3 * PARTS, LANES), F32)
    mine, *others = call(
        fourth_kernel, [one] * half, [VMEM] * 2, [VMEM] * half, [], "core_pair_sums"
    )(keep, got)
    others = [
        lax.ppermute(v, "blk", [(i, i ^ (2 * (k + 1))) for i in range(blocks)]) for k, v in enumerate(others)
    ]
    sensitivity = call(
        last_kernel, struct((3, VERT_DEV), F32), [VMEM] * half, VMEM, [], "own_sums"
    )(mine, *others)
    return adjoint, sensitivity


def solution(mesh):
    return jax.shard_map(
        local,
        mesh=mesh,
        in_specs=(
            P(None, "grp", "blk"),
            P(None, "grp", "blk"),
            P(None, "grp", "blk"),
            P(None, "grp", "blk"),
            P("grp", "blk"),
            P(None, None, ("grp", "blk")),
            P(None, ("grp", "blk")),
            P(("grp", "blk")),
            P(None, ("grp", "blk")),
            P(("grp", "blk"), None),
        ),
        out_specs=(P(None, "grp", "blk"), P(None, ("grp", "blk"))),
        check_vma=False,
    )
```

```python
import functools
import jax
import jax.numpy as jnp
from jax import lax
from jax.experimental import pallas as pl
from jax.experimental.pallas import tpu as pltpu
from jax.sharding import PartitionSpec as P

VERT_DEV = 1536
GAMMA = 1.4
LANES = 128
ROWS = 8
PARTS = VERT_DEV // LANES
F32 = jnp.float32
BF16 = jnp.bfloat16
VMEM = pl.BlockSpec(memory_space=pltpu.VMEM)
SMEM = pl.BlockSpec(memory_space=pltpu.SMEM)
HBM = pl.BlockSpec(memory_space=pltpu.HBM)
LIMIT = 40 * 1024 * 1024


def call(kernel, outs, in_specs, out_specs, scratch, name, flops=1000, aliases={}):
    return pl.pallas_call(
        kernel,
        out_shape=outs,
        in_specs=in_specs,
        out_specs=out_specs,
        scratch_shapes=scratch,
        compiler_params=pltpu.CompilerParams(vmem_limit_bytes=LIMIT),
        cost_estimate=pl.CostEstimate(flops=flops, bytes_accessed=flops // 4, transcendentals=0),
        input_output_aliases=aliases,
        name=name,
    )


def is_even(axis):
    return lax.rem(lax.axis_index(axis), 2) == 0


def reach_of(speed_sq, enthalpy):
    sound_sq = (GAMMA - 1.0) * (enthalpy - 0.5 * speed_sq)
    return jnp.sqrt(speed_sq) + jnp.sqrt(sound_sq)


def transposed(vel, enthalpy, half_sq, axis_id, field):
    normal = vel[axis_id]
    energy = normal * field[4]
    common = vel[0] * field[1] + vel[1] * field[2] + vel[2] * field[3] + enthalpy * field[4]
    along = field[1 + axis_id] + energy
    scaled = (GAMMA - 1.0) * along
    out = [half_sq * along - normal * common]
    for j in range(3):
        entry = normal * field[1 + j] - vel[j] * scaled
        if j == axis_id:
            entry = entry + (field[0] + common)
        out.append(entry)
    out.append(scaled + energy)
    return out


def one_sided(vel, enthalpy, axis_id, sign, field):
    speed_sq = vel[0] * vel[0] + vel[1] * vel[1] + vel[2] * vel[2]
    reach = reach_of(speed_sq, enthalpy)
    turned = transposed(vel, enthalpy, 0.5 * (GAMMA - 1.0) * speed_sq, axis_id, field)
    return [sign * turned[k] + reach * field[k] for k in range(5)]


def cell_state(state):
    density, m1, m2, m3, energy = state
    inverse = 1.0 / density
    vel = [m1 * inverse, m2 * inverse, m3 * inverse]
    speed_sq = vel[0] * vel[0] + vel[1] * vel[1] + vel[2] * vel[2]
    pressure = (GAMMA - 1.0) * (energy - 0.5 * density * speed_sq)
    enthalpy = (energy + pressure) * inverse
    reach = jnp.sqrt(speed_sq) + jnp.sqrt(GAMMA * pressure * inverse)
    return vel, speed_sq, pressure, enthalpy, reach


def combine(rhs, reach, vel, speed_sq, enthalpy, faces, pairs):
    spread = None
    scaled = None
    for axis_id, (upper, lower) in enumerate(pairs):
        upper = [faces[2 * axis_id] * v for v in upper]
        lower = [faces[2 * axis_id + 1] * v for v in lower]
        both = [u + v for u, v in zip(upper, lower)]
        field = [u - v for u, v in zip(upper, lower)]
        spread = both if spread is None else [u + v for u, v in zip(spread, both)]
        normal = vel[axis_id]
        energy = normal * field[4]
        common = vel[0] * field[1] + vel[1] * field[2] + vel[2] * field[3] + enthalpy * field[4]
        along = field[1 + axis_id] + energy
        parts = [normal * common] + [normal * field[1 + j] for j in range(3)] + [energy]
        parts[1 + axis_id] = parts[1 + axis_id] + (field[0] + common)
        if scaled is None:
            scaled, total = along, parts
        else:
            scaled = scaled + along
            total = [u + v for u, v in zip(total, parts)]
    scaled = (GAMMA - 1.0) * scaled
    turned = [0.5 * speed_sq * scaled - total[0]]
    turned += [total[1 + j] - vel[j] * scaled for j in range(3)]
    turned.append(scaled + total[4])
    return [rhs[k] + turned[k] + reach * spread[k] for k in range(5)]


def inside_faces(faces, edge, shape):
    depth = lax.rem(lax.broadcasted_iota(jnp.int32, shape, 1), edge)
    faces = list(faces)
    faces[4] = jnp.where(depth == edge - 1, 0.0, faces[4])
    faces[5] = jnp.where(depth == 0, 0.0, faces[5])
    return faces


def lane_pairs(here, after, before, edge, shape):
    place = lax.broadcasted_iota(jnp.int32, shape, 1)
    first = place < edge
    last = place >= LANES - edge
    along_y = (
        [pltpu.roll(jnp.where(first, a, h), LANES - edge, 1) for h, a in zip(here, after)],
        [pltpu.roll(jnp.where(last, b, h), edge, 1) for h, b in zip(here, before)],
    )
    along_z = ([pltpu.roll(h, LANES - 1, 1) for h in here], [pltpu.roll(h, 1, 1) for h in here])
    return along_y, along_z


def sweep_tile(grid, row, lane, edge, vel, speed_sq, enthalpy, reach, faces, rhs):
    def at(drow, dlane):
        return [grid[k, pl.ds(row + drow, ROWS), pl.ds(lane + dlane, LANES)] for k in range(5)]

    shape = (ROWS, LANES)
    pairs = lane_pairs(at(0, 0), at(0, LANES), at(0, -LANES), edge, shape)
    return combine(
        rhs, reach, vel, speed_sq, enthalpy, inside_faces(faces, edge, shape), ((at(1, 0), at(-1, 0)),) + pairs
    )


def coefficients(state, faces, pseudo, rhs):
    vel, speed_sq, pressure, enthalpy, reach = cell_state(state)
    area = faces[0]
    for f in faces[1:]:
        area = area + f
    inverse = 1.0 / (pseudo + 0.5 * reach * area)
    half = 0.5 * inverse
    return vel, speed_sq, pressure, enthalpy, reach, [half * f for f in faces], [inverse * v for v in rhs]


def tile_coefficients(i_half, rows, lanes, state_ref, face_tiles, pseudo_ref, rhs_ref):
    return coefficients(
        [state_ref[k, rows, lanes] for k in range(5)],
        [f[i_half * ROWS : (i_half + 1) * ROWS] for f in face_tiles],
        pseudo_ref[rows, lanes],
        [rhs_ref[k, rows, lanes] for k in range(5)],
    )


def clear_pads(grid, edge, span):
    high = grid.shape[1]
    wide = grid.shape[2]
    for k in range(5):
        grid[k, 0:ROWS, :] = jnp.zeros((ROWS, wide), F32)
        grid[k, ROWS + edge : high, :] = jnp.zeros((high - ROWS - edge, wide), F32)
        grid[k, ROWS : ROWS + edge, 0:LANES] = jnp.zeros((edge, LANES), F32)
        grid[k, ROWS : ROWS + edge, LANES + span : wide] = jnp.zeros((edge, LANES), F32)


def for_each_tile(edge, first, last, body):
    for top in range(0, edge, 2 * ROWS):

        def step(j, carry, top=top):
            body(top, pl.multiple_of(j * LANES, LANES))
            return carry

        lax.fori_loop(first, last, step, 0, unroll=True)


def plane_kernel(
    adjoint_hbm, rhs_hbm, state_hbm, face_hbm, pseudo_hbm, coord_hbm, weight_hbm, cell_hbm, vertex_hbm,
    xa_ref, xb_ref, adjoint_ref, rhs_ref, state_ref, face_ref, pseudo_ref, coord_ref, weight_ref, cell_ref,
    vertex_ref,
    xsides, sem,
):
    edge, span = pseudo_hbm.shape
    early, late = [], []

    def move(into, source, target):
        into.append(pltpu.make_async_copy(source, target, sem.at[len(early) + len(late)]))
        into[-1].start()

    fields = (
        (state_hbm, state_ref), (adjoint_hbm, adjoint_ref), (rhs_hbm, rhs_ref), (pseudo_hbm, pseudo_ref)
    )

    def rows_of(ref, first, count):
        return ref.at[(slice(None),) * (len(ref.shape) - 2) + (pl.ds(first, count),)]

    move(early, face_hbm, face_ref)
    for source, target in fields:
        for first in (0, edge - ROWS):
            move(early, rows_of(source, first, ROWS), rows_of(target, first, ROWS))
    for source, target in fields:
        move(late, rows_of(source, ROWS, edge - 2 * ROWS), rows_of(target, ROWS, edge - 2 * ROWS))
    for source, target in (
        (coord_hbm, coord_ref), (weight_hbm, weight_ref), (cell_hbm, cell_ref), (vertex_hbm, vertex_ref)
    ):
        move(late, source, target)
    for copy in early:
        copy.wait()
    even = is_even("grp")
    shape = (2, LANES)
    upper_row = lax.broadcasted_iota(jnp.int32, shape, 0) == 1
    sub = lax.broadcasted_iota(jnp.int32, (ROWS, LANES), 0)
    place = lax.broadcasted_iota(jnp.int32, shape, 1)
    tiles = span // LANES
    zero = jnp.zeros(shape, F32)

    def planes(ref, k, j, inner=0):
        at = (k,) if k is not None else ()
        lanes = slice(j * LANES, (j + 1) * LANES)
        last = edge - 2 - inner
        return jnp.where(upper_row, ref[at + (slice(last, last + 2), lanes)], ref[at + (slice(inner, inner + 2), lanes)])

    for j in range(tiles):
        lanes = pl.ds(j * LANES, LANES)
        faces = []
        for d in range(6):
            low = face_ref[d, pl.ds(0, 2 * ROWS), lanes].astype(F32)[:ROWS]
            high = face_ref[d, pl.ds(edge - 2 * ROWS, 2 * ROWS), lanes].astype(F32)[ROWS:]
            faces.append(jnp.where(sub == 0, low, pltpu.roll(high, 2, 0))[:2])
        vel, speed_sq, pressure, enthalpy, reach, faces, rhs = coefficients(
            [planes(state_ref, k, j) for k in range(5)],
            faces,
            planes(pseudo_ref, None, j),
            [planes(rhs_ref, k, j) for k in range(5)],
        )
        here = [planes(adjoint_ref, k, j) for k in range(5)]
        after = [planes(adjoint_ref, k, j + 1) if j + 1 < tiles else zero for k in range(5)]
        before = [planes(adjoint_ref, k, j - 1) if j > 0 else zero for k in range(5)]
        inner = [planes(adjoint_ref, k, j, 1) for k in range(5)]
        along_x = ([jnp.where(upper_row, 0.0, v) for v in inner], [jnp.where(upper_row, v, 0.0) for v in inner])
        pairs = lane_pairs(here, after, before, edge, shape)
        out = combine(
            rhs, reach, vel, speed_sq, enthalpy, inside_faces(faces, edge, shape), (along_x,) + pairs
        )
        message = out + here + [jnp.where(upper_row, faces[0], faces[1])] + vel + [enthalpy]
        message.append(jnp.where(place < edge, faces[3], faces[2]) if j == 0 else faces[2])
        for side in (0, 1):
            slot = jnp.where(even, 1 - side, side)
            for k, value in enumerate(message):
                xsides[slot, k : k + 1, lanes] = value[side : side + 1]
    xa_ref[...] = xsides[0]
    xb_ref[...] = xsides[1]
    for copy in late:
        copy.wait()


def first_kernel(
    adjoint_ref, rhs_ref, state_ref, face_ref, pseudo_ref, coord_ref, weight_ref, cell_ref, vertex_ref, count_ref,
    part_ref, ylo_ref, yhi_ref, column_ref, vertex_hot_ref, shape_ref,
    grid, coef,
):
    edge, span = pseudo_ref.shape
    clear_pads(grid, edge, span)
    for k in range(5):
        grid[k, ROWS : ROWS + edge, LANES : LANES + span] = adjoint_ref[k]

    def body(top, offset):
        lanes = pl.ds(offset, LANES)
        face_tiles = [face_ref[d, pl.ds(top, 2 * ROWS), lanes].astype(F32) for d in range(6)]
        for i_half in range(2):
            rows = pl.ds(top + i_half * ROWS, ROWS)
            vel, speed_sq, pressure, enthalpy, reach, faces, rhs = tile_coefficients(
                i_half, rows, lanes, state_ref, face_tiles, pseudo_ref, rhs_ref
            )
            out = sweep_tile(
                grid, ROWS + top + i_half * ROWS, pl.multiple_of(LANES + offset, LANES), edge,
                vel, speed_sq, enthalpy, reach, faces, rhs,
            )
            for k in range(5):
                part_ref[k, rows, lanes] = out[k]
            for k, value in enumerate(vel + [enthalpy] + faces[2:4]):
                coef[k, rows, lanes] = value

    for_each_tile(edge, 0, span // LANES, body)

    lane = lax.broadcasted_iota(jnp.int32, (edge, LANES), 1)
    quarter = lane // edge
    for side, base, ref in ((0, 0, ylo_ref), (1, span - LANES, yhi_ref)):
        lanes = slice(base, base + LANES)
        fields = [part_ref[k, :, lanes] for k in range(5)]
        fields += [grid[k, ROWS : ROWS + edge, LANES + base : LANES + base + LANES] for k in range(5)]
        fields += [coef[4 + 1 - side, :, lanes]]
        fields += [coef[k, :, lanes] for k in range(4)]
        start = 0 if side == 0 else LANES - edge
        per = LANES // edge
        for g in range(4):
            packed = None
            for q in range(per):
                k = g * per + q
                if k >= len(fields):
                    value = jnp.zeros((edge, LANES), F32)
                else:
                    shift = (q * edge - start) % LANES
                    value = pltpu.roll(fields[k], shift, 1) if shift else fields[k]
                packed = value if packed is None else jnp.where(quarter == q, value, packed)
            ref[g] = packed

    owners = count_ref.shape[1]
    slots = weight_ref.shape[1]
    capacity = slots // owners
    width = 2 * LANES
    step = min(slots, 512)
    for s in range(0, slots, step):
        part = slice(s, s + step)
        column = lax.rem(cell_ref[:, part] + LANES, width)
        column_ref[:, part] = hot((width, step), column)
        for c in range(4):
            vertex_hot_ref[c, :, part] = hot((LANES, step), lax.rem(vertex_ref[c : c + 1, part], LANES))

    group = max(capacity, LANES)
    together = group // capacity
    lane_group = lax.broadcasted_iota(jnp.int32, (1, group), 1)
    chunk = lane_group // capacity
    within = lax.rem(lane_group, capacity)
    for s in range(0, slots // group):
        lanes = slice(s * group, (s + 1) * group)
        count = count_ref[0, s * together]
        for q in range(1, together):
            count = jnp.where(chunk == q, count_ref[0, s * together + q], count)
        live = jnp.where(within < count, 1.0, 0.0)
        weights = [weight_ref[c : c + 1, lanes] * live for c in range(4)]
        corner = [[coord_ref[k, c : c + 1, lanes] for k in range(3)] for c in range(4)]
        for k, value in enumerate(tet_shapes(corner, weights)):
            shape_ref[k : k + 1, lanes] = value


def meet(axis_id, side, own, other):
    sign = 1.0 if side == 1 else -1.0
    mine = one_sided(own[11:14], own[14], axis_id, sign, other[5:10])
    theirs = one_sided(other[11:14], other[14], axis_id, -sign, own[5:10])
    added = [own[10] * v for v in mine]
    finished = [other[k] + other[10] * theirs[k] for k in range(5)]
    return added, finished


def second_kernel(xa_ref, xb_ref, ra_ref, rb_ref, ylo_ref, yhi_ref, res_ref, ya_ref, yb_ref, ysides):
    span = xa_ref.shape[1]
    edge = ylo_ref.shape[1]
    per = LANES // edge
    even = is_even("grp")
    even_y = is_even("blk")
    ysides[0] = ylo_ref[...]
    ysides[1] = yhi_ref[...]
    lane = lax.broadcasted_iota(jnp.int32, (1, LANES), 1)
    quarter = lane // edge

    def pick(a_ref, b_ref, flag):
        return [jnp.where(flag, a_ref[k : k + 1, :], b_ref[k : k + 1, :]) for k in range(15)]

    for side in (0, 1):
        flag = even if side == 1 else jnp.logical_not(even)
        own = pick(xa_ref, xb_ref, flag)
        other = pick(ra_ref, rb_ref, flag)
        added, finished = meet(0, side, own, other)
        row = 0 if side == 0 else edge - 1
        for k in range(5):
            res_ref[side, k : k + 1, :] = added[k]
            res_ref[side, 5 + k : 6 + k, :] = finished[k]
        for ys, base, start in ((0, 0, 0), (1, span - LANES, LANES - edge)):
            for k in range(5):
                g, q = divmod(k, per)
                shift = (q * edge - start) % LANES
                piece = added[k][:, base : base + LANES]
                piece = pltpu.roll(piece, shift, 1) if shift else piece
                old = ysides[ys, g, row : row + 1, :]
                ysides[ys, g, row : row + 1, :] = old + jnp.where(quarter == q, piece, 0.0)
                g, q = divmod(15, per)
                shift = (q * edge - start) % LANES
                piece = other[5 + k][:, base : base + LANES]
                piece = pltpu.roll(piece, shift, 1) if shift else piece
                at = 2 * k + side
                old = ysides[ys, g, at : at + 1, :]
                ysides[ys, g, at : at + 1, :] = jnp.where(quarter == q, piece, old)
    ya_ref[...] = ysides[jnp.where(even_y, 1, 0)]
    yb_ref[...] = ysides[jnp.where(even_y, 0, 1)]


def cross(left, right):
    return [
        left[1] * right[2] - left[2] * right[1],
        left[2] * right[0] - left[0] * right[2],
        left[0] * right[1] - left[1] * right[0],
    ]


def minus(left, right):
    return [u - v for u, v in zip(left, right)]


def tet_shapes(corner, weights):
    edge_one = minus(corner[1], corner[0])
    edge_two = minus(corner[2], corner[0])
    edge_three = minus(corner[3], corner[0])
    g1 = cross(edge_two, edge_three)
    g2 = cross(edge_three, edge_one)
    g3 = cross(edge_one, edge_two)
    g0 = [-(u + v + w) for u, v, w in zip(g1, g2, g3)]
    sixth = [w * (1.0 / 6.0) for w in weights]
    half = [w * 0.5 for w in weights]
    out = []
    for c, g in enumerate((g0, g1, g2, g3)):
        out += [sixth[c] * v for v in g]
    out += [half[1] * v for v in minus(corner[2], corner[3])]
    out += [half[2] * v for v in minus(corner[3], corner[1])]
    out += [half[3] * v for v in minus(corner[1], corner[2])]
    return out


def tet_terms(volume, face, shape):
    terms = []
    for c in range(4):
        term = [volume * shape[3 * c + k] for k in range(3)]
        if c:
            turned = cross(shape[9 + 3 * c : 12 + 3 * c], face)
            term = [u + v for u, v in zip(term, turned)]
        terms.append(term)
    return terms


def split(value):
    high = value.astype(BF16)
    return high, (value - high.astype(F32)).astype(BF16)


def hot(shape, index):
    rows = lax.broadcasted_iota(jnp.int16, shape, 0)
    return jnp.where(rows == index.astype(jnp.int16), jnp.ones((), BF16), jnp.zeros((), BF16))


def gather(high, low, column_ref, row):
    table_rows = high.shape[0] // 4
    slots = column_ref.shape[1]
    step = min(slots, 512)
    gathered = [[], [], [], []]
    for s in range(0, slots, step):
        column = column_ref[:, s : s + step]
        product = jnp.dot(high[...], column, preferred_element_type=F32)
        product = product + jnp.dot(low[...], column, preferred_element_type=F32)
        here = lax.broadcasted_iota(jnp.int32, (table_rows, step), 0) == row[:, s : s + step]
        for k in range(4):
            piece = product[k * table_rows : (k + 1) * table_rows]
            gathered[k].append(jnp.sum(jnp.where(here, piece, 0.0), axis=0, keepdims=True))
    return [jnp.concatenate(v, axis=1) for v in gathered]


def chunk_of(cell, span):
    yz = lax.rem(cell, span) + LANES
    return cell // span, lax.rem(yz // (2 * LANES), span // (2 * LANES))


def middle_kernel(
    part_ref, rhs_ref, state_ref, face_ref, pseudo_ref, res_ref, column_ref, cell_ref,
    out_ref, gathered_ref,
    grid, field, high, low, sem,
):
    edge, span = pseudo_ref.shape
    tiles = span // LANES
    for k in range(5):
        grid[k, ROWS : ROWS + edge, LANES : LANES + span] = part_ref[k]
    for k in range(5):
        for side, row, beyond in ((0, ROWS, ROWS - 1), (1, ROWS + edge - 1, ROWS + edge)):
            at = (k, slice(row, row + 1), slice(LANES, LANES + span))
            grid[at] = grid[at] + res_ref[side, k : k + 1, :]
            grid[k, beyond : beyond + 1, LANES : LANES + span] = res_ref[side, 5 + k : 6 + k, :]

    def body(top, offset):
        lanes = pl.ds(offset, LANES)
        face_tiles = [face_ref[d, pl.ds(top, 2 * ROWS), lanes].astype(F32) for d in range(6)]
        tables = [[], [], [], []]
        for i_half in range(2):
            rows = pl.ds(top + i_half * ROWS, ROWS)
            vel, speed_sq, pressure, enthalpy, reach, faces, rhs = tile_coefficients(
                i_half, rows, lanes, state_ref, face_tiles, pseudo_ref, rhs_ref
            )
            out = sweep_tile(
                grid, ROWS + top + i_half * ROWS, pl.multiple_of(LANES + offset, LANES), edge,
                vel, speed_sq, enthalpy, reach, faces, rhs,
            )
            for k in range(5):
                field[k, rows, pl.ds(pl.multiple_of(offset - LANES, LANES), LANES)] = out[k]
            for k in range(4):
                tables[k].append(pressure * out[1 + k])
        chunk = (offset - LANES) // (2 * LANES)
        wide = pl.ds(pl.multiple_of(lax.rem(offset - LANES, 2 * LANES), LANES), LANES)
        for k in range(4):
            big, small = split(jnp.concatenate(tables[k], axis=0))
            at = pl.ds(pl.multiple_of(k * (high.shape[0] // 4) + chunk * edge + top, 2 * ROWS), 2 * ROWS)
            high[at, wide] = big
            low[at, wide] = small

    for_each_tile(edge, 1, tiles - 1, body)
    store = pltpu.make_async_copy(field, out_ref.at[:, :, pl.ds(LANES, span - 2 * LANES)], sem)
    store.start()
    x, chunk = chunk_of(cell_ref[...], span)
    row = jnp.where(chunk > 0, (chunk - 1) * edge + x, -1)
    for k, value in enumerate(gather(high, low, column_ref, row)):
        gathered_ref[k : k + 1, :] = value
    store.wait()


def third_kernel(
    adjoint_ref, part_ref, rhs_ref, state_ref, face_ref, pseudo_ref, res_ref, ra_ref, rb_ref,
    ya_ref, yb_ref, sa_ref, sb_ref, gathered_ref, column_ref, cell_ref, vertex_ref, vertex_hot_ref, shape_ref,
    out_ref, keep_ref, send_ref,
    grids, field, high, low, sums, sem,
):
    edge, span = pseudo_ref.shape
    per = LANES // edge
    owners = 2 * keep_ref.shape[0]
    slots = cell_ref.shape[1]
    capacity = slots // owners
    even = is_even("grp")
    even_y = is_even("blk")
    lane = lax.broadcasted_iota(jnp.int32, (edge, LANES), 1)
    lane_row = lax.broadcasted_iota(jnp.int32, (1, LANES), 1)
    rows = slice(ROWS, ROWS + edge)
    stores = []

    def pick(a_ref, b_ref, flag, k):
        g, q = divmod(k, per)
        value = jnp.where(flag, a_ref[g], b_ref[g])
        return pltpu.roll(value, LANES - q * edge, 1) if q else value

    for side in (0, 1):
        grid = grids.at[side]
        start = 0 if side == 0 else span - 2 * LANES
        lanes = slice(start, start + 2 * LANES)
        base = LANES if side == 0 else 0
        into = slice(base, base + 2 * LANES)
        for k in range(5):
            grid[k, rows, into] = part_ref[k, :, lanes]
            for xs, row, beyond in ((0, ROWS, ROWS - 1), (1, ROWS + edge - 1, ROWS + edge)):
                at = (k, slice(row, row + 1), into)
                grid[at] = grid[at] + res_ref[xs, k : k + 1, lanes]
                grid[k, beyond : beyond + 1, into] = res_ref[xs, 5 + k : 6 + k, lanes]
        flag = even_y if side == 1 else jnp.logical_not(even_y)
        own = [pick(ya_ref, yb_ref, flag, k) for k in range(15)]
        other = [pick(sa_ref, sb_ref, flag, k) for k in range(16)]
        added, finished = meet(1, side, own, other[:15])
        beyond = 0 if side == 0 else 2 * LANES
        for k in range(5):
            if side == 0:
                extra = jnp.where(lane < edge, added[k], 0.0)
                halo = pltpu.roll(finished[k], LANES - edge, 1)
            else:
                extra = jnp.where(lane >= LANES - edge, pltpu.roll(added[k], LANES - edge, 1), 0.0)
                halo = finished[k]
            at = (k, rows, slice(LANES, 2 * LANES))
            grid[at] = grid[at] + extra
            grid[k, rows, beyond : beyond + LANES] = halo
        start = 0 if side == 0 else span - LANES
        for xs, row in ((0, ROWS - 1), (1, ROWS + edge)):
            flag_x = even if xs == 1 else jnp.logical_not(even)
            lanes = slice(start, start + LANES)
            state = [jnp.where(flag_x, ra_ref[k : k + 1, lanes], rb_ref[k : k + 1, lanes]) for k in range(11, 16)]
            corner = [other[15][2 * k + xs : 2 * k + xs + 1, :] for k in range(5)]
            if side == 1:
                corner = [pltpu.roll(v, LANES - edge, 1) for v in corner]
            extra = one_sided(state[:3], state[3], 1, 1.0 if side == 1 else -1.0, corner)
            inside = lane_row < edge if side == 0 else lane_row >= LANES - edge
            for k in range(5):
                at = (k, slice(row, row + 1), slice(LANES, 2 * LANES))
                grid[at] = grid[at] + jnp.where(inside, state[4] * extra[k], 0.0)

        lanes = pl.ds(start, LANES)
        wide = slice(LANES, 2 * LANES) if side == 0 else slice(0, LANES)
        for top in range(0, edge, 2 * ROWS):
            face_tiles = [face_ref[d, pl.ds(top, 2 * ROWS), lanes].astype(F32) for d in range(6)]
            tables = [[], [], [], []]
            for i_half in range(2):
                here = pl.ds(top + i_half * ROWS, ROWS)
                vel, speed_sq, pressure, enthalpy, reach, faces, rhs = tile_coefficients(
                    i_half, here, lanes, state_ref, face_tiles, pseudo_ref, rhs_ref
                )
                out = sweep_tile(
                    grid, ROWS + top + i_half * ROWS, LANES, edge, vel, speed_sq, enthalpy, reach, faces, rhs
                )
                for k in range(5):
                    field[side, k, here, :] = out[k]
                for k in range(4):
                    tables[k].append(pressure * out[1 + k])
            for k in range(4):
                big, small = split(jnp.concatenate(tables[k], axis=0))
                at = slice(k * edge + top, k * edge + top + 2 * ROWS)
                high[at, wide] = big
                low[at, wide] = small
        store = pltpu.make_async_copy(field.at[side], out_ref.at[:, :, lanes], sem.at[side])
        store.start()
        stores.append(store)

    x, number = chunk_of(cell_ref[...], span)
    gathered = gather(high, low, column_ref, jnp.where(number == 0, x, -1))
    gathered = [gathered_ref[k : k + 1, :] + v for k, v in enumerate(gathered)]

    group = max(capacity, LANES)
    together = group // capacity
    vertex_rows = -(-together * PARTS // 16) * 16
    chunk = lax.broadcasted_iota(jnp.int32, (1, group), 1) // capacity
    for s in range(0, slots // group):
        lanes = slice(s * group, (s + 1) * group)
        shape = [shape_ref[k : k + 1, lanes] for k in range(21)]
        terms = tet_terms(gathered[3][:, lanes], [gathered[k][:, lanes] for k in range(3)], shape)
        left, right = [], []
        for c in range(4):
            row = vertex_ref[c : c + 1, lanes] // LANES + chunk * PARTS
            match = lax.broadcasted_iota(jnp.int16, (vertex_rows, group), 0) == row.astype(jnp.int16)
            blocks = []
            for k in range(3):
                blocks += [jnp.where(match, v, jnp.zeros((), BF16)) for v in split(terms[c][k])]
            left.append(jnp.concatenate(blocks, axis=0))
            right.append(vertex_hot_ref[c, :, lanes])
        product = lax.dot_general(
            jnp.concatenate(left, axis=1), jnp.concatenate(right, axis=1),
            (((1,), (1,)), ((), ())), preferred_element_type=F32,
        )
        for k in range(3):
            big = product[2 * k * vertex_rows : (2 * k + 1) * vertex_rows]
            small = product[(2 * k + 1) * vertex_rows : (2 * k + 2) * vertex_rows]
            total = big + small
            for q in range(together):
                owner = s * together + q
                sums[owner % 2, owner // 2, k * PARTS : (k + 1) * PARTS, :] = total[q * PARTS : (q + 1) * PARTS]
    core = lax.rem(lax.axis_index("blk"), 2)
    keep_ref[...] = sums[1 - core]
    send_ref[...] = sums[core]
    for store in stores:
        store.wait()


def fourth_kernel(keep_ref, got_ref, *refs):
    count = keep_ref.shape[0]
    me = lax.rem(lax.axis_index("blk") // 2, count)
    for k, ref in enumerate(refs):
        partner = lax.bitwise_xor(me, k)
        ref[...] = keep_ref[partner] + got_ref[partner]


def last_kernel(*refs):
    total = refs[0][...]
    for ref in refs[1:-1]:
        total = total + ref[...]
    for k in range(3):
        for part in range(PARTS):
            at = k * PARTS + part
            refs[-1][k : k + 1, part * LANES : (part + 1) * LANES] = total[at : at + 1, :]


def swap(value, axis, pairs):
    return lax.ppermute(value, axis, pairs + [(b, a) for a, b in pairs])


def neighbours(value_a, value_b, axis):
    count = lax.axis_size(axis)
    first = [(i, i + 1) for i in range(0, count - 1, 2)]
    second = [(i, i + 1) for i in range(1, count - 1, 2)]
    return swap(value_a, axis, first), swap(value_b, axis, second)


def local(
    adjoint_init, adjoint_rhs, flow_state, face_weights, pseudo_time,
    tet_coords, tet_weights, tet_cell, tet_vertex, tet_count,
):
    edge, span = pseudo_time.shape
    owners = tet_count.shape[1]
    blocks = lax.axis_size("blk")
    padded = (5, edge + 2 * ROWS, span + 2 * LANES)
    struct = jax.ShapeDtypeStruct
    packed = (16 * edge // LANES, edge, LANES)
    slots = tet_cell.shape[0]
    cell = tet_cell.reshape(1, slots)
    message = struct((16, span), F32)
    fields = (adjoint_init, adjoint_rhs, flow_state, face_weights, pseudo_time)
    arrays = (*fields, jnp.transpose(tet_coords, (1, 0, 2)), tet_weights, cell, tet_vertex)
    xa, xb, *arrays = call(
        plane_kernel,
        [message] * 2 + [struct(v.shape, v.dtype) for v in arrays],
        [HBM] * 9,
        [VMEM] * 11,
        [pltpu.VMEM((2, 16, span), F32), pltpu.SemaphoreType.DMA((17,))],
        "plane_messages",
    )(*(pltpu.with_memory_space_constraint(v, pltpu.HBM) for v in arrays))
    fields, (coords, weights, cell, vertex) = arrays[:5], arrays[5:]
    ra, rb = neighbours(xa, xb, "grp")
    part, ylo, yhi, column, vertex_hot, shapes = call(
        first_kernel,
        [struct((5, edge, span), F32), struct(packed, F32), struct(packed, F32), struct((2 * LANES, slots), BF16),
         struct((4, LANES, slots), BF16), struct((24, slots), F32)],
        [VMEM] * 9 + [SMEM],
        [VMEM] * 6,
        [pltpu.VMEM(padded, F32), pltpu.VMEM((6, edge, span), F32)],
        "partial_sweep",
        flops=12_000_000,
    )(*fields, coords, weights, cell, vertex, tet_count)
    res, ya, yb = call(
        second_kernel,
        [struct((2, 16, span), F32), struct(packed, F32), struct(packed, F32)],
        [VMEM] * 6,
        [VMEM] * 3,
        [pltpu.VMEM((2,) + packed, F32)],
        "streamwise_halo",
    )(xa, xb, ra, rb, ylo, yhi)
    sa, sb = neighbours(ya, yb, "blk")
    table = (4 * edge * (span // (2 * LANES) - 1), 2 * LANES)
    adjoint, gathered = call(
        middle_kernel,
        [struct((5, edge, span), F32), struct((4, slots), F32)],
        [VMEM] * 8,
        [HBM, VMEM],
        [pltpu.VMEM(padded, F32), pltpu.VMEM((5, edge, span - 2 * LANES), F32), pltpu.VMEM(table, BF16),
         pltpu.VMEM(table, BF16), pltpu.SemaphoreType.DMA],
        "middle_sweep",
        flops=12_000_000,
    )(part, *fields[1:], res, column, cell)
    half = owners // 2
    sums_shape = (half, 3 * PARTS, LANES)
    table = (4 * edge, 2 * LANES)
    adjoint, keep, send = call(
        third_kernel,
        [struct((5, edge, span), F32), struct(sums_shape, F32), struct(sums_shape, F32)],
        [HBM] + [VMEM] * 18,
        [HBM, VMEM, VMEM],
        [pltpu.VMEM((2, 5, edge + 2 * ROWS, 3 * LANES), F32), pltpu.VMEM((2, 5, edge, LANES), F32),
         pltpu.VMEM(table, BF16), pltpu.VMEM(table, BF16), pltpu.VMEM((2,) + sums_shape, F32),
         pltpu.SemaphoreType.DMA((2,))],
        "edge_sweep_and_sums",
        flops=12_000_000,
        aliases={0: 0},
    )(
        adjoint, part, *fields[1:], res, ra, rb, ya, yb, sa, sb,
        gathered, column, cell, vertex, vertex_hot, shapes,
    )
    got = swap(send, "blk", [(i, i + 1) for i in range(0, blocks, 2)])
    place = lax.axis_index("blk") // 2
    while half > 4:
        half //= 2
        both = (keep + got).reshape(2, half, 3 * PARTS, LANES)
        bit = lax.rem(place // half, 2)
        keep = lax.dynamic_index_in_dim(both, bit, 0, keepdims=False)
        send = lax.dynamic_index_in_dim(both, 1 - bit, 0, keepdims=False)
        got = lax.ppermute(send, "blk", [(i, i ^ (2 * half)) for i in range(blocks)])
    one = struct((3 * PARTS, LANES), F32)
    parts = call(
        fourth_kernel, [one] * half, [VMEM] * 2, [VMEM] * half, [], "core_pair_sums"
    )(keep, got)
    parts = [lax.ppermute(v, "blk", [(i, i ^ (2 * k + 1)) for i in range(blocks)]) for k, v in enumerate(parts)]
    sensitivity = call(last_kernel, struct((3, VERT_DEV), F32), [VMEM] * half, VMEM, [], "own_sums")(*parts)
    return adjoint, sensitivity


def solution(mesh):
    return jax.shard_map(
        local,
        mesh=mesh,
        in_specs=(
            P(None, "grp", "blk"),
            P(None, "grp", "blk"),
            P(None, "grp", "blk"),
            P(None, "grp", "blk"),
            P("grp", "blk"),
            P(None, None, ("grp", "blk")),
            P(None, ("grp", "blk")),
            P(("grp", "blk")),
            P(None, ("grp", "blk")),
            P(("grp", "blk"), None),
        ),
        out_specs=(P(None, "grp", "blk"), P(None, ("grp", "blk"))),
        check_vma=False,
    )
```

```python
import functools
import jax
import jax.numpy as jnp
from jax import lax
from jax.experimental import pallas as pl
from jax.experimental.pallas import tpu as pltpu
from jax.sharding import PartitionSpec as P

VERT_DEV = 1536
GAMMA = 1.4
LANES = 128
ROWS = 8
PARTS = VERT_DEV // LANES
F32 = jnp.float32
BF16 = jnp.bfloat16
VMEM = pl.BlockSpec(memory_space=pltpu.VMEM)
SMEM = pl.BlockSpec(memory_space=pltpu.SMEM)
HBM = pl.BlockSpec(memory_space=pltpu.HBM)
LIMIT = 40 * 1024 * 1024


def call(kernel, outs, in_specs, out_specs, scratch, name, flops=1000, aliases={}):
    return pl.pallas_call(
        kernel,
        out_shape=outs,
        in_specs=in_specs,
        out_specs=out_specs,
        scratch_shapes=scratch,
        compiler_params=pltpu.CompilerParams(vmem_limit_bytes=LIMIT),
        cost_estimate=pl.CostEstimate(flops=flops, bytes_accessed=flops // 4, transcendentals=0),
        input_output_aliases=aliases,
        name=name,
    )


def is_even(axis):
    return lax.rem(lax.axis_index(axis), 2) == 0


def reach_of(speed_sq, enthalpy):
    sound_sq = (GAMMA - 1.0) * (enthalpy - 0.5 * speed_sq)
    return jnp.sqrt(speed_sq) + jnp.sqrt(sound_sq)


def transposed(vel, enthalpy, half_sq, axis_id, field):
    normal = vel[axis_id]
    energy = normal * field[4]
    common = vel[0] * field[1] + vel[1] * field[2] + vel[2] * field[3] + enthalpy * field[4]
    along = field[1 + axis_id] + energy
    scaled = (GAMMA - 1.0) * along
    out = [half_sq * along - normal * common]
    for j in range(3):
        entry = normal * field[1 + j] - vel[j] * scaled
        if j == axis_id:
            entry = entry + (field[0] + common)
        out.append(entry)
    out.append(scaled + energy)
    return out


def one_sided(vel, enthalpy, axis_id, sign, field):
    speed_sq = vel[0] * vel[0] + vel[1] * vel[1] + vel[2] * vel[2]
    reach = reach_of(speed_sq, enthalpy)
    turned = transposed(vel, enthalpy, 0.5 * (GAMMA - 1.0) * speed_sq, axis_id, field)
    return [sign * turned[k] + reach * field[k] for k in range(5)]


def cell_state(state):
    density, m1, m2, m3, energy = state
    inverse = 1.0 / density
    vel = [m1 * inverse, m2 * inverse, m3 * inverse]
    speed_sq = vel[0] * vel[0] + vel[1] * vel[1] + vel[2] * vel[2]
    pressure = (GAMMA - 1.0) * (energy - 0.5 * density * speed_sq)
    enthalpy = (energy + pressure) * inverse
    reach = jnp.sqrt(speed_sq) + jnp.sqrt(GAMMA * pressure * inverse)
    return vel, speed_sq, pressure, enthalpy, reach


def combine(rhs, reach, vel, speed_sq, enthalpy, faces, pairs):
    spread = None
    scaled = None
    for axis_id, (upper, lower) in enumerate(pairs):
        upper = [faces[2 * axis_id] * v for v in upper]
        lower = [faces[2 * axis_id + 1] * v for v in lower]
        both = [u + v for u, v in zip(upper, lower)]
        field = [u - v for u, v in zip(upper, lower)]
        spread = both if spread is None else [u + v for u, v in zip(spread, both)]
        normal = vel[axis_id]
        energy = normal * field[4]
        common = vel[0] * field[1] + vel[1] * field[2] + vel[2] * field[3] + enthalpy * field[4]
        along = field[1 + axis_id] + energy
        parts = [normal * common] + [normal * field[1 + j] for j in range(3)] + [energy]
        parts[1 + axis_id] = parts[1 + axis_id] + (field[0] + common)
        if scaled is None:
            scaled, total = along, parts
        else:
            scaled = scaled + along
            total = [u + v for u, v in zip(total, parts)]
    scaled = (GAMMA - 1.0) * scaled
    turned = [0.5 * speed_sq * scaled - total[0]]
    turned += [total[1 + j] - vel[j] * scaled for j in range(3)]
    turned.append(scaled + total[4])
    return [rhs[k] + turned[k] + reach * spread[k] for k in range(5)]


def inside_faces(faces, edge, shape):
    depth = lax.rem(lax.broadcasted_iota(jnp.int32, shape, 1), edge)
    faces = list(faces)
    faces[4] = jnp.where(depth == edge - 1, 0.0, faces[4])
    faces[5] = jnp.where(depth == 0, 0.0, faces[5])
    return faces


def lane_pairs(here, after, before, edge, shape):
    place = lax.broadcasted_iota(jnp.int32, shape, 1)
    first = place < edge
    last = place >= LANES - edge
    along_y = (
        [pltpu.roll(jnp.where(first, a, h), LANES - edge, 1) for h, a in zip(here, after)],
        [pltpu.roll(jnp.where(last, b, h), edge, 1) for h, b in zip(here, before)],
    )
    along_z = ([pltpu.roll(h, LANES - 1, 1) for h in here], [pltpu.roll(h, 1, 1) for h in here])
    return along_y, along_z


def sweep_tile(grid, row, lane, edge, vel, speed_sq, enthalpy, reach, faces, rhs):
    def at(drow, dlane):
        return [grid[k, pl.ds(row + drow, ROWS), pl.ds(lane + dlane, LANES)] for k in range(5)]

    shape = (ROWS, LANES)
    pairs = lane_pairs(at(0, 0), at(0, LANES), at(0, -LANES), edge, shape)
    return combine(
        rhs, reach, vel, speed_sq, enthalpy, inside_faces(faces, edge, shape), ((at(1, 0), at(-1, 0)),) + pairs
    )


def coefficients(state, faces, pseudo, rhs):
    vel, speed_sq, pressure, enthalpy, reach = cell_state(state)
    area = faces[0]
    for f in faces[1:]:
        area = area + f
    inverse = 1.0 / (pseudo + 0.5 * reach * area)
    half = 0.5 * inverse
    return vel, speed_sq, pressure, enthalpy, reach, [half * f for f in faces], [inverse * v for v in rhs]


def tile_coefficients(i_half, rows, lanes, state_ref, face_tiles, pseudo_ref, rhs_ref):
    return coefficients(
        [state_ref[k, rows, lanes] for k in range(5)],
        [f[i_half * ROWS : (i_half + 1) * ROWS] for f in face_tiles],
        pseudo_ref[rows, lanes],
        [rhs_ref[k, rows, lanes] for k in range(5)],
    )


def clear_pads(grid, edge, span):
    high = grid.shape[1]
    wide = grid.shape[2]
    for k in range(5):
        grid[k, 0:ROWS, :] = jnp.zeros((ROWS, wide), F32)
        grid[k, ROWS + edge : high, :] = jnp.zeros((high - ROWS - edge, wide), F32)
        grid[k, ROWS : ROWS + edge, 0:LANES] = jnp.zeros((edge, LANES), F32)
        grid[k, ROWS : ROWS + edge, LANES + span : wide] = jnp.zeros((edge, LANES), F32)


def for_each_tile(edge, first, last, body):
    for top in range(0, edge, 2 * ROWS):

        def step(j, carry, top=top):
            body(top, pl.multiple_of(j * LANES, LANES))
            return carry

        lax.fori_loop(first, last, step, 0, unroll=True)


def plane_kernel(
    adjoint_hbm, rhs_hbm, state_hbm, face_hbm, pseudo_hbm, coord_hbm, weight_hbm, cell_hbm, vertex_hbm,
    xa_ref, xb_ref, adjoint_ref, rhs_ref, state_ref, face_ref, pseudo_ref, coord_ref, weight_ref, cell_ref,
    vertex_ref,
    xsides, sem,
):
    edge, span = pseudo_hbm.shape
    early, late = [], []

    def move(into, source, target):
        into.append(pltpu.make_async_copy(source, target, sem.at[len(early) + len(late)]))
        into[-1].start()

    fields = (
        (state_hbm, state_ref), (adjoint_hbm, adjoint_ref), (rhs_hbm, rhs_ref), (pseudo_hbm, pseudo_ref)
    )

    def rows_of(ref, first, count):
        return ref.at[(slice(None),) * (len(ref.shape) - 2) + (pl.ds(first, count),)]

    move(early, face_hbm, face_ref)
    for source, target in fields:
        for first in (0, edge - ROWS):
            move(early, rows_of(source, first, ROWS), rows_of(target, first, ROWS))
    for source, target in fields:
        move(late, rows_of(source, ROWS, edge - 2 * ROWS), rows_of(target, ROWS, edge - 2 * ROWS))
    for source, target in (
        (coord_hbm, coord_ref), (weight_hbm, weight_ref), (cell_hbm, cell_ref), (vertex_hbm, vertex_ref)
    ):
        move(late, source, target)
    for copy in early:
        copy.wait()
    even = is_even("grp")
    shape = (2, LANES)
    upper_row = lax.broadcasted_iota(jnp.int32, shape, 0) == 1
    sub = lax.broadcasted_iota(jnp.int32, (ROWS, LANES), 0)
    place = lax.broadcasted_iota(jnp.int32, shape, 1)
    tiles = span // LANES
    zero = jnp.zeros(shape, F32)

    def planes(ref, k, j, inner=0):
        at = (k,) if k is not None else ()
        lanes = slice(j * LANES, (j + 1) * LANES)
        last = edge - 2 - inner
        return jnp.where(upper_row, ref[at + (slice(last, last + 2), lanes)], ref[at + (slice(inner, inner + 2), lanes)])

    for j in range(tiles):
        lanes = pl.ds(j * LANES, LANES)
        faces = []
        for d in range(6):
            low = face_ref[d, pl.ds(0, 2 * ROWS), lanes].astype(F32)[:ROWS]
            high = face_ref[d, pl.ds(edge - 2 * ROWS, 2 * ROWS), lanes].astype(F32)[ROWS:]
            faces.append(jnp.where(sub == 0, low, pltpu.roll(high, 2, 0))[:2])
        vel, speed_sq, pressure, enthalpy, reach, faces, rhs = coefficients(
            [planes(state_ref, k, j) for k in range(5)],
            faces,
            planes(pseudo_ref, None, j),
            [planes(rhs_ref, k, j) for k in range(5)],
        )
        here = [planes(adjoint_ref, k, j) for k in range(5)]
        after = [planes(adjoint_ref, k, j + 1) if j + 1 < tiles else zero for k in range(5)]
        before = [planes(adjoint_ref, k, j - 1) if j > 0 else zero for k in range(5)]
        inner = [planes(adjoint_ref, k, j, 1) for k in range(5)]
        along_x = ([jnp.where(upper_row, 0.0, v) for v in inner], [jnp.where(upper_row, v, 0.0) for v in inner])
        pairs = lane_pairs(here, after, before, edge, shape)
        out = combine(
            rhs, reach, vel, speed_sq, enthalpy, inside_faces(faces, edge, shape), (along_x,) + pairs
        )
        message = out + here + [jnp.where(upper_row, faces[0], faces[1])] + vel + [enthalpy]
        message.append(jnp.where(place < edge, faces[3], faces[2]) if j == 0 else faces[2])
        for side in (0, 1):
            slot = jnp.where(even, 1 - side, side)
            for k, value in enumerate(message):
                xsides[slot, k : k + 1, lanes] = value[side : side + 1]
    xa_ref[...] = xsides[0]
    xb_ref[...] = xsides[1]
    for copy in late:
        copy.wait()


def first_kernel(
    adjoint_ref, rhs_ref, state_ref, face_ref, pseudo_ref, coord_ref, weight_ref, cell_ref, vertex_ref, count_ref,
    part_ref, ylo_ref, yhi_ref, column_ref, vertex_hot_ref, shape_ref,
    grid, coef,
):
    edge, span = pseudo_ref.shape
    clear_pads(grid, edge, span)
    for k in range(5):
        grid[k, ROWS : ROWS + edge, LANES : LANES + span] = adjoint_ref[k]

    def body(top, offset):
        lanes = pl.ds(offset, LANES)
        face_tiles = [face_ref[d, pl.ds(top, 2 * ROWS), lanes].astype(F32) for d in range(6)]
        for i_half in range(2):
            rows = pl.ds(top + i_half * ROWS, ROWS)
            vel, speed_sq, pressure, enthalpy, reach, faces, rhs = tile_coefficients(
                i_half, rows, lanes, state_ref, face_tiles, pseudo_ref, rhs_ref
            )
            out = sweep_tile(
                grid, ROWS + top + i_half * ROWS, pl.multiple_of(LANES + offset, LANES), edge,
                vel, speed_sq, enthalpy, reach, faces, rhs,
            )
            for k in range(5):
                part_ref[k, rows, lanes] = out[k]
            for k, value in enumerate(vel + [enthalpy] + faces[2:4]):
                coef[k, rows, lanes] = value

    for_each_tile(edge, 0, span // LANES, body)

    lane = lax.broadcasted_iota(jnp.int32, (edge, LANES), 1)
    quarter = lane // edge
    for side, base, ref in ((0, 0, ylo_ref), (1, span - LANES, yhi_ref)):
        lanes = slice(base, base + LANES)
        fields = [part_ref[k, :, lanes] for k in range(5)]
        fields += [grid[k, ROWS : ROWS + edge, LANES + base : LANES + base + LANES] for k in range(5)]
        fields += [coef[4 + 1 - side, :, lanes]]
        fields += [coef[k, :, lanes] for k in range(4)]
        start = 0 if side == 0 else LANES - edge
        per = LANES // edge
        for g in range(4):
            packed = None
            for q in range(per):
                k = g * per + q
                if k >= len(fields):
                    value = jnp.zeros((edge, LANES), F32)
                else:
                    shift = (q * edge - start) % LANES
                    value = pltpu.roll(fields[k], shift, 1) if shift else fields[k]
                packed = value if packed is None else jnp.where(quarter == q, value, packed)
            ref[g] = packed

    owners = count_ref.shape[1]
    slots = weight_ref.shape[1]
    capacity = slots // owners
    width = 2 * LANES
    step = min(slots, 512)
    for s in range(0, slots, step):
        part = slice(s, s + step)
        column = lax.rem(cell_ref[:, part] + LANES, width)
        column_ref[:, part] = hot((width, step), column)
        for c in range(4):
            vertex_hot_ref[c, :, part] = hot((LANES, step), lax.rem(vertex_ref[c : c + 1, part], LANES))

    group = max(capacity, LANES)
    together = group // capacity
    lane_group = lax.broadcasted_iota(jnp.int32, (1, group), 1)
    chunk = lane_group // capacity
    within = lax.rem(lane_group, capacity)
    for s in range(0, slots // group):
        lanes = slice(s * group, (s + 1) * group)
        count = count_ref[0, s * together]
        for q in range(1, together):
            count = jnp.where(chunk == q, count_ref[0, s * together + q], count)
        live = jnp.where(within < count, 1.0, 0.0)
        weights = [weight_ref[c : c + 1, lanes] * live for c in range(4)]
        corner = [[coord_ref[k, c : c + 1, lanes] for k in range(3)] for c in range(4)]
        for k, value in enumerate(tet_shapes(corner, weights)):
            shape_ref[k : k + 1, lanes] = value


def meet(axis_id, side, own, other):
    sign = 1.0 if side == 1 else -1.0
    mine = one_sided(own[11:14], own[14], axis_id, sign, other[5:10])
    theirs = one_sided(other[11:14], other[14], axis_id, -sign, own[5:10])
    added = [own[10] * v for v in mine]
    finished = [other[k] + other[10] * theirs[k] for k in range(5)]
    return added, finished


def second_kernel(xa_ref, xb_ref, ra_ref, rb_ref, ylo_ref, yhi_ref, res_ref, ya_ref, yb_ref, ysides):
    span = xa_ref.shape[1]
    edge = ylo_ref.shape[1]
    per = LANES // edge
    even = is_even("grp")
    even_y = is_even("blk")
    ysides[0] = ylo_ref[...]
    ysides[1] = yhi_ref[...]
    lane = lax.broadcasted_iota(jnp.int32, (1, LANES), 1)
    quarter = lane // edge

    def pick(a_ref, b_ref, flag):
        return [jnp.where(flag, a_ref[k : k + 1, :], b_ref[k : k + 1, :]) for k in range(15)]

    for side in (0, 1):
        flag = even if side == 1 else jnp.logical_not(even)
        own = pick(xa_ref, xb_ref, flag)
        other = pick(ra_ref, rb_ref, flag)
        added, finished = meet(0, side, own, other)
        row = 0 if side == 0 else edge - 1
        for k in range(5):
            res_ref[side, k : k + 1, :] = added[k]
            res_ref[side, 5 + k : 6 + k, :] = finished[k]
        for ys, base, start in ((0, 0, 0), (1, span - LANES, LANES - edge)):
            for k in range(5):
                g, q = divmod(k, per)
                shift = (q * edge - start) % LANES
                piece = added[k][:, base : base + LANES]
                piece = pltpu.roll(piece, shift, 1) if shift else piece
                old = ysides[ys, g, row : row + 1, :]
                ysides[ys, g, row : row + 1, :] = old + jnp.where(quarter == q, piece, 0.0)
                g, q = divmod(15, per)
                shift = (q * edge - start) % LANES
                piece = other[5 + k][:, base : base + LANES]
                piece = pltpu.roll(piece, shift, 1) if shift else piece
                at = 2 * k + side
                old = ysides[ys, g, at : at + 1, :]
                ysides[ys, g, at : at + 1, :] = jnp.where(quarter == q, piece, old)
    ya_ref[...] = ysides[jnp.where(even_y, 1, 0)]
    yb_ref[...] = ysides[jnp.where(even_y, 0, 1)]


def cross(left, right):
    return [
        left[1] * right[2] - left[2] * right[1],
        left[2] * right[0] - left[0] * right[2],
        left[0] * right[1] - left[1] * right[0],
    ]


def minus(left, right):
    return [u - v for u, v in zip(left, right)]


def tet_shapes(corner, weights):
    edge_one = minus(corner[1], corner[0])
    edge_two = minus(corner[2], corner[0])
    edge_three = minus(corner[3], corner[0])
    g1 = cross(edge_two, edge_three)
    g2 = cross(edge_three, edge_one)
    g3 = cross(edge_one, edge_two)
    g0 = [-(u + v + w) for u, v, w in zip(g1, g2, g3)]
    sixth = [w * (1.0 / 6.0) for w in weights]
    half = [w * 0.5 for w in weights]
    out = []
    for c, g in enumerate((g0, g1, g2, g3)):
        out += [sixth[c] * v for v in g]
    out += [half[1] * v for v in minus(corner[2], corner[3])]
    out += [half[2] * v for v in minus(corner[3], corner[1])]
    out += [half[3] * v for v in minus(corner[1], corner[2])]
    return out


def tet_terms(volume, face, shape):
    terms = []
    for c in range(4):
        term = [volume * shape[3 * c + k] for k in range(3)]
        if c:
            turned = cross(shape[9 + 3 * c : 12 + 3 * c], face)
            term = [u + v for u, v in zip(term, turned)]
        terms.append(term)
    return terms


def split(value):
    high = value.astype(BF16)
    return high, (value - high.astype(F32)).astype(BF16)


def hot(shape, index):
    rows = lax.broadcasted_iota(jnp.int16, shape, 0)
    return jnp.where(rows == index.astype(jnp.int16), jnp.ones((), BF16), jnp.zeros((), BF16))


def gather(high, low, column_ref, row):
    table_rows = high.shape[0] // 4
    slots = column_ref.shape[1]
    step = min(slots, 512)
    gathered = [[], [], [], []]
    for s in range(0, slots, step):
        column = column_ref[:, s : s + step]
        product = jnp.dot(high[...], column, preferred_element_type=F32)
        product = product + jnp.dot(low[...], column, preferred_element_type=F32)
        here = lax.broadcasted_iota(jnp.int32, (table_rows, step), 0) == row[:, s : s + step]
        for k in range(4):
            piece = product[k * table_rows : (k + 1) * table_rows]
            gathered[k].append(jnp.sum(jnp.where(here, piece, 0.0), axis=0, keepdims=True))
    return [jnp.concatenate(v, axis=1) for v in gathered]


def chunk_of(cell, span):
    yz = lax.rem(cell, span) + LANES
    return cell // span, lax.rem(yz // (2 * LANES), span // (2 * LANES))


def middle_kernel(
    part_ref, rhs_ref, state_ref, face_ref, pseudo_ref, res_ref, column_ref, cell_ref,
    out_ref, gathered_ref,
    grid, field, high, low, sem,
):
    edge, span = pseudo_ref.shape
    tiles = span // LANES
    for k in range(5):
        grid[k, ROWS : ROWS + edge, LANES : LANES + span] = part_ref[k]
    for k in range(5):
        for side, row, beyond in ((0, ROWS, ROWS - 1), (1, ROWS + edge - 1, ROWS + edge)):
            at = (k, slice(row, row + 1), slice(LANES, LANES + span))
            grid[at] = grid[at] + res_ref[side, k : k + 1, :]
            grid[k, beyond : beyond + 1, LANES : LANES + span] = res_ref[side, 5 + k : 6 + k, :]

    def body(top, offset):
        lanes = pl.ds(offset, LANES)
        face_tiles = [face_ref[d, pl.ds(top, 2 * ROWS), lanes].astype(F32) for d in range(6)]
        tables = [[], [], [], []]
        for i_half in range(2):
            rows = pl.ds(top + i_half * ROWS, ROWS)
            vel, speed_sq, pressure, enthalpy, reach, faces, rhs = tile_coefficients(
                i_half, rows, lanes, state_ref, face_tiles, pseudo_ref, rhs_ref
            )
            out = sweep_tile(
                grid, ROWS + top + i_half * ROWS, pl.multiple_of(LANES + offset, LANES), edge,
                vel, speed_sq, enthalpy, reach, faces, rhs,
            )
            for k in range(5):
                field[k, rows, pl.ds(pl.multiple_of(offset - LANES, LANES), LANES)] = out[k]
            for k in range(4):
                tables[k].append(pressure * out[1 + k])
        chunk = (offset - LANES) // (2 * LANES)
        wide = pl.ds(pl.multiple_of(lax.rem(offset - LANES, 2 * LANES), LANES), LANES)
        for k in range(4):
            big, small = split(jnp.concatenate(tables[k], axis=0))
            at = pl.ds(pl.multiple_of(k * (high.shape[0] // 4) + chunk * edge + top, 2 * ROWS), 2 * ROWS)
            high[at, wide] = big
            low[at, wide] = small

    for_each_tile(edge, 1, tiles - 1, body)
    store = pltpu.make_async_copy(field, out_ref.at[:, :, pl.ds(LANES, span - 2 * LANES)], sem)
    store.start()
    x, chunk = chunk_of(cell_ref[...], span)
    row = jnp.where(chunk > 0, (chunk - 1) * edge + x, -1)
    for k, value in enumerate(gather(high, low, column_ref, row)):
        gathered_ref[k : k + 1, :] = value
    store.wait()


def add_up(value_ref, shape_ref, vertex_ref, vertex_hot_ref, out_ref, parity, capacity):
    slots = value_ref.shape[1]
    group = max(capacity, LANES)
    together = group // capacity
    vertex_rows = -(-together * PARTS // 16) * 16
    chunk = lax.broadcasted_iota(jnp.int32, (1, group), 1) // capacity
    if together == 1:
        groups = [pl.multiple_of((s + parity) * group, group) for s in range(0, slots // group, 2)]
    else:
        groups = [s * group for s in range(slots // group)]
    for s, start in enumerate(groups):
        lanes = pl.ds(start, group)
        shape = [shape_ref[k : k + 1, lanes] for k in range(21)]
        values = [value_ref[k : k + 1, lanes] for k in range(4)]
        terms = tet_terms(values[3], values[:3], shape)
        left, right = [], []
        for c in range(4):
            row = vertex_ref[c : c + 1, lanes] // LANES + chunk * PARTS
            match = lax.broadcasted_iota(jnp.int16, (vertex_rows, group), 0) == row.astype(jnp.int16)
            blocks = []
            for k in range(3):
                blocks += [jnp.where(match, v, jnp.zeros((), BF16)) for v in split(terms[c][k])]
            left.append(jnp.concatenate(blocks, axis=0))
            right.append(vertex_hot_ref[c, :, lanes])
        product = lax.dot_general(
            jnp.concatenate(left, axis=1), jnp.concatenate(right, axis=1),
            (((1,), (1,)), ((), ())), preferred_element_type=F32,
        )
        for k in range(3):
            big = product[2 * k * vertex_rows : (2 * k + 1) * vertex_rows]
            small = product[(2 * k + 1) * vertex_rows : (2 * k + 2) * vertex_rows]
            total = big + small
            rows = slice(k * PARTS, (k + 1) * PARTS)
            if together == 1:
                out_ref[s, rows, :] = total[:PARTS]
            for q in range(0, together - 1, 2):
                pair = [total[(q + i) * PARTS : (q + i + 1) * PARTS] for i in range(2)]
                out_ref[(s * together + q) // 2, rows, :] = jnp.where(parity == 0, *pair)


def keep_kernel(value_ref, shape_ref, vertex_ref, vertex_hot_ref, keep_ref):
    capacity = value_ref.shape[1] // (2 * keep_ref.shape[0])
    parity = 1 - lax.rem(lax.axis_index("blk"), 2)
    add_up(value_ref, shape_ref, vertex_ref, vertex_hot_ref, keep_ref, parity, capacity)


def third_kernel(
    part_ref, rhs_ref, state_ref, face_ref, pseudo_ref, res_ref, ra_ref, rb_ref,
    ya_ref, yb_ref, sa_ref, sb_ref, gathered_ref, column_ref, cell_ref, vertex_ref, vertex_hot_ref, shape_ref,
    field, value_ref, send_ref,
    grids, high, low,
):
    edge, span = pseudo_ref.shape
    per = LANES // edge
    owners = 2 * send_ref.shape[0]
    slots = cell_ref.shape[1]
    capacity = slots // owners
    even = is_even("grp")
    even_y = is_even("blk")
    lane = lax.broadcasted_iota(jnp.int32, (edge, LANES), 1)
    lane_row = lax.broadcasted_iota(jnp.int32, (1, LANES), 1)
    rows = slice(ROWS, ROWS + edge)

    def pick(a_ref, b_ref, flag, k):
        g, q = divmod(k, per)
        value = jnp.where(flag, a_ref[g], b_ref[g])
        return pltpu.roll(value, LANES - q * edge, 1) if q else value

    for side in (0, 1):
        grid = grids.at[side]
        start = 0 if side == 0 else span - 2 * LANES
        lanes = slice(start, start + 2 * LANES)
        base = LANES if side == 0 else 0
        into = slice(base, base + 2 * LANES)
        for k in range(5):
            grid[k, rows, into] = part_ref[k, :, lanes]
            for xs, row, beyond in ((0, ROWS, ROWS - 1), (1, ROWS + edge - 1, ROWS + edge)):
                at = (k, slice(row, row + 1), into)
                grid[at] = grid[at] + res_ref[xs, k : k + 1, lanes]
                grid[k, beyond : beyond + 1, into] = res_ref[xs, 5 + k : 6 + k, lanes]
        flag = even_y if side == 1 else jnp.logical_not(even_y)
        own = [pick(ya_ref, yb_ref, flag, k) for k in range(15)]
        other = [pick(sa_ref, sb_ref, flag, k) for k in range(16)]
        added, finished = meet(1, side, own, other[:15])
        beyond = 0 if side == 0 else 2 * LANES
        for k in range(5):
            if side == 0:
                extra = jnp.where(lane < edge, added[k], 0.0)
                halo = pltpu.roll(finished[k], LANES - edge, 1)
            else:
                extra = jnp.where(lane >= LANES - edge, pltpu.roll(added[k], LANES - edge, 1), 0.0)
                halo = finished[k]
            at = (k, rows, slice(LANES, 2 * LANES))
            grid[at] = grid[at] + extra
            grid[k, rows, beyond : beyond + LANES] = halo
        start = 0 if side == 0 else span - LANES
        for xs, row in ((0, ROWS - 1), (1, ROWS + edge)):
            flag_x = even if xs == 1 else jnp.logical_not(even)
            lanes = slice(start, start + LANES)
            state = [jnp.where(flag_x, ra_ref[k : k + 1, lanes], rb_ref[k : k + 1, lanes]) for k in range(11, 16)]
            corner = [other[15][2 * k + xs : 2 * k + xs + 1, :] for k in range(5)]
            if side == 1:
                corner = [pltpu.roll(v, LANES - edge, 1) for v in corner]
            extra = one_sided(state[:3], state[3], 1, 1.0 if side == 1 else -1.0, corner)
            inside = lane_row < edge if side == 0 else lane_row >= LANES - edge
            for k in range(5):
                at = (k, slice(row, row + 1), slice(LANES, 2 * LANES))
                grid[at] = grid[at] + jnp.where(inside, state[4] * extra[k], 0.0)

        lanes = pl.ds(start, LANES)
        wide = slice(LANES, 2 * LANES) if side == 0 else slice(0, LANES)
        for top in range(0, edge, 2 * ROWS):
            face_tiles = [face_ref[d, pl.ds(top, 2 * ROWS), lanes].astype(F32) for d in range(6)]
            tables = [[], [], [], []]
            for i_half in range(2):
                here = pl.ds(top + i_half * ROWS, ROWS)
                vel, speed_sq, pressure, enthalpy, reach, faces, rhs = tile_coefficients(
                    i_half, here, lanes, state_ref, face_tiles, pseudo_ref, rhs_ref
                )
                out = sweep_tile(
                    grid, ROWS + top + i_half * ROWS, LANES, edge, vel, speed_sq, enthalpy, reach, faces, rhs
                )
                for k in range(5):
                    field[side, k, here, :] = out[k]
                for k in range(4):
                    tables[k].append(pressure * out[1 + k])
            for k in range(4):
                big, small = split(jnp.concatenate(tables[k], axis=0))
                at = slice(k * edge + top, k * edge + top + 2 * ROWS)
                high[at, wide] = big
                low[at, wide] = small

    x, number = chunk_of(cell_ref[...], span)
    gathered = gather(high, low, column_ref, jnp.where(number == 0, x, -1))
    gathered = [gathered_ref[k : k + 1, :] + v for k, v in enumerate(gathered)]

    for k in range(4):
        value_ref[k : k + 1, :] = gathered[k]
    add_up(value_ref, shape_ref, vertex_ref, vertex_hot_ref, send_ref, lax.rem(lax.axis_index("blk"), 2), capacity)


def store_kernel(adjoint_ref, field_ref, after_ref, out_ref, sem):
    span = out_ref.shape[2]
    copies = [
        pltpu.make_async_copy(field_ref.at[side], out_ref.at[:, :, pl.ds(start, LANES)], sem.at[side])
        for side, start in ((0, 0), (1, span - LANES))
    ]
    for copy in copies:
        copy.start()
    for copy in copies:
        copy.wait()


def fourth_kernel(keep_ref, got_ref, *refs):
    count = keep_ref.shape[0]
    me = lax.rem(lax.axis_index("blk") // 2, count)
    for k, ref in enumerate(refs):
        partner = lax.bitwise_xor(me, k)
        ref[...] = keep_ref[partner] + got_ref[partner]


def last_kernel(*refs):
    total = refs[0][...]
    for ref in refs[1:-1]:
        total = total + ref[...]
    for k in range(3):
        for part in range(PARTS):
            at = k * PARTS + part
            refs[-1][k : k + 1, part * LANES : (part + 1) * LANES] = total[at : at + 1, :]


def swap(value, axis, pairs):
    return lax.ppermute(value, axis, pairs + [(b, a) for a, b in pairs])


def neighbours(value_a, value_b, axis):
    count = lax.axis_size(axis)
    first = [(i, i + 1) for i in range(0, count - 1, 2)]
    second = [(i, i + 1) for i in range(1, count - 1, 2)]
    return swap(value_a, axis, first), swap(value_b, axis, second)


def local(
    adjoint_init, adjoint_rhs, flow_state, face_weights, pseudo_time,
    tet_coords, tet_weights, tet_cell, tet_vertex, tet_count,
):
    edge, span = pseudo_time.shape
    owners = tet_count.shape[1]
    blocks = lax.axis_size("blk")
    padded = (5, edge + 2 * ROWS, span + 2 * LANES)
    struct = jax.ShapeDtypeStruct
    packed = (16 * edge // LANES, edge, LANES)
    slots = tet_cell.shape[0]
    cell = tet_cell.reshape(1, slots)
    message = struct((16, span), F32)
    fields = (adjoint_init, adjoint_rhs, flow_state, face_weights, pseudo_time)
    arrays = (*fields, jnp.transpose(tet_coords, (1, 0, 2)), tet_weights, cell, tet_vertex)
    xa, xb, *arrays = call(
        plane_kernel,
        [message] * 2 + [struct(v.shape, v.dtype) for v in arrays],
        [HBM] * 9,
        [VMEM] * 11,
        [pltpu.VMEM((2, 16, span), F32), pltpu.SemaphoreType.DMA((17,))],
        "plane_messages",
    )(*(pltpu.with_memory_space_constraint(v, pltpu.HBM) for v in arrays))
    fields, (coords, weights, cell, vertex) = arrays[:5], arrays[5:]
    ra, rb = neighbours(xa, xb, "grp")
    part, ylo, yhi, column, vertex_hot, shapes = call(
        first_kernel,
        [struct((5, edge, span), F32), struct(packed, F32), struct(packed, F32), struct((2 * LANES, slots), BF16),
         struct((4, LANES, slots), BF16), struct((24, slots), F32)],
        [VMEM] * 9 + [SMEM],
        [VMEM] * 6,
        [pltpu.VMEM(padded, F32), pltpu.VMEM((6, edge, span), F32)],
        "partial_sweep",
        flops=12_000_000,
    )(*fields, coords, weights, cell, vertex, tet_count)
    res, ya, yb = call(
        second_kernel,
        [struct((2, 16, span), F32), struct(packed, F32), struct(packed, F32)],
        [VMEM] * 6,
        [VMEM] * 3,
        [pltpu.VMEM((2,) + packed, F32)],
        "streamwise_halo",
    )(xa, xb, ra, rb, ylo, yhi)
    sa, sb = neighbours(ya, yb, "blk")
    table = (4 * edge * (span // (2 * LANES) - 1), 2 * LANES)
    adjoint, gathered = call(
        middle_kernel,
        [struct((5, edge, span), F32), struct((4, slots), F32)],
        [VMEM] * 8,
        [HBM, VMEM],
        [pltpu.VMEM(padded, F32), pltpu.VMEM((5, edge, span - 2 * LANES), F32), pltpu.VMEM(table, BF16),
         pltpu.VMEM(table, BF16), pltpu.SemaphoreType.DMA],
        "middle_sweep",
        flops=12_000_000,
    )(part, *fields[1:], res, column, cell)
    half = owners // 2
    sums_shape = (half, 3 * PARTS, LANES)
    table = (4 * edge, 2 * LANES)
    ends, values, send = call(
        third_kernel,
        [struct((2, 5, edge, LANES), F32), struct((4, slots), F32), struct(sums_shape, F32)],
        [VMEM] * 18,
        [VMEM] * 3,
        [pltpu.VMEM((2, 5, edge + 2 * ROWS, 3 * LANES), F32), pltpu.VMEM(table, BF16), pltpu.VMEM(table, BF16)],
        "edge_sweep_and_sums",
        flops=12_000_000,
    )(
        part, *fields[1:], res, ra, rb, ya, yb, sa, sb,
        gathered, column, cell, vertex, vertex_hot, shapes,
    )
    got = swap(send, "blk", [(i, i + 1) for i in range(0, blocks, 2)])
    keep = call(
        keep_kernel, struct(sums_shape, F32), [VMEM] * 4, VMEM, [], "kept_sums", flops=3_000_000
    )(values, shapes, vertex, vertex_hot)
    place = lax.axis_index("blk") // 2
    while half > 4:
        half //= 2
        both = (keep + got).reshape(2, half, 3 * PARTS, LANES)
        bit = lax.rem(place // half, 2)
        keep = lax.dynamic_index_in_dim(both, bit, 0, keepdims=False)
        send = lax.dynamic_index_in_dim(both, 1 - bit, 0, keepdims=False)
        got = lax.ppermute(send, "blk", [(i, i ^ (2 * half)) for i in range(blocks)])
    one = struct((3 * PARTS, LANES), F32)
    parts = call(
        fourth_kernel, [one] * half, [VMEM] * 2, [VMEM] * half, [], "core_pair_sums"
    )(keep, got)
    adjoint = call(
        store_kernel, struct((5, edge, span), F32), [HBM, VMEM, VMEM], HBM, [pltpu.SemaphoreType.DMA((2,))],
        "store_field", flops=3_000_000, aliases={0: 0},
    )(adjoint, ends, parts[0])
    parts = [lax.ppermute(v, "blk", [(i, i ^ (2 * k + 1)) for i in range(blocks)]) for k, v in enumerate(parts)]
    sensitivity = call(last_kernel, struct((3, VERT_DEV), F32), [VMEM] * half, VMEM, [], "own_sums")(*parts)
    return adjoint, sensitivity


def solution(mesh):
    return jax.shard_map(
        local,
        mesh=mesh,
        in_specs=(
            P(None, "grp", "blk"),
            P(None, "grp", "blk"),
            P(None, "grp", "blk"),
            P(None, "grp", "blk"),
            P("grp", "blk"),
            P(None, None, ("grp", "blk")),
            P(None, ("grp", "blk")),
            P(("grp", "blk")),
            P(None, ("grp", "blk")),
            P(("grp", "blk"), None),
        ),
        out_specs=(P(None, "grp", "blk"), P(None, ("grp", "blk"))),
        check_vma=False,
    )
```

```python
import functools
import jax
import jax.numpy as jnp
from jax import lax
from jax.experimental import pallas as pl
from jax.experimental.pallas import tpu as pltpu
from jax.sharding import PartitionSpec as P

VERT_DEV = 1536
GAMMA = 1.4
LANES = 128
ROWS = 8
PARTS = VERT_DEV // LANES
F32 = jnp.float32
BF16 = jnp.bfloat16
VMEM = pl.BlockSpec(memory_space=pltpu.VMEM)
HBM = pl.BlockSpec(memory_space=pltpu.HBM)
LIMIT = 40 * 1024 * 1024


def call(kernel, outs, in_specs, out_specs, scratch, name, flops=1000, aliases={}):
    return pl.pallas_call(
        kernel,
        out_shape=outs,
        in_specs=in_specs,
        out_specs=out_specs,
        scratch_shapes=scratch,
        compiler_params=pltpu.CompilerParams(vmem_limit_bytes=LIMIT),
        cost_estimate=pl.CostEstimate(flops=flops, bytes_accessed=flops // 4, transcendentals=0),
        input_output_aliases=aliases,
        name=name,
    )


def is_even(axis):
    return lax.rem(lax.axis_index(axis), 2) == 0


def reach_of(speed_sq, enthalpy):
    sound_sq = (GAMMA - 1.0) * (enthalpy - 0.5 * speed_sq)
    return jnp.sqrt(speed_sq) + jnp.sqrt(sound_sq)


def transposed(vel, enthalpy, half_sq, axis_id, field):
    normal = vel[axis_id]
    energy = normal * field[4]
    common = vel[0] * field[1] + vel[1] * field[2] + vel[2] * field[3] + enthalpy * field[4]
    along = field[1 + axis_id] + energy
    scaled = (GAMMA - 1.0) * along
    out = [half_sq * along - normal * common]
    for j in range(3):
        entry = normal * field[1 + j] - vel[j] * scaled
        if j == axis_id:
            entry = entry + (field[0] + common)
        out.append(entry)
    out.append(scaled + energy)
    return out


def one_sided(vel, enthalpy, axis_id, sign, field):
    speed_sq = vel[0] * vel[0] + vel[1] * vel[1] + vel[2] * vel[2]
    reach = reach_of(speed_sq, enthalpy)
    turned = transposed(vel, enthalpy, 0.5 * (GAMMA - 1.0) * speed_sq, axis_id, field)
    return [sign * turned[k] + reach * field[k] for k in range(5)]


def cell_state(state):
    density, m1, m2, m3, energy = state
    inverse = 1.0 / density
    vel = [m1 * inverse, m2 * inverse, m3 * inverse]
    speed_sq = vel[0] * vel[0] + vel[1] * vel[1] + vel[2] * vel[2]
    pressure = (GAMMA - 1.0) * (energy - 0.5 * density * speed_sq)
    enthalpy = (energy + pressure) * inverse
    reach = jnp.sqrt(speed_sq) + jnp.sqrt(GAMMA * pressure * inverse)
    return vel, speed_sq, pressure, enthalpy, reach


def combine(rhs, reach, vel, speed_sq, enthalpy, faces, pairs):
    spread = None
    scaled = None
    for axis_id, (upper, lower) in enumerate(pairs):
        upper = [faces[2 * axis_id] * v for v in upper]
        lower = [faces[2 * axis_id + 1] * v for v in lower]
        both = [u + v for u, v in zip(upper, lower)]
        field = [u - v for u, v in zip(upper, lower)]
        spread = both if spread is None else [u + v for u, v in zip(spread, both)]
        normal = vel[axis_id]
        energy = normal * field[4]
        common = vel[0] * field[1] + vel[1] * field[2] + vel[2] * field[3] + enthalpy * field[4]
        along = field[1 + axis_id] + energy
        parts = [normal * common] + [normal * field[1 + j] for j in range(3)] + [energy]
        parts[1 + axis_id] = parts[1 + axis_id] + (field[0] + common)
        if scaled is None:
            scaled, total = along, parts
        else:
            scaled = scaled + along
            total = [u + v for u, v in zip(total, parts)]
    scaled = (GAMMA - 1.0) * scaled
    turned = [0.5 * speed_sq * scaled - total[0]]
    turned += [total[1 + j] - vel[j] * scaled for j in range(3)]
    turned.append(scaled + total[4])
    return [rhs[k] + turned[k] + reach * spread[k] for k in range(5)]


def inside_faces(faces, edge, shape):
    depth = lax.rem(lax.broadcasted_iota(jnp.int32, shape, 1), edge)
    faces = list(faces)
    faces[4] = jnp.where(depth == edge - 1, 0.0, faces[4])
    faces[5] = jnp.where(depth == 0, 0.0, faces[5])
    return faces


def lane_pairs(here, after, before, edge, shape):
    place = lax.broadcasted_iota(jnp.int32, shape, 1)
    first = place < edge
    last = place >= LANES - edge
    along_y = (
        [pltpu.roll(jnp.where(first, a, h), LANES - edge, 1) for h, a in zip(here, after)],
        [pltpu.roll(jnp.where(last, b, h), edge, 1) for h, b in zip(here, before)],
    )
    along_z = ([pltpu.roll(h, LANES - 1, 1) for h in here], [pltpu.roll(h, 1, 1) for h in here])
    return along_y, along_z


def sweep_tile(grid, row, lane, edge, vel, speed_sq, enthalpy, reach, faces, rhs):
    def at(drow, dlane):
        return [grid[k, pl.ds(row + drow, ROWS), pl.ds(lane + dlane, LANES)] for k in range(5)]

    shape = (ROWS, LANES)
    pairs = lane_pairs(at(0, 0), at(0, LANES), at(0, -LANES), edge, shape)
    return combine(
        rhs, reach, vel, speed_sq, enthalpy, inside_faces(faces, edge, shape), ((at(1, 0), at(-1, 0)),) + pairs
    )


def coefficients(state, faces, pseudo, rhs):
    vel, speed_sq, pressure, enthalpy, reach = cell_state(state)
    area = faces[0]
    for f in faces[1:]:
        area = area + f
    inverse = 1.0 / (pseudo + 0.5 * reach * area)
    half = 0.5 * inverse
    return vel, speed_sq, pressure, enthalpy, reach, [half * f for f in faces], [inverse * v for v in rhs]


def tile_coefficients(i_half, rows, lanes, state_ref, face_tiles, pseudo_ref, rhs_ref):
    return coefficients(
        [state_ref[k, rows, lanes] for k in range(5)],
        [f[i_half * ROWS : (i_half + 1) * ROWS] for f in face_tiles],
        pseudo_ref[rows, lanes],
        [rhs_ref[k, rows, lanes] for k in range(5)],
    )


def clear_pads(grid, edge, span):
    high = grid.shape[1]
    wide = grid.shape[2]
    for k in range(5):
        grid[k, 0:ROWS, :] = jnp.zeros((ROWS, wide), F32)
        grid[k, ROWS + edge : high, :] = jnp.zeros((high - ROWS - edge, wide), F32)
        grid[k, ROWS : ROWS + edge, 0:LANES] = jnp.zeros((edge, LANES), F32)
        grid[k, ROWS : ROWS + edge, LANES + span : wide] = jnp.zeros((edge, LANES), F32)


def for_each_tile(edge, first, last, body):
    for top in range(0, edge, 2 * ROWS):

        def step(j, carry, top=top):
            body(top, pl.multiple_of(j * LANES, LANES))
            return carry

        lax.fori_loop(first, last, step, 0, unroll=True)


def plane_kernel(
    adjoint_hbm, rhs_hbm, state_hbm, face_hbm, pseudo_hbm, coord_hbm, weight_hbm, cell_hbm, vertex_hbm,
    count_hbm,
    xa_ref, xb_ref, adjoint_ref, rhs_ref, state_ref, face_ref, pseudo_ref, coord_ref, weight_ref, cell_ref,
    vertex_ref, count_ref,
    xsides, sem,
):
    edge, span = pseudo_hbm.shape
    early, late = [], []

    def move(into, source, target):
        into.append(pltpu.make_async_copy(source, target, sem.at[len(early) + len(late)]))
        into[-1].start()

    fields = (
        (state_hbm, state_ref), (adjoint_hbm, adjoint_ref), (rhs_hbm, rhs_ref), (pseudo_hbm, pseudo_ref)
    )

    def rows_of(ref, first, count):
        return ref.at[(slice(None),) * (len(ref.shape) - 2) + (pl.ds(first, count),)]

    move(early, face_hbm, face_ref)
    for source, target in fields:
        for first in (0, edge - ROWS):
            move(early, rows_of(source, first, ROWS), rows_of(target, first, ROWS))
    for source, target in fields:
        move(late, rows_of(source, ROWS, edge - 2 * ROWS), rows_of(target, ROWS, edge - 2 * ROWS))
    for source, target in (
        (coord_hbm, coord_ref), (weight_hbm, weight_ref), (cell_hbm, cell_ref), (vertex_hbm, vertex_ref),
        (count_hbm, count_ref),
    ):
        move(late, source, target)
    for copy in early:
        copy.wait()
    even = is_even("grp")
    shape = (2, LANES)
    upper_row = lax.broadcasted_iota(jnp.int32, shape, 0) == 1
    sub = lax.broadcasted_iota(jnp.int32, (ROWS, LANES), 0)
    place = lax.broadcasted_iota(jnp.int32, shape, 1)
    tiles = span // LANES
    zero = jnp.zeros(shape, F32)

    def planes(ref, k, j, inner=0):
        at = (k,) if k is not None else ()
        lanes = slice(j * LANES, (j + 1) * LANES)
        last = edge - 2 - inner
        return jnp.where(upper_row, ref[at + (slice(last, last + 2), lanes)], ref[at + (slice(inner, inner + 2), lanes)])

    for j in range(tiles):
        lanes = pl.ds(j * LANES, LANES)
        faces = []
        for d in range(6):
            low = face_ref[d, pl.ds(0, 2 * ROWS), lanes].astype(F32)[:ROWS]
            high = face_ref[d, pl.ds(edge - 2 * ROWS, 2 * ROWS), lanes].astype(F32)[ROWS:]
            faces.append(jnp.where(sub == 0, low, pltpu.roll(high, 2, 0))[:2])
        vel, speed_sq, pressure, enthalpy, reach, faces, rhs = coefficients(
            [planes(state_ref, k, j) for k in range(5)],
            faces,
            planes(pseudo_ref, None, j),
            [planes(rhs_ref, k, j) for k in range(5)],
        )
        here = [planes(adjoint_ref, k, j) for k in range(5)]
        after = [planes(adjoint_ref, k, j + 1) if j + 1 < tiles else zero for k in range(5)]
        before = [planes(adjoint_ref, k, j - 1) if j > 0 else zero for k in range(5)]
        inner = [planes(adjoint_ref, k, j, 1) for k in range(5)]
        along_x = ([jnp.where(upper_row, 0.0, v) for v in inner], [jnp.where(upper_row, v, 0.0) for v in inner])
        pairs = lane_pairs(here, after, before, edge, shape)
        out = combine(
            rhs, reach, vel, speed_sq, enthalpy, inside_faces(faces, edge, shape), (along_x,) + pairs
        )
        message = out + here + [jnp.where(upper_row, faces[0], faces[1])] + vel + [enthalpy]
        message.append(jnp.where(place < edge, faces[3], faces[2]) if j == 0 else faces[2])
        for side in (0, 1):
            slot = jnp.where(even, 1 - side, side)
            for k, value in enumerate(message):
                xsides[slot, k : k + 1, lanes] = value[side : side + 1]
    xa_ref[...] = xsides[0]
    xb_ref[...] = xsides[1]
    for copy in late:
        copy.wait()


def first_kernel(
    adjoint_ref, rhs_ref, state_ref, face_ref, pseudo_ref, coord_ref, weight_ref, cell_ref, vertex_ref, count_ref,
    part_ref, ylo_ref, yhi_ref, column_ref, vertex_hot_ref, shape_ref,
    grid, coef,
):
    edge, span = pseudo_ref.shape
    clear_pads(grid, edge, span)
    for k in range(5):
        grid[k, ROWS : ROWS + edge, LANES : LANES + span] = adjoint_ref[k]

    def body(top, offset):
        lanes = pl.ds(offset, LANES)
        face_tiles = [face_ref[d, pl.ds(top, 2 * ROWS), lanes].astype(F32) for d in range(6)]
        for i_half in range(2):
            rows = pl.ds(top + i_half * ROWS, ROWS)
            vel, speed_sq, pressure, enthalpy, reach, faces, rhs = tile_coefficients(
                i_half, rows, lanes, state_ref, face_tiles, pseudo_ref, rhs_ref
            )
            out = sweep_tile(
                grid, ROWS + top + i_half * ROWS, pl.multiple_of(LANES + offset, LANES), edge,
                vel, speed_sq, enthalpy, reach, faces, rhs,
            )
            for k in range(5):
                part_ref[k, rows, lanes] = out[k]
            for k, value in enumerate(vel + [enthalpy] + faces[2:4]):
                coef[k, rows, lanes] = value

    for_each_tile(edge, 0, span // LANES, body)

    lane = lax.broadcasted_iota(jnp.int32, (edge, LANES), 1)
    quarter = lane // edge
    for side, base, ref in ((0, 0, ylo_ref), (1, span - LANES, yhi_ref)):
        lanes = slice(base, base + LANES)
        fields = [part_ref[k, :, lanes] for k in range(5)]
        fields += [grid[k, ROWS : ROWS + edge, LANES + base : LANES + base + LANES] for k in range(5)]
        fields += [coef[4 + 1 - side, :, lanes]]
        fields += [coef[k, :, lanes] for k in range(4)]
        start = 0 if side == 0 else LANES - edge
        per = LANES // edge
        for g in range(4):
            packed = None
            for q in range(per):
                k = g * per + q
                if k >= len(fields):
                    value = jnp.zeros((edge, LANES), F32)
                else:
                    shift = (q * edge - start) % LANES
                    value = pltpu.roll(fields[k], shift, 1) if shift else fields[k]
                packed = value if packed is None else jnp.where(quarter == q, value, packed)
            ref[g] = packed

    owners = count_ref.shape[1]
    slots = weight_ref.shape[1]
    capacity = slots // owners
    width = 2 * LANES
    step = min(slots, 512)
    for s in range(0, slots, step):
        part = slice(s, s + step)
        column = lax.rem(cell_ref[:, part] + LANES, width)
        column_ref[:, part] = hot((width, step), column)
        for c in range(4):
            vertex_hot_ref[c, :, part] = hot((LANES, step), lax.rem(vertex_ref[c : c + 1, part], LANES))

    group = max(capacity, LANES)
    together = group // capacity
    lane_group = lax.broadcasted_iota(jnp.int32, (1, group), 1)
    chunk = lane_group // capacity
    within = lax.rem(lane_group, capacity)
    for s in range(0, slots // group):
        lanes = slice(s * group, (s + 1) * group)
        first = s * together
        count = jnp.broadcast_to(count_ref[:, first : first + 1], (1, group))
        for q in range(1, together):
            count = jnp.where(chunk == q, count_ref[:, first + q : first + q + 1], count)
        live = jnp.where(within < count, 1.0, 0.0)
        weights = [weight_ref[c : c + 1, lanes] * live for c in range(4)]
        corner = [[coord_ref[k, c : c + 1, lanes] for k in range(3)] for c in range(4)]
        for k, value in enumerate(tet_shapes(corner, weights)):
            shape_ref[k : k + 1, lanes] = value


def meet(axis_id, side, own, other):
    sign = 1.0 if side == 1 else -1.0
    mine = one_sided(own[11:14], own[14], axis_id, sign, other[5:10])
    theirs = one_sided(other[11:14], other[14], axis_id, -sign, own[5:10])
    added = [own[10] * v for v in mine]
    finished = [other[k] + other[10] * theirs[k] for k in range(5)]
    return added, finished


def second_kernel(xa_ref, xb_ref, ra_ref, rb_ref, ylo_ref, yhi_ref, res_ref, ya_ref, yb_ref, ysides):
    span = xa_ref.shape[1]
    edge = ylo_ref.shape[1]
    per = LANES // edge
    even = is_even("grp")
    even_y = is_even("blk")
    ysides[0] = ylo_ref[...]
    ysides[1] = yhi_ref[...]
    lane = lax.broadcasted_iota(jnp.int32, (1, LANES), 1)
    quarter = lane // edge

    def pick(a_ref, b_ref, flag):
        return [jnp.where(flag, a_ref[k : k + 1, :], b_ref[k : k + 1, :]) for k in range(15)]

    for side in (0, 1):
        flag = even if side == 1 else jnp.logical_not(even)
        own = pick(xa_ref, xb_ref, flag)
        other = pick(ra_ref, rb_ref, flag)
        added, finished = meet(0, side, own, other)
        row = 0 if side == 0 else edge - 1
        for k in range(5):
            res_ref[side, k : k + 1, :] = added[k]
            res_ref[side, 5 + k : 6 + k, :] = finished[k]
        for ys, base, start in ((0, 0, 0), (1, span - LANES, LANES - edge)):
            for k in range(5):
                g, q = divmod(k, per)
                shift = (q * edge - start) % LANES
                piece = added[k][:, base : base + LANES]
                piece = pltpu.roll(piece, shift, 1) if shift else piece
                old = ysides[ys, g, row : row + 1, :]
                ysides[ys, g, row : row + 1, :] = old + jnp.where(quarter == q, piece, 0.0)
                g, q = divmod(15, per)
                shift = (q * edge - start) % LANES
                piece = other[5 + k][:, base : base + LANES]
                piece = pltpu.roll(piece, shift, 1) if shift else piece
                at = 2 * k + side
                old = ysides[ys, g, at : at + 1, :]
                ysides[ys, g, at : at + 1, :] = jnp.where(quarter == q, piece, old)
    ya_ref[...] = ysides[jnp.where(even_y, 1, 0)]
    yb_ref[...] = ysides[jnp.where(even_y, 0, 1)]


def cross(left, right):
    return [
        left[1] * right[2] - left[2] * right[1],
        left[2] * right[0] - left[0] * right[2],
        left[0] * right[1] - left[1] * right[0],
    ]


def minus(left, right):
    return [u - v for u, v in zip(left, right)]


def tet_shapes(corner, weights):
    edge_one = minus(corner[1], corner[0])
    edge_two = minus(corner[2], corner[0])
    edge_three = minus(corner[3], corner[0])
    g1 = cross(edge_two, edge_three)
    g2 = cross(edge_three, edge_one)
    g3 = cross(edge_one, edge_two)
    g0 = [-(u + v + w) for u, v, w in zip(g1, g2, g3)]
    sixth = [w * (1.0 / 6.0) for w in weights]
    half = [w * 0.5 for w in weights]
    out = []
    for c, g in enumerate((g0, g1, g2, g3)):
        out += [sixth[c] * v for v in g]
    out += [half[1] * v for v in minus(corner[2], corner[3])]
    out += [half[2] * v for v in minus(corner[3], corner[1])]
    out += [half[3] * v for v in minus(corner[1], corner[2])]
    return out


def tet_terms(volume, face, shape):
    terms = []
    for c in range(4):
        term = [volume * shape[3 * c + k] for k in range(3)]
        if c:
            turned = cross(shape[9 + 3 * c : 12 + 3 * c], face)
            term = [u + v for u, v in zip(term, turned)]
        terms.append(term)
    return terms


def split(value):
    high = value.astype(BF16)
    return high, (value - high.astype(F32)).astype(BF16)


def hot(shape, index):
    rows = lax.broadcasted_iota(jnp.int16, shape, 0)
    return jnp.where(rows == index.astype(jnp.int16), jnp.ones((), BF16), jnp.zeros((), BF16))


def gather(high, low, column_ref, row):
    table_rows = high.shape[0] // 4
    slots = column_ref.shape[1]
    step = min(slots, 512)
    gathered = [[], [], [], []]
    for s in range(0, slots, step):
        column = column_ref[:, s : s + step]
        product = jnp.dot(high[...], column, preferred_element_type=F32)
        product = product + jnp.dot(low[...], column, preferred_element_type=F32)
        here = lax.broadcasted_iota(jnp.int32, (table_rows, step), 0) == row[:, s : s + step]
        for k in range(4):
            piece = product[k * table_rows : (k + 1) * table_rows]
            gathered[k].append(jnp.sum(jnp.where(here, piece, 0.0), axis=0, keepdims=True))
    return [jnp.concatenate(v, axis=1) for v in gathered]


def chunk_of(cell, span):
    yz = lax.rem(cell, span) + LANES
    return cell // span, lax.rem(yz // (2 * LANES), span // (2 * LANES))


def middle_kernel(
    part_ref, rhs_ref, state_ref, face_ref, pseudo_ref, res_ref, column_ref, cell_ref,
    out_ref, gathered_ref,
    grid, field, high, low, sem,
):
    edge, span = pseudo_ref.shape
    tiles = span // LANES
    for k in range(5):
        grid[k, ROWS : ROWS + edge, LANES : LANES + span] = part_ref[k]
    for k in range(5):
        for side, row, beyond in ((0, ROWS, ROWS - 1), (1, ROWS + edge - 1, ROWS + edge)):
            at = (k, slice(row, row + 1), slice(LANES, LANES + span))
            grid[at] = grid[at] + res_ref[side, k : k + 1, :]
            grid[k, beyond : beyond + 1, LANES : LANES + span] = res_ref[side, 5 + k : 6 + k, :]

    def body(top, offset):
        lanes = pl.ds(offset, LANES)
        face_tiles = [face_ref[d, pl.ds(top, 2 * ROWS), lanes].astype(F32) for d in range(6)]
        tables = [[], [], [], []]
        for i_half in range(2):
            rows = pl.ds(top + i_half * ROWS, ROWS)
            vel, speed_sq, pressure, enthalpy, reach, faces, rhs = tile_coefficients(
                i_half, rows, lanes, state_ref, face_tiles, pseudo_ref, rhs_ref
            )
            out = sweep_tile(
                grid, ROWS + top + i_half * ROWS, pl.multiple_of(LANES + offset, LANES), edge,
                vel, speed_sq, enthalpy, reach, faces, rhs,
            )
            for k in range(5):
                field[k, rows, pl.ds(pl.multiple_of(offset - LANES, LANES), LANES)] = out[k]
            for k in range(4):
                tables[k].append(pressure * out[1 + k])
        chunk = (offset - LANES) // (2 * LANES)
        wide = pl.ds(pl.multiple_of(lax.rem(offset - LANES, 2 * LANES), LANES), LANES)
        for k in range(4):
            big, small = split(jnp.concatenate(tables[k], axis=0))
            at = pl.ds(pl.multiple_of(k * (high.shape[0] // 4) + chunk * edge + top, 2 * ROWS), 2 * ROWS)
            high[at, wide] = big
            low[at, wide] = small

    for_each_tile(edge, 1, tiles - 1, body)
    store = pltpu.make_async_copy(field, out_ref.at[:, :, pl.ds(LANES, span - 2 * LANES)], sem)
    store.start()
    x, chunk = chunk_of(cell_ref[...], span)
    row = jnp.where(chunk > 0, (chunk - 1) * edge + x, -1)
    for k, value in enumerate(gather(high, low, column_ref, row)):
        gathered_ref[k : k + 1, :] = value
    store.wait()


def add_up(value_ref, shape_ref, vertex_ref, vertex_hot_ref, out_ref, parity, capacity):
    slots = value_ref.shape[1]
    group = max(capacity, LANES)
    together = group // capacity
    vertex_rows = -(-together * PARTS // 16) * 16
    chunk = lax.broadcasted_iota(jnp.int32, (1, group), 1) // capacity
    if together == 1:
        groups = [pl.multiple_of((s + parity) * group, group) for s in range(0, slots // group, 2)]
    else:
        groups = [s * group for s in range(slots // group)]
    for s, start in enumerate(groups):
        lanes = pl.ds(start, group)
        shape = [shape_ref[k : k + 1, lanes] for k in range(21)]
        values = [value_ref[k : k + 1, lanes] for k in range(4)]
        terms = tet_terms(values[3], values[:3], shape)
        left, right = [], []
        for c in range(4):
            row = vertex_ref[c : c + 1, lanes] // LANES + chunk * PARTS
            match = lax.broadcasted_iota(jnp.int16, (vertex_rows, group), 0) == row.astype(jnp.int16)
            blocks = []
            for k in range(3):
                blocks += [jnp.where(match, v, jnp.zeros((), BF16)) for v in split(terms[c][k])]
            left.append(jnp.concatenate(blocks, axis=0))
            right.append(vertex_hot_ref[c, :, lanes])
        product = lax.dot_general(
            jnp.concatenate(left, axis=1), jnp.concatenate(right, axis=1),
            (((1,), (1,)), ((), ())), preferred_element_type=F32,
        )
        for k in range(3):
            big = product[2 * k * vertex_rows : (2 * k + 1) * vertex_rows]
            small = product[(2 * k + 1) * vertex_rows : (2 * k + 2) * vertex_rows]
            total = big + small
            rows = slice(k * PARTS, (k + 1) * PARTS)
            if together == 1:
                out_ref[s, rows, :] = total[:PARTS]
            for q in range(0, together - 1, 2):
                pair = [total[(q + i) * PARTS : (q + i + 1) * PARTS] for i in range(2)]
                out_ref[(s * together + q) // 2, rows, :] = jnp.where(parity == 0, *pair)


def keep_kernel(value_ref, shape_ref, vertex_ref, vertex_hot_ref, keep_ref):
    capacity = value_ref.shape[1] // (2 * keep_ref.shape[0])
    parity = 1 - lax.rem(lax.axis_index("blk"), 2)
    add_up(value_ref, shape_ref, vertex_ref, vertex_hot_ref, keep_ref, parity, capacity)


def third_kernel(
    part_ref, rhs_ref, state_ref, face_ref, pseudo_ref, res_ref, ra_ref, rb_ref,
    ya_ref, yb_ref, sa_ref, sb_ref, gathered_ref, column_ref, cell_ref, vertex_ref, vertex_hot_ref, shape_ref,
    field, value_ref, send_ref,
    grids, high, low,
):
    edge, span = pseudo_ref.shape
    per = LANES // edge
    owners = 2 * send_ref.shape[0]
    slots = cell_ref.shape[1]
    capacity = slots // owners
    even = is_even("grp")
    even_y = is_even("blk")
    lane = lax.broadcasted_iota(jnp.int32, (edge, LANES), 1)
    lane_row = lax.broadcasted_iota(jnp.int32, (1, LANES), 1)
    rows = slice(ROWS, ROWS + edge)

    def pick(a_ref, b_ref, flag, k):
        g, q = divmod(k, per)
        value = jnp.where(flag, a_ref[g], b_ref[g])
        return pltpu.roll(value, LANES - q * edge, 1) if q else value

    for side in (0, 1):
        grid = grids.at[side]
        start = 0 if side == 0 else span - 2 * LANES
        lanes = slice(start, start + 2 * LANES)
        base = LANES if side == 0 else 0
        into = slice(base, base + 2 * LANES)
        for k in range(5):
            grid[k, rows, into] = part_ref[k, :, lanes]
            for xs, row, beyond in ((0, ROWS, ROWS - 1), (1, ROWS + edge - 1, ROWS + edge)):
                at = (k, slice(row, row + 1), into)
                grid[at] = grid[at] + res_ref[xs, k : k + 1, lanes]
                grid[k, beyond : beyond + 1, into] = res_ref[xs, 5 + k : 6 + k, lanes]
        flag = even_y if side == 1 else jnp.logical_not(even_y)
        own = [pick(ya_ref, yb_ref, flag, k) for k in range(15)]
        other = [pick(sa_ref, sb_ref, flag, k) for k in range(16)]
        added, finished = meet(1, side, own, other[:15])
        beyond = 0 if side == 0 else 2 * LANES
        for k in range(5):
            if side == 0:
                extra = jnp.where(lane < edge, added[k], 0.0)
                halo = pltpu.roll(finished[k], LANES - edge, 1)
            else:
                extra = jnp.where(lane >= LANES - edge, pltpu.roll(added[k], LANES - edge, 1), 0.0)
                halo = finished[k]
            at = (k, rows, slice(LANES, 2 * LANES))
            grid[at] = grid[at] + extra
            grid[k, rows, beyond : beyond + LANES] = halo
        start = 0 if side == 0 else span - LANES
        for xs, row in ((0, ROWS - 1), (1, ROWS + edge)):
            flag_x = even if xs == 1 else jnp.logical_not(even)
            lanes = slice(start, start + LANES)
            state = [jnp.where(flag_x, ra_ref[k : k + 1, lanes], rb_ref[k : k + 1, lanes]) for k in range(11, 16)]
            corner = [other[15][2 * k + xs : 2 * k + xs + 1, :] for k in range(5)]
            if side == 1:
                corner = [pltpu.roll(v, LANES - edge, 1) for v in corner]
            extra = one_sided(state[:3], state[3], 1, 1.0 if side == 1 else -1.0, corner)
            inside = lane_row < edge if side == 0 else lane_row >= LANES - edge
            for k in range(5):
                at = (k, slice(row, row + 1), slice(LANES, 2 * LANES))
                grid[at] = grid[at] + jnp.where(inside, state[4] * extra[k], 0.0)

        lanes = pl.ds(start, LANES)
        wide = slice(LANES, 2 * LANES) if side == 0 else slice(0, LANES)
        for top in range(0, edge, 2 * ROWS):
            face_tiles = [face_ref[d, pl.ds(top, 2 * ROWS), lanes].astype(F32) for d in range(6)]
            tables = [[], [], [], []]
            for i_half in range(2):
                here = pl.ds(top + i_half * ROWS, ROWS)
                vel, speed_sq, pressure, enthalpy, reach, faces, rhs = tile_coefficients(
                    i_half, here, lanes, state_ref, face_tiles, pseudo_ref, rhs_ref
                )
                out = sweep_tile(
                    grid, ROWS + top + i_half * ROWS, LANES, edge, vel, speed_sq, enthalpy, reach, faces, rhs
                )
                for k in range(5):
                    field[side, k, here, :] = out[k]
                for k in range(4):
                    tables[k].append(pressure * out[1 + k])
            for k in range(4):
                big, small = split(jnp.concatenate(tables[k], axis=0))
                at = slice(k * edge + top, k * edge + top + 2 * ROWS)
                high[at, wide] = big
                low[at, wide] = small

    x, number = chunk_of(cell_ref[...], span)
    gathered = gather(high, low, column_ref, jnp.where(number == 0, x, -1))
    gathered = [gathered_ref[k : k + 1, :] + v for k, v in enumerate(gathered)]

    for k in range(4):
        value_ref[k : k + 1, :] = gathered[k]
    add_up(value_ref, shape_ref, vertex_ref, vertex_hot_ref, send_ref, lax.rem(lax.axis_index("blk"), 2), capacity)


def store_kernel(adjoint_ref, field_ref, after_ref, out_ref, sem):
    span = out_ref.shape[2]
    copies = [
        pltpu.make_async_copy(field_ref.at[side], out_ref.at[:, :, pl.ds(start, LANES)], sem.at[side])
        for side, start in ((0, 0), (1, span - LANES))
    ]
    for copy in copies:
        copy.start()
    for copy in copies:
        copy.wait()


def fourth_kernel(keep_ref, got_ref, *refs):
    count = keep_ref.shape[0]
    me = lax.rem(lax.axis_index("blk") // 2, count)
    for k, ref in enumerate(refs):
        partner = lax.bitwise_xor(me, k)
        ref[...] = keep_ref[partner] + got_ref[partner]


def last_kernel(*refs):
    total = refs[0][...]
    for ref in refs[1:-1]:
        total = total + ref[...]
    for k in range(3):
        for part in range(PARTS):
            at = k * PARTS + part
            refs[-1][k : k + 1, part * LANES : (part + 1) * LANES] = total[at : at + 1, :]


def swap(value, axis, pairs):
    return lax.ppermute(value, axis, pairs + [(b, a) for a, b in pairs])


def neighbours(value_a, value_b, axis):
    count = lax.axis_size(axis)
    first = [(i, i + 1) for i in range(0, count - 1, 2)]
    second = [(i, i + 1) for i in range(1, count - 1, 2)]
    return swap(value_a, axis, first), swap(value_b, axis, second)


def local(
    adjoint_init, adjoint_rhs, flow_state, face_weights, pseudo_time,
    tet_coords, tet_weights, tet_cell, tet_vertex, tet_count,
):
    edge, span = pseudo_time.shape
    owners = tet_count.shape[1]
    blocks = lax.axis_size("blk")
    padded = (5, edge + 2 * ROWS, span + 2 * LANES)
    struct = jax.ShapeDtypeStruct
    packed = (16 * edge // LANES, edge, LANES)
    slots = tet_cell.shape[0]
    cell = tet_cell.reshape(1, slots)
    message = struct((16, span), F32)
    fields = (adjoint_init, adjoint_rhs, flow_state, face_weights, pseudo_time)
    arrays = (*fields, jnp.transpose(tet_coords, (1, 0, 2)), tet_weights, cell, tet_vertex, tet_count)
    xa, xb, *arrays = call(
        plane_kernel,
        [message] * 2 + [struct(v.shape, v.dtype) for v in arrays],
        [HBM] * 10,
        [VMEM] * 12,
        [pltpu.VMEM((2, 16, span), F32), pltpu.SemaphoreType.DMA((18,))],
        "plane_messages",
    )(*(pltpu.with_memory_space_constraint(v, pltpu.HBM) for v in arrays))
    fields, (coords, weights, cell, vertex, counts) = arrays[:5], arrays[5:]
    ra, rb = neighbours(xa, xb, "grp")
    part, ylo, yhi, column, vertex_hot, shapes = call(
        first_kernel,
        [struct((5, edge, span), F32), struct(packed, F32), struct(packed, F32), struct((2 * LANES, slots), BF16),
         struct((4, LANES, slots), BF16), struct((24, slots), F32)],
        [VMEM] * 10,
        [VMEM] * 6,
        [pltpu.VMEM(padded, F32), pltpu.VMEM((6, edge, span), F32)],
        "partial_sweep",
        flops=12_000_000,
    )(*fields, coords, weights, cell, vertex, counts)
    res, ya, yb = call(
        second_kernel,
        [struct((2, 16, span), F32), struct(packed, F32), struct(packed, F32)],
        [VMEM] * 6,
        [VMEM] * 3,
        [pltpu.VMEM((2,) + packed, F32)],
        "streamwise_halo",
    )(xa, xb, ra, rb, ylo, yhi)
    sa, sb = neighbours(ya, yb, "blk")
    table = (4 * edge * (span // (2 * LANES) - 1), 2 * LANES)
    adjoint, gathered = call(
        middle_kernel,
        [struct((5, edge, span), F32), struct((4, slots), F32)],
        [VMEM] * 8,
        [HBM, VMEM],
        [pltpu.VMEM(padded, F32), pltpu.VMEM((5, edge, span - 2 * LANES), F32), pltpu.VMEM(table, BF16),
         pltpu.VMEM(table, BF16), pltpu.SemaphoreType.DMA],
        "middle_sweep",
        flops=12_000_000,
    )(part, *fields[1:], res, column, cell)
    half = owners // 2
    sums_shape = (half, 3 * PARTS, LANES)
    table = (4 * edge, 2 * LANES)
    ends, values, send = call(
        third_kernel,
        [struct((2, 5, edge, LANES), F32), struct((4, slots), F32), struct(sums_shape, F32)],
        [VMEM] * 18,
        [VMEM] * 3,
        [pltpu.VMEM((2, 5, edge + 2 * ROWS, 3 * LANES), F32), pltpu.VMEM(table, BF16), pltpu.VMEM(table, BF16)],
        "edge_sweep_and_sums",
        flops=12_000_000,
    )(
        part, *fields[1:], res, ra, rb, ya, yb, sa, sb,
        gathered, column, cell, vertex, vertex_hot, shapes,
    )
    got = swap(send, "blk", [(i, i + 1) for i in range(0, blocks, 2)])
    keep = call(
        keep_kernel, struct(sums_shape, F32), [VMEM] * 4, VMEM, [], "kept_sums", flops=3_000_000
    )(values, shapes, vertex, vertex_hot)
    place = lax.axis_index("blk") // 2
    while half > 4:
        half //= 2
        both = (keep + got).reshape(2, half, 3 * PARTS, LANES)
        bit = lax.rem(place // half, 2)
        keep = lax.dynamic_index_in_dim(both, bit, 0, keepdims=False)
        send = lax.dynamic_index_in_dim(both, 1 - bit, 0, keepdims=False)
        got = lax.ppermute(send, "blk", [(i, i ^ (2 * half)) for i in range(blocks)])
    one = struct((3 * PARTS, LANES), F32)
    parts = call(
        fourth_kernel, [one] * half, [VMEM] * 2, [VMEM] * half, [], "core_pair_sums"
    )(keep, got)
    adjoint = call(
        store_kernel, struct((5, edge, span), F32), [HBM, VMEM, VMEM], HBM, [pltpu.SemaphoreType.DMA((2,))],
        "store_field", flops=3_000_000, aliases={0: 0},
    )(adjoint, ends, parts[0])
    parts = [lax.ppermute(v, "blk", [(i, i ^ (2 * k + 1)) for i in range(blocks)]) for k, v in enumerate(parts)]
    sensitivity = call(last_kernel, struct((3, VERT_DEV), F32), [VMEM] * half, VMEM, [], "own_sums")(*parts)
    return adjoint, sensitivity


def solution(mesh):
    return jax.shard_map(
        local,
        mesh=mesh,
        in_specs=(
            P(None, "grp", "blk"),
            P(None, "grp", "blk"),
            P(None, "grp", "blk"),
            P(None, "grp", "blk"),
            P("grp", "blk"),
            P(None, None, ("grp", "blk")),
            P(None, ("grp", "blk")),
            P(("grp", "blk")),
            P(None, ("grp", "blk")),
            P(("grp", "blk"), None),
        ),
        out_specs=(P(None, "grp", "blk"), P(None, ("grp", "blk"))),
        check_vma=False,
    )
```
